512 devices in a mesh: outer: 32 (over x, y), inner: 16 (over z, core).
Axes of the slice: x: 4, y: 8, z: 8, core: 2. Of those that a mesh axis runs over, the one named last changes fastest.
Arguments:
- offsets: float32 [3, 262144], P(None, ('outer', 'inner')), may hold values from -0.45 to 0.45
- charges: float32 [64, 262144], P(None, ('outer', 'inner')), may hold values from -1.2 to 1.2
- counts: int32 [8192], P(('outer', 'inner')), may hold values from 1 to 32, as said below
- near: int32 [8192, 12], P(('outer', 'inner')), may hold values from 0 to 8191, as said below
- far: int32 [8192, 12], P(('outer', 'inner')), may hold values from 0 to 8191, as said below
- upward: float32 [165, 165], replicated
- downward: float32 [165, 165], replicated
Outputs:
- potential: float32 [64, 262144], P(None, ('outer', 'inner'))
The draws below stay inside these ranges and needn't reach their ends.
Inputs may be any that keep to these rules, and one draw needn't show every extreme that they name: `counts`: some leaf of every device's range has exactly 32 occupied slots. near[g] holds 12 different leaves, g itself among them; far[g] holds 12 different leaves, none of them in near[g]. All of them belong to the device that owns g or to a device whose inner index differs by one, in the same outer group. `far`: as for near.
All inputs are finite; a program needn't handle non-finite values.
Results may differ from the reference program's by a relative error of at most 0.0003.
Values sent between devices are 32-bit elements; how exact they have to be, the bound alone decides.
No kernel may reach another device: no remote copies, remote signals or barrier semaphores. Data moves between devices by JAX's collectives and lax.ppermute only.
A program may use at most 64 MiB of HBM per device.

```python
import jax
import jax.numpy as jnp
from jax import lax

RHS = 64
SURFACE_POINTS = 165
LEAF = 32
LEAF_DEV = 16
NEAR = 12
FAR = 12
LEAVES = 8192
NPTS = 262144
N_OUTER = 32
N_INNER = 16


def leaf_lists(key):
    leaf_ids = jnp.arange(LEAVES, dtype=jnp.int32)
    owner = leaf_ids // LEAF_DEV
    first = owner // N_INNER * (N_INNER * LEAF_DEV)
    neighbour_window = jnp.arange(3 * LEAF_DEV, dtype=jnp.int32)
    candidate = (owner[:, None] - 1) * LEAF_DEV + neighbour_window[None, :]
    inside = (candidate >= first[:, None]) & (candidate < first[:, None] + N_INNER * LEAF_DEV)
    noise = jax.random.randint(key, (LEAVES, 3 * LEAF_DEV), 0, 4096)
    scores = noise * 256 + neighbour_window[None, :] + inside.astype(jnp.int32) * 2097152 + (candidate == leaf_ids[:, None]).astype(jnp.int32) * 4194304
    picked = lax.top_k(scores, NEAR + FAR)[1]
    return jnp.take_along_axis(candidate, picked, axis=1).astype(jnp.int32)


def draw_near(key, part):
    chosen = leaf_lists(key)
    return chosen[:, :NEAR]


def draw_far(key, part):
    chosen = leaf_lists(key)
    return chosen[:, NEAR:]


def draw_counts(key, part):
    key = jax.random.fold_in(key, 3)
    first_key, second_key = jax.random.split(key)
    filled = jax.random.randint(first_key, (LEAVES,), 1, LEAF + 1)
    chosen = jax.random.randint(second_key, (LEAVES // LEAF_DEV,), 0, LEAF_DEV)
    hit = jnp.arange(LEAVES, dtype=jnp.int32) % LEAF_DEV == jnp.repeat(chosen, LEAF_DEV)
    return jnp.where(hit, LEAF, filled).astype(jnp.int32)


def square_map(key, spread):
    noise = jax.random.normal(key, (SURFACE_POINTS, SURFACE_POINTS), jnp.float32)
    return 0.1 * jnp.eye(SURFACE_POINTS, dtype=jnp.float32) + spread / jnp.sqrt(jnp.float32(SURFACE_POINTS)) * noise


def draw_upward(key, part):
    key = jax.random.fold_in(key, 5)
    return square_map(key, 0.04)


def draw_downward(key, part):
    key = jax.random.fold_in(key, 7)
    return square_map(key, 0.04)


def shard_levels(key, shape, cuts, low, largest):
    def one(position, parts):
        heights = jax.random.uniform(jax.random.fold_in(jax.random.fold_in(key, 6), position), (parts,), jnp.float32, low / len(cuts), largest / len(cuts))
        return jnp.repeat(jnp.exp(heights), shape[position] // parts).reshape((-1,) + (1,) * (len(shape) - position - 1))

    gain = one(*cuts[0])
    for cut in cuts[1:]:
        gain = gain * one(*cut)
    return gain


def centred(rng, dims, scale, bound, cuts=(), kind=jnp.bfloat16):
    factor_of = shard_levels(rng, dims, cuts, -0.22, 0.18) if cuts else 1.0
    result = jax.random.normal(rng, dims, jnp.float32) * scale * factor_of
    return jnp.minimum(jnp.maximum(result, -bound), bound).astype(kind)


def setup_inputs(seed: int = 0) -> dict:
    splits = jax.random.split(jax.random.key(seed), 8)
    offsets = jnp.clip(jax.random.uniform(splits[0], (3, NPTS), jnp.float32, -0.45, 0.45) * shard_levels(splits[0], (3, NPTS), ((1, 512),), -0.4, 0.0), -0.45, 0.45)
    charges = centred(splits[1], (RHS, NPTS), 0.2, 1.2, ((1, 512),), jnp.float32)
    counts = draw_counts(jax.random.fold_in(splits[7], 71), 0)
    near = draw_near(jax.random.fold_in(splits[7], 71), 0)
    far = draw_far(jax.random.fold_in(splits[7], 71), 0)
    upward = draw_upward(jax.random.fold_in(splits[7], 71), 0)
    downward = draw_downward(jax.random.fold_in(splits[7], 71), 0)
    return dict(offsets=offsets, charges=charges, counts=counts, near=near, far=far, upward=upward, downward=downward)


SOFTEN = 0.25
GOLDEN = 2.399963229728653
UPPER_LEVEL = lax.Precision.HIGHEST

def sphere(count):
    steps_t = jnp.arange(count, dtype=jnp.float32)
    height = 1.0 - (2.0 * steps_t + 1.0) / count
    radial = jnp.sqrt(jnp.maximum(1.0 - height * height, 0.0))
    return jnp.stack([radial * jnp.cos(steps_t * GOLDEN), radial * jnp.sin(steps_t * GOLDEN), height])

def morton(leaf_ids):
    coords = []
    for axis_id in range(3):
        bitsum = jnp.zeros_like(leaf_ids)
        for bit_level in range(10):
            bitsum = bitsum | (leaf_ids >> 3 * bit_level + axis_id & 1) << bit_level
        coords.append(bitsum)
    return jnp.stack(coords).astype(jnp.float32) + 0.5

def green(target, source):
    first = target[0] - source[0]
    second = target[1] - source[1]
    third = target[2] - source[2]
    return lax.rsqrt(first * first + second * second + third * third + SOFTEN)

def leaf_expand(centres, points, charges, upward, dirs):
    checks = centres[:, :, None] + 1.8 * dirs[:, None, :]
    kern = green(checks[:, :, :, None], points[:, :, None, :])
    check_pot = jnp.einsum('ltp,rlp->lrt', kern, charges, precision=UPPER_LEVEL)
    return 18.0 / upward.shape[0] * jnp.einsum('lrt,ti->lri', check_pot, upward, precision=UPPER_LEVEL)

def device_expand(centres, equiv, dev_centre, upward, dirs):
    checks = dev_centre[:, None] + 6.0 * dirs
    sources = centres[:, :, None] + 0.9 * dirs[:, None, :]
    kern = green(checks[:, None, :, None], sources[:, :, None, :])
    check_pot = jnp.einsum('lti,lri->rt', kern, equiv, precision=UPPER_LEVEL)
    return 60.0 / upward.shape[0] * jnp.dot(check_pot, upward, precision=UPPER_LEVEL)

def reference(offsets, charges, counts, near, far, upward, downward):
    dirs = sphere(SURFACE_POINTS)
    device_n = N_OUTER * N_INNER
    leaf_ids = jnp.arange(LEAVES, dtype=jnp.int32)
    centres = morton(leaf_ids)
    filled = (jnp.arange(LEAF, dtype=jnp.int32)[None, :] < counts[:, None]).astype(jnp.float32)
    masked = charges.reshape(RHS, LEAVES, LEAF) * filled[None]
    shifts = offsets.reshape(3, LEAVES, LEAF)
    device_table = centres.reshape(3, device_n, LEAF_DEV).mean(axis=2)
    group_table = centres.reshape(3, N_OUTER, N_INNER * LEAF_DEV).mean(axis=2)

    def upward_device(device):
        first = device * LEAF_DEV
        own_centres = lax.dynamic_slice_in_dim(centres, first, LEAF_DEV, 1)
        own_shifts = lax.dynamic_slice_in_dim(shifts, first, LEAF_DEV, 1)
        own_charges = lax.dynamic_slice_in_dim(masked, first, LEAF_DEV, 1)
        own_equiv = leaf_expand(own_centres, own_centres[:, :, None] + own_shifts, own_charges, upward, dirs)
        dev_centre = lax.dynamic_index_in_dim(device_table, device, 1, keepdims=False)
        dev_equiv = device_expand(own_centres, own_equiv, dev_centre, upward, dirs)
        cluster_centre = lax.dynamic_index_in_dim(group_table, device // N_INNER, 1, keepdims=False)
        kern = green(cluster_centre[:, None, None] + 20.0 * dirs[:, :, None], dev_centre[:, None, None] + 3.0 * dirs[:, None, :])
        return (dev_equiv, jnp.einsum('ti,ri->rt', kern, dev_equiv, precision=UPPER_LEVEL))
    dev_equivs, partials = lax.map(upward_device, jnp.arange(device_n, dtype=jnp.int32))
    cluster_check_surface = partials.reshape(N_OUTER, N_INNER, RHS, SURFACE_POINTS).sum(axis=1)
    cluster_equivalent_charges = 200.0 / SURFACE_POINTS * jnp.einsum('ozb,bx->ozx', cluster_check_surface, upward, precision=UPPER_LEVEL)

    def group_section(group):
        cluster_centre = lax.dynamic_index_in_dim(group_table, group, 1, keepdims=False)
        targets = cluster_centre[:, None] + 10.0 * dirs
        sources = group_table[:, :, None] + 20.0 * dirs[:, None, :]
        kern = green(targets[:, None, :, None], sources[:, :, None, :])
        weight = (jnp.abs(jnp.arange(N_OUTER, dtype=jnp.int32) - group) >= 2).astype(jnp.float32)
        down = jnp.einsum('gti,gri->rt', kern * weight[:, None, None], cluster_equivalent_charges, precision=UPPER_LEVEL)
        return 200.0 / SURFACE_POINTS * jnp.dot(down, downward, precision=UPPER_LEVEL)
    group_locals = lax.map(group_section, jnp.arange(N_OUTER, dtype=jnp.int32))

    def device_section(device):
        group = device // N_INNER
        inner_id = device % N_INNER
        dev_centre = lax.dynamic_index_in_dim(device_table, device, 1, keepdims=False)
        peers = lax.dynamic_slice_in_dim(device_table, group * N_INNER, N_INNER, 1)
        peer_equiv = lax.dynamic_slice_in_dim(dev_equivs, group * N_INNER, N_INNER, 0)
        targets = dev_centre[:, None] + 3.0 * dirs
        kern = green(targets[:, None, :, None], peers[:, :, None, None] + 3.0 * dirs[:, None, None, :])
        weight = (jnp.abs(jnp.arange(N_INNER, dtype=jnp.int32) - inner_id) >= 2).astype(jnp.float32)
        down = jnp.einsum('eti,eri->rt', kern * weight[:, None, None], peer_equiv, precision=UPPER_LEVEL)
        cluster_centre = lax.dynamic_index_in_dim(group_table, group, 1, keepdims=False)
        kern_group = green(targets[:, :, None], cluster_centre[:, None, None] + 20.0 * dirs[:, None, :])
        group_local = lax.dynamic_index_in_dim(group_locals, group, 0, keepdims=False)
        down = down + jnp.einsum('ti,ri->rt', kern_group, group_local, precision=UPPER_LEVEL)
        return 60.0 / SURFACE_POINTS * jnp.dot(down, downward, precision=UPPER_LEVEL)
    device_locals = lax.map(device_section, jnp.arange(device_n, dtype=jnp.int32))

    def leaf_section(device):
        group = device // N_INNER
        base = (device - 1) * LEAF_DEV
        neighbour_window_index = base + jnp.arange(3 * LEAF_DEV, dtype=jnp.int32)
        start = group * (N_INNER * LEAF_DEV)
        inside = ((neighbour_window_index >= start) & (neighbour_window_index < start + N_INNER * LEAF_DEV)).astype(jnp.float32)
        clipped = jnp.clip(neighbour_window_index, 0, LEAVES - 1).astype(jnp.int32)
        window_centres = morton(neighbour_window_index)
        window_points = window_centres[:, :, None] + jnp.take(shifts, clipped, axis=1) * inside[None, :, None]
        window_charges = jnp.take(masked, clipped, axis=1) * inside[None, :, None]
        window_equiv = leaf_expand(window_centres, window_points, window_charges, upward, dirs)
        own_centres = window_centres[:, LEAF_DEV:2 * LEAF_DEV]
        own_points = window_points[:, LEAF_DEV:2 * LEAF_DEV]
        dev_centre = lax.dynamic_index_in_dim(device_table, device, 1, keepdims=False)
        device_local = lax.dynamic_index_in_dim(device_locals, device, 0, keepdims=False)
        far_dev = lax.dynamic_slice_in_dim(far, device * LEAF_DEV, LEAF_DEV, 0) - base
        near_dev = lax.dynamic_slice_in_dim(near, device * LEAF_DEV, LEAF_DEV, 0) - base
        leaf_target_points = own_centres[:, :, None] + 0.9 * dirs[:, None, :]

        def far_add(turn, total):
            column = lax.dynamic_index_in_dim(far_dev, turn, 1, keepdims=False)
            source_equiv = jnp.take(window_equiv, column, axis=0)
            source_centre = jnp.take(window_centres, column, axis=1)
            kern = green(leaf_target_points[:, :, :, None], source_centre[:, :, None, None] + 1.8 * dirs[:, None, None, :])
            return total + jnp.einsum('lti,lri->lrt', kern, source_equiv, precision=UPPER_LEVEL)
        leaf_down = lax.fori_loop(0, FAR, far_add, jnp.zeros((LEAF_DEV, RHS, SURFACE_POINTS), jnp.float32))
        kern = green(leaf_target_points[:, :, :, None], dev_centre[:, None, None, None] + 6.0 * dirs[:, None, None, :])
        leaf_down = leaf_down + jnp.einsum('lti,ri->lrt', kern, device_local, precision=UPPER_LEVEL)
        leaf_local = 18.0 / SURFACE_POINTS * jnp.einsum('lrt,ti->lri', leaf_down, downward, precision=UPPER_LEVEL)
        kern = green(own_points[:, :, :, None], own_centres[:, :, None, None] + 1.8 * dirs[:, None, None, :])
        far_part = jnp.einsum('lpi,lri->rlp', kern, leaf_local, precision=UPPER_LEVEL)
        near_points = jnp.take(window_points, near_dev, axis=1)
        near_charges = jnp.take(window_charges, near_dev, axis=1)
        kern = green(own_points[:, :, None, :, None], near_points[:, :, :, None, :])
        near_part = jnp.einsum('lkps,rlks->rlp', kern, near_charges, precision=UPPER_LEVEL)
        return (far_part + near_part).reshape(RHS, LEAF_DEV * LEAF)
    blocks = lax.map(leaf_section, jnp.arange(device_n, dtype=jnp.int32))
    return jnp.transpose(blocks, (1, 0, 2)).reshape(RHS, NPTS)
```

```python
import functools

import jax
import jax.numpy as jnp
import numpy as np
from jax import lax
from jax.experimental import pallas as pl
from jax.experimental.pallas import tpu as pltpu
from jax.sharding import PartitionSpec as P

SOFTEN = 0.25
GOLDEN = 2.399963229728653
RHS = 64
TERMS = 165
SUB = 176
LANE = 256
LEAVES = 16
SLOTS = 32
POINTS = LEAVES * SLOTS
ROWS = 72
INNER = 16
OUTER = 32
PART = RHS // INNER
BF = jnp.bfloat16
F32 = jnp.float32


def sphere_tables():
    steps = np.arange(TERMS, dtype=np.float32)
    height = (np.float32(1.0) - (np.float32(2.0) * steps + np.float32(1.0)) / np.float32(TERMS)).astype(np.float32)
    radial = np.sqrt(np.maximum(np.float32(1.0) - height * height, np.float32(0.0))).astype(np.float32)
    angle = (steps * np.float32(GOLDEN)).astype(np.float32)
    dirs = np.stack([radial * np.cos(angle), radial * np.sin(angle), height]).astype(np.float32)
    col = np.zeros((SUB, 128), np.float32)
    col[:TERMS, :3] = dirs.T
    row = np.zeros((8, LANE), np.float32)
    row[:3, :TERMS] = dirs
    return col, row


def split(x):
    high = x.astype(BF)
    return high, (x - high.astype(F32)).astype(BF)


def dot(a, b):
    return jnp.dot(a, b, preferred_element_type=F32)


def dot_nt(a, b):
    return lax.dot_general(a, b, (((1,), (1,)), ((), ())), preferred_element_type=F32)


def mm3(a, b, f=dot):
    return f(a[0], b[0]) + f(a[1], b[0]) + f(a[0], b[1])


def columns(col_ref):
    return [jnp.broadcast_to(col_ref[:, c : c + 1], (SUB, 128)) for c in range(3)]


def two(x):
    return jnp.concatenate([x, x], axis=1)


def surface_products(col_ref, row_ref):
    cols = [two(c) for c in columns(col_ref)]
    return (
        cols[0] * row_ref[0:1, :] + cols[1] * row_ref[1:2, :] + cols[2] * row_ref[2:3, :]
    )


def pair_kernel(base, col_ref, row_ref, shift, radius_t, radius_i):
    dx, dy, dz = shift
    cols = columns(col_ref)
    side = (-2.0 * radius_i * dx) * cols[0] + (-2.0 * radius_i * dy) * cols[1] + (-2.0 * radius_i * dz) * cols[2]
    along = (
        (2.0 * radius_t * dx) * row_ref[0:1, :]
        + (2.0 * radius_t * dy) * row_ref[1:2, :]
        + (2.0 * radius_t * dz) * row_ref[2:3, :]
        + (dx * dx + dy * dy + dz * dz)
    )
    return lax.rsqrt(base + two(side) + along)


def base_of(products, radius_t, radius_i):
    return products * (-2.0 * radius_t * radius_i) + (radius_t * radius_t + radius_i * radius_i + SOFTEN)


def bits(ids, low, axis, top=14):
    total = 0
    for level in range(5):
        place = 3 * level + axis
        if low <= place < top:
            total = total + (((ids >> place) & 1) << level)
    return total


def corner(leaf_id, low):
    return [bits(leaf_id, low, axis) for axis in range(3)]


def local_leaf(index):
    return ((index & 1) + ((index >> 3) & 1) * 2, (index >> 1) & 1, (index >> 2) & 1)


def peer_box(inner):
    return (((inner >> 2) & 1) * 4, (inner & 1) * 2 + ((inner >> 3) & 1) * 4, ((inner >> 1) & 1) * 2)


def leaf_kernel(offs, col_ref):
    total = SOFTEN
    for c in range(3):
        col = jnp.broadcast_to(col_ref[:, c : c + 1], (SUB, 128)) * 1.8
        diff = jnp.concatenate([col] * (POINTS // 128), axis=1) - offs[c : c + 1, :]
        total = total + diff * diff
    return lax.rsqrt(total)


def padded(map_ref, pad_ref, scale):
    pad_ref[...] = jnp.zeros_like(pad_ref)
    pad_ref[0:TERMS, 0:TERMS] = map_ref[...] * scale
    return split(pad_ref[...])


def leaf_equivalents(charges, kern, up):
    block = lax.broadcasted_iota(jnp.int32, (RHS, 256), 1) // SLOTS
    out = []
    for half in range(2):
        lanes = slice(half * 256, half * 256 + 256)
        own = charges[:, lanes]
        spread = split(jnp.concatenate([jnp.where(block == g, own, 0.0) for g in range(8)], axis=0))
        check = mm3(spread, (kern[0][:, lanes], kern[1][:, lanes]), dot_nt)
        out.append(mm3(split(check), up))
    return out


def pack(rows):
    low, high = rows[:, :128], rows[:, 128:]
    n = rows.shape[0]
    top = lax.broadcasted_iota(jnp.int32, (n, 128), 0) % 8 < 4
    first = jnp.where(top, low, pltpu.roll(high, 4, 0))
    second = jnp.where(top, pltpu.roll(low, n - 4, 0), high)
    tiles = []
    for m in range(n // 8):
        tiles += [first[8 * m : 8 * m + 8], second[8 * m : 8 * m + 8]]
    return jnp.concatenate(tiles, axis=0)


def unpack(tiles):
    n = tiles.shape[0] // 2
    first = jnp.concatenate([tiles[16 * m : 16 * m + 8] for m in range(n // 8)], axis=0)
    second = jnp.concatenate([tiles[16 * m + 8 : 16 * m + 16] for m in range(n // 8)], axis=0)
    top = lax.broadcasted_iota(jnp.int32, (n, 128), 0) % 8 < 4
    low = jnp.where(top, first, pltpu.roll(second, 4, 0))
    high = jnp.where(top, pltpu.roll(first, n - 4, 0), second)
    return jnp.concatenate([low, high], axis=1)


def tile_dot(tile, high, low, acc):
    a_high, a_low = split(tile)
    both = jnp.concatenate([a_high, a_low], axis=0)
    rest = SUB - 128
    front = dot(both, high[:128]) + dot(both, low[:128])
    back = dot(both[:, :rest], high[128:]) + dot(both[:, :rest], low[128:])
    return acc[0] + front, acc[1] + back


def tile_sum(acc):
    front = acc[0][:8] + acc[0][8:]
    back = acc[1][:8] + acc[1][8:]
    return front + pltpu.roll(back, 4, 0)


def head_kernel(
    off_hbm, q_hbm, counts_hbm, up_hbm, down_hbm, col_hbm, row_hbm,
    out_ref, halo_ref, up_ref, down_ref, col_ref, row_ref,
    off_ref, q_ref, counts_ref, pad_ref, sems,
):
    moves = [
        pltpu.make_async_copy(src, dst, sems.at[n])
        for n, (src, dst) in enumerate(
            (
                (q_hbm, q_ref),
                (off_hbm, off_ref),
                (counts_hbm, counts_ref),
                (up_hbm, up_ref),
                (col_hbm, col_ref),
                (row_hbm, row_ref),
                (down_hbm, down_ref),
            )
        )
    ]
    for move in moves:
        move.start()
    for move in moves[:-1]:
        move.wait()
    lane = lax.broadcasted_iota(jnp.int32, (8, POINTS), 1)
    limit = jnp.zeros((8, POINTS), jnp.int32)
    for g in range(LEAVES):
        limit = jnp.where(lane // SLOTS == g, counts_ref[g], limit)
    filled = (lane % SLOTS < limit)[0:1]
    charges = jnp.where(filled, q_ref[...], 0.0)
    halo_ref[0:RHS, :] = charges
    halo_ref[RHS:ROWS, :] = jnp.zeros((ROWS - RHS, POINTS), F32)
    halo_ref[RHS : RHS + 3, :] = off_ref[...]
    kern = split(leaf_kernel(off_ref[...], col_ref))
    up = padded(up_ref, pad_ref, 18.0 / TERMS)
    up = (up[0][:, :], up[1][:, :])
    halves = leaf_equivalents(charges, kern, up)
    base = base_of(surface_products(col_ref, row_ref), 6.0, 0.9)
    acc = jnp.zeros((RHS, LANE), F32)
    for half in range(2):
        equiv = split(halves[half])
        for g in range(8):
            x, y, z = local_leaf(half * 8 + g)
            k_high, k_low = split(pair_kernel(base, col_ref, row_ref, (1.5 - x, 0.5 - y, 0.5 - z), 6.0, 0.9))
            rows = slice(g * RHS, g * RHS + RHS)
            acc = acc + dot(equiv[0][rows, :SUB], k_high) + dot(equiv[1][rows, :SUB], k_high) + dot(
                equiv[0][rows, :SUB], k_low
            )
    up60 = padded(up_ref, pad_ref, 60.0 / TERMS)
    out_ref[...] = pack(mm3(split(acc[:, :SUB]), up60))
    moves[-1].wait()


def group_up_kernel(x_ref, up_ref, col_ref, row_ref, out_ref, pad_ref):
    base = base_of(surface_products(col_ref, row_ref), 20.0, 3.0)
    acc = (jnp.zeros((16, LANE), F32), jnp.zeros((16, LANE), F32))
    for e in range(INNER):
        x, y, z = peer_box(e)
        kern = split(pair_kernel(base, col_ref, row_ref, (4.0 - x - 2.0, 4.0 - y - 1.0, 2.0 - z - 1.0), 20.0, 3.0))
        acc = tile_dot(x_ref[8 * e : 8 * e + 8, :], kern[0], kern[1], acc)
    check = tile_sum(acc)
    both = jnp.concatenate([check, check], axis=0)
    equiv = mm3(split(both[:, :SUB]), padded(up_ref, pad_ref, 200.0 / TERMS))[:8]
    top = lax.broadcasted_iota(jnp.int32, (8, 128), 0) < 4
    tile = jnp.where(top, equiv[:, :128], pltpu.roll(equiv[:, 128:], 4, 0))
    for p in range(OUTER):
        out_ref[8 * p : 8 * p + 8, :] = tile


def peers_kernel(x_ref, col_ref, row_ref, out_ref):
    equiv = unpack(x_ref[...])
    both = jnp.concatenate(split(equiv), axis=1)
    base = base_of(surface_products(col_ref, row_ref), 3.0, 3.0)
    row = lax.broadcasted_iota(jnp.int32, (RHS, RHS), 0)
    lane = lax.broadcasted_iota(jnp.int32, (RHS, RHS), 1)
    dest = row // PART
    px = (dest >> 2) & 1
    py = (dest & 1) + ((dest >> 3) & 1) * 2
    pz = (dest >> 1) & 1

    def one(dx, dy, dz, acc):
        sx, sy, sz = px - dx, py - dy, pz - dz
        inside = (sx >= 0) & (sx < 2) & (sy >= 0) & (sy < 4) & (sz >= 0) & (sz < 2)
        source = (sy & 1) + (sz & 1) * 2 + (sx & 1) * 4 + ((sy >> 1) & 1) * 8
        apart = jnp.abs(source - dest) >= 2
        pick = (inside & apart & (lane == source * PART + row % PART)).astype(F32).astype(BF)
        moved = dot(pick, both).astype(BF)
        shift = (dx.astype(F32) * 4.0, dy * 2.0, dz.astype(F32) * 2.0)
        kern = split(pair_kernel(base, col_ref, row_ref, shift, 3.0, 3.0))
        a = (moved[:, :SUB], moved[:, LANE : LANE + SUB])
        return acc + mm3(a, kern)

    def step(turn, acc):
        for dy in range(-3, 4):
            acc = one(turn // 3 - 1, dy, turn % 3 - 1, acc)
        return acc

    out_ref[...] = lax.fori_loop(0, 9, step, jnp.zeros((RHS, LANE), F32))


def group_maps_kernel(flow_ref, col_ref, row_ref, out_ref, down_ref):
    outer = lax.axis_index("outer")
    own = corner(outer * 256, 8)
    cols = [two(c) * 20.0 for c in columns(col_ref)]

    def step(turn, carry):
        for n in range(4):
            p = turn * 4 + n
            other = corner(p * 256, 8)
            total = SOFTEN
            for c in range(3):
                shift = (own[c] - other[c]).astype(F32)
                diff = (shift + 10.0 * row_ref[c : c + 1, :]) - cols[c]
                total = total + diff * diff
            high, low = split(lax.rsqrt(total))
            out_ref[p, 0, :, :] = high
            out_ref[p, 1, :, :] = low
        return carry

    lax.fori_loop(0, OUTER // 4, step, 0)
    base = base_of(surface_products(col_ref, row_ref), 3.0, 20.0)
    for d in range(INNER):
        x, y, z = peer_box(d)
        high, low = split(pair_kernel(base, col_ref, row_ref, (x + 2.0 - 4.0, y + 1.0 - 4.0, z + 1.0 - 2.0), 3.0, 20.0))
        down_ref[d, 0, :, :] = high
        down_ref[d, 1, :, :] = low


def local_kernel(x_ref, peers_ref, maps_ref, to_dev_ref, down_ref, out_ref, pad_ref):
    outer = lax.axis_index("outer")
    acc = (jnp.zeros((16, LANE), F32), jnp.zeros((16, LANE), F32))
    for p in range(OUTER):
        weight = (jnp.abs(p - outer) >= 2).astype(F32)
        acc = tile_dot(x_ref[8 * p : 8 * p + 8, :] * weight, maps_ref[p, 0], maps_ref[p, 1], acc)
    check = tile_sum(acc)
    both = jnp.concatenate([check, check], axis=0)
    group = mm3(split(both[:, :SUB]), padded(down_ref, pad_ref, 200.0 / TERMS))[:8]
    pieces = jnp.concatenate(split(group[:, :SUB]), axis=0)
    top = lax.broadcasted_iota(jnp.int32, (8, LANE), 0) < 4
    found = []
    for d in range(INNER):
        part = dot(pieces, to_dev_ref[d, 0]) + dot(pieces, to_dev_ref[d, 1])
        found.append(part[:8] + part[8:])
    merged = [jnp.where(top, found[2 * m], pltpu.roll(found[2 * m + 1], 4, 0)) for m in range(INNER // 2)]
    total = jnp.concatenate(merged, axis=0) + peers_ref[...]
    out_ref[...] = pack(mm3(split(total[:, :SUB]), padded(down_ref, pad_ref, 60.0 / TERMS)))


def operator_kernel(own_ref, down_ref, col_ref, row_ref, w_ref, m_ref, halo_ref, pad_ref):
    halo_ref[...] = own_ref[...]
    off = own_ref[RHS : RHS + 3, :]
    down = padded(down_ref, pad_ref, 18.0 / TERMS)
    down = (down[0][:, :SUB], down[1][:, :SUB])
    weights = split(mm3(down, split(leaf_kernel(off, col_ref))))
    w_ref[0, :, :] = weights[0]
    w_ref[1, :, :] = weights[1]
    base = base_of(surface_products(col_ref, row_ref), 0.9, 6.0)
    block = lax.broadcasted_iota(jnp.int32, (SUB, 256), 1) // SLOTS
    for half in range(2):
        lanes = slice(half * 256, half * 256 + 256)
        own = (weights[0][:, lanes], weights[1][:, lanes])
        acc = jnp.zeros((SUB, 256), F32)
        for g in range(8):
            x, y, z = local_leaf(half * 8 + g)
            kern = pair_kernel(base, col_ref, row_ref, (x - 1.5, y - 0.5, z - 0.5), 0.9, 6.0)
            acc = jnp.where(block == g, mm3(split(kern[:, :SUB]), own), acc)
        m_high, m_low = split(acc)
        m_ref[0, :, lanes] = m_high
        m_ref[1, :, lanes] = m_low


def near_kernel(near_ref, left_ref, own_ref, right_ref, out_ref, mask_ref, high_ref, low_ref):
    offs = jnp.concatenate([own_ref[RHS:ROWS, :], jnp.zeros((120, POINTS), F32)], axis=0).T
    inner = lax.axis_index("inner")
    device = lax.axis_index("outer") * INNER + inner
    base = (device - 1) * LEAVES
    total = 3 * POINTS
    lane = lax.broadcasted_iota(jnp.int32, (LEAVES, total), 1) // SLOTS
    found = jnp.zeros((LEAVES, total), F32)
    near = near_ref[...] - base
    for k in range(12):
        found = jnp.where(lane == near[:, k : k + 1], 1.0, found)
    mask_ref[...] = found
    leaf = lax.broadcasted_iota(jnp.int32, (1, POINTS), 1) // SLOTS
    within = local_leaf(leaf)
    own_box = corner(device * LEAVES, 4)
    sources = []
    for c in range(3):
        lanes = []
        for side, ref in ((-1, left_ref), (0, own_ref), (1, right_ref)):
            box = corner((device + side) * LEAVES, 4)[c] - own_box[c]
            lanes.append(ref[RHS + c : RHS + c + 1, :] + (box + within[c]).astype(F32))
        sources.append(jnp.concatenate(lanes, axis=1))
    for g in range(LEAVES):
        rows = slice(g * SLOTS, g * SLOTS + SLOTS)
        place = local_leaf(g)
        dist = SOFTEN
        for c in range(3):
            diff = (offs[rows, c : c + 1] + float(place[c])) - sources[c]
            dist = dist + diff * diff
        k_high, k_low = split(lax.rsqrt(dist) * mask_ref[g : g + 1, :])
        high_ref[rows, :] = k_high
        low_ref[rows, :] = k_low
    charges = jnp.concatenate([r[0:RHS, :] for r in (left_ref, own_ref, right_ref)], axis=1)
    q_high, q_low = split(charges)
    both = jnp.concatenate([q_high, q_low], axis=0)
    res = dot_nt(high_ref[...], both)
    res = res + jnp.concatenate([dot_nt(low_ref[...], q_high), jnp.zeros((POINTS, RHS), F32)], axis=1)
    flipped = res.T
    out_ref[...] = flipped[:RHS] + flipped[RHS:]


def far_kernel(far_ref, left_ref, own_ref, right_ref, w_ref, up_ref, near_ref, col_ref, row_ref, out_ref, pad_ref, base_ref, e_ref, dl_ref, side_ref):
    inner = lax.axis_index("inner")
    device = lax.axis_index("outer") * INNER + inner
    up = padded(up_ref, pad_ref, 18.0 / TERMS)
    for side, ref in enumerate((left_ref, own_ref, right_ref)):
        kern = split(leaf_kernel(ref[RHS : RHS + 3, :], col_ref))
        halves = leaf_equivalents(ref[0:RHS, :], kern, up)
        for half in range(2):
            e_high, e_low = split(halves[half])
            for g in range(8):
                start = ((side * 2 + half) * 8 + g) * 2 * RHS
                e_ref[start : start + RHS, :] = e_high[g * RHS : g * RHS + RHS]
                e_ref[start + RHS : start + 2 * RHS, :] = e_low[g * RHS : g * RHS + RHS]
    products = base_of(surface_products(col_ref, row_ref), 0.9, 1.8)
    first = (device - 1) * LEAVES
    boxes = [corner((device + side) * LEAVES, 4) for side in (-1, 0, 1)]
    boxes = [[(box[c] - boxes[1][c]).astype(F32) for c in range(3)] for box in boxes]
    cols = [c * 3.6 for c in columns(col_ref)]
    for window in range(3 * LEAVES):
        place = local_leaf(window % LEAVES)
        at = [boxes[window // LEAVES][c] + float(place[c]) for c in range(3)]
        side_ref[window * SUB : (window + 1) * SUB, :] = at[0] * cols[0] + at[1] * cols[1] + at[2] * cols[2]

    def one_leaf(g, carry):
        own = [p.astype(F32) for p in local_leaf(g)]
        own_side = side_ref[pl.ds(pl.multiple_of((g + LEAVES) * SUB, SUB), SUB), :]
        base_ref[...] = products - two(own_side)
        acc = jnp.zeros((RHS, LANE), F32)
        for k in range(12):
            window = far_ref[g, k] - first
            side = window >> 4
            place = local_leaf(window & 15)
            shift = []
            for c in range(3):
                box = jnp.where(side == 0, boxes[0][c], jnp.where(side == 1, 0.0, boxes[2][c]))
                shift.append(own[c] - box - place[c].astype(F32))
            along = (
                (1.8 * shift[0]) * row_ref[0:1, :]
                + (1.8 * shift[1]) * row_ref[1:2, :]
                + (1.8 * shift[2]) * row_ref[2:3, :]
                + (shift[0] * shift[0] + shift[1] * shift[1] + shift[2] * shift[2])
            )
            source_side = side_ref[pl.ds(pl.multiple_of(window * SUB, SUB), SUB), :]
            k_high, k_low = split(lax.rsqrt(base_ref[...] + two(source_side) + along))
            start = pl.multiple_of(window * (2 * RHS), 2 * RHS)
            equiv = e_ref[pl.ds(start, 2 * RHS), :][:, :SUB]
            wide = dot(equiv, k_high)
            acc = acc + wide[:RHS] + wide[RHS:] + dot(equiv[:RHS], k_low)
        high, low = split(acc)
        start = pl.multiple_of(g * RHS, RHS)
        dl_ref[0, pl.ds(start, RHS), :] = high
        dl_ref[1, pl.ds(start, RHS), :] = low
        return carry

    lax.fori_loop(0, LEAVES, one_leaf, 0)
    block = lax.broadcasted_iota(jnp.int32, (RHS, 256), 1) // SLOTS
    for half in range(2):
        lanes = slice(half * 256, half * 256 + 256)
        rows = slice(half * 8 * RHS, (half + 1) * 8 * RHS)
        local = (dl_ref[0, rows, :][:, :SUB], dl_ref[1, rows, :][:, :SUB])
        res = mm3(local, (w_ref[0, :, lanes], w_ref[1, :, lanes]))
        acc = near_ref[:, lanes]
        for g in range(8):
            acc = acc + jnp.where(block == g, res[g * RHS : (g + 1) * RHS], 0.0)
        out_ref[:, lanes] = acc


def tail_kernel(x_ref, base_ref, m_ref, out_ref):
    local = split(unpack(x_ref[...])[:, :SUB])
    out_ref[...] = base_ref[...] + mm3(local, (m_ref[0], m_ref[1]))


VM = pl.BlockSpec(memory_space=pltpu.VMEM)
SM = pl.BlockSpec(memory_space=pltpu.SMEM)


def call(kernel, name, outs, specs, scratch, cost, *args, vmem=32):
    return pl.pallas_call(
        kernel,
        name=name,
        out_shape=outs,
        in_specs=specs,
        out_specs=jax.tree.map(lambda _: VM, outs),
        scratch_shapes=scratch,
        compiler_params=pltpu.CompilerParams(vmem_limit_bytes=vmem * 1024 * 1024),
        cost_estimate=pl.CostEstimate(flops=cost, bytes_accessed=500000, transcendentals=0),
    )(*args)


def tie(value, *others):
    return lax.optimization_barrier((value,) + others)[0]


def shards(offsets, charges, counts, near, far, upward, downward):
    col_np, row_np = sphere_tables()
    col, row = jnp.asarray(col_np), jnp.asarray(row_np)
    pad = pltpu.VMEM((SUB, LANE), F32)
    sds = jax.ShapeDtypeStruct
    flow = sds((2 * RHS, 128), F32)
    us = 400_000_000

    hbm = pl.BlockSpec(memory_space=pltpu.HBM)
    square = sds((TERMS, TERMS), F32)
    dev_equiv, own, upward, downward, col, row = call(
        head_kernel, "leaf_and_device_equiv",
        (flow, sds((ROWS, POINTS), F32), square, square, sds((SUB, 128), F32), sds((8, LANE), F32)), [hbm] * 7,
        [
            pltpu.VMEM((3, POINTS), F32),
            pltpu.VMEM((RHS, POINTS), F32),
            pltpu.SMEM((LEAVES,), jnp.int32),
            pad,
            pltpu.SemaphoreType.DMA((7,)),
        ],
        3 * us, *(pltpu.with_memory_space_constraint(a, pltpu.HBM) for a in (offsets, charges, counts, upward, downward, col, row)),
    )
    peers_equiv = lax.all_to_all(dev_equiv, "inner", 0, 0, tiled=True)
    weights, evaluate, halo = call(
        operator_kernel, "evaluation_maps",
        (sds((2, SUB, POINTS), BF), sds((2, SUB, POINTS), BF), sds((ROWS, POINTS), F32)), [VM, VM, VM, VM], [pad], 5 * us,
        own, downward, col, row,
    )
    ends = INNER - 1
    left = lax.ppermute(halo, "inner", [(i, i + 1) for i in range(ends)])
    right = lax.ppermute(halo, "inner", [(i + 1, i) for i in range(ends)])
    group_maps, to_devices = call(
        group_maps_kernel, "group_maps",
        (sds((OUTER, 2, SUB, LANE), BF), sds((INNER, 2, SUB, LANE), BF)), [VM, VM, VM], [], 5 * us,
        dev_equiv, col, row,
    )
    peers_equiv = tie(peers_equiv, weights, evaluate, group_maps, to_devices)
    group_equiv = call(
        group_up_kernel, "group_equiv", sds((8 * OUTER, 128), F32), [VM, VM, VM, VM], [pad], 2 * us,
        peers_equiv, upward, col, row,
    )
    groups = lax.all_to_all(group_equiv, "outer", 0, 0, tiled=True)
    peers_part = call(
        peers_kernel, "device_to_device", sds((RHS, LANE), F32), [VM, VM, VM], [], 8 * us, peers_equiv, col, row,
    )
    near_part = call(
        near_kernel, "near_field", sds((RHS, POINTS), F32), [VM, VM, VM, VM],
        [pltpu.VMEM((LEAVES, 3 * POINTS), F32), pltpu.VMEM((POINTS, 3 * POINTS), BF), pltpu.VMEM((POINTS, 3 * POINTS), BF)], 4 * us,
        near, left, own, right,
    )
    groups = tie(groups, near_part, peers_part)
    local = call(
        local_kernel, "group_and_device_local", flow, [VM, VM, VM, VM, VM], [pad], 3 * us,
        groups, peers_part, group_maps, to_devices, downward,
    )
    dev_local = lax.all_to_all(local, "inner", 0, 0, tiled=True)
    base = call(
        far_kernel, "far_field", sds((RHS, POINTS), F32), [SM, VM, VM, VM, VM, VM, VM, VM, VM],
        [
            pad,
            pad,
            pltpu.VMEM((3 * LEAVES * 2 * RHS, LANE), BF),
            pltpu.VMEM((2, LEAVES * RHS, LANE), BF),
            pltpu.VMEM((3 * LEAVES * SUB, 128), F32),
        ],
        12 * us, far, left, own, right, weights, upward, near_part, col, row,
    )
    return call(tail_kernel, "potential", sds((RHS, POINTS), F32), [VM, VM, VM], [], us, dev_local, base, evaluate)


def solution(mesh):
    both = ("outer", "inner")
    in_specs = (P(None, both), P(None, both), P(both), P(both, None), P(both, None), P(), P())
    return jax.shard_map(shards, mesh=mesh, in_specs=in_specs, out_specs=P(None, both), check_vma=False)
```

```python
import functools

import jax
import jax.numpy as jnp
import numpy as np
from jax import lax
from jax.experimental import pallas as pl
from jax.experimental.pallas import tpu as pltpu
from jax.sharding import PartitionSpec as P

SOFTEN = 0.25
GOLDEN = 2.399963229728653
RHS = 64
TERMS = 165
SUB = 176
LANE = 256
LEAVES = 16
SLOTS = 32
POINTS = LEAVES * SLOTS
ROWS = 72
INNER = 16
OUTER = 32
PART = RHS // INNER
BF = jnp.bfloat16
F32 = jnp.float32


def sphere_tables():
    steps = np.arange(TERMS, dtype=np.float32)
    height = (np.float32(1.0) - (np.float32(2.0) * steps + np.float32(1.0)) / np.float32(TERMS)).astype(np.float32)
    radial = np.sqrt(np.maximum(np.float32(1.0) - height * height, np.float32(0.0))).astype(np.float32)
    angle = (steps * np.float32(GOLDEN)).astype(np.float32)
    dirs = np.stack([radial * np.cos(angle), radial * np.sin(angle), height]).astype(np.float32)
    col = np.zeros((SUB, 128), np.float32)
    col[:TERMS, :3] = dirs.T
    row = np.zeros((8, LANE), np.float32)
    row[:3, :TERMS] = dirs
    return col, row


def split(x):
    high = x.astype(BF)
    return high, (x - high.astype(F32)).astype(BF)


def dot(a, b):
    return jnp.dot(a, b, preferred_element_type=F32)


def dot_nt(a, b):
    return lax.dot_general(a, b, (((1,), (1,)), ((), ())), preferred_element_type=F32)


def mm3(a, b, f=dot):
    return f(a[0], b[0]) + f(a[1], b[0]) + f(a[0], b[1])


def columns(col_ref):
    return [jnp.broadcast_to(col_ref[:, c : c + 1], (SUB, 128)) for c in range(3)]


def two(x):
    return jnp.concatenate([x, x], axis=1)


def square_of(axis, shift, radius_t, radius_i, cols, row_ref):
    diff = (radius_t * row_ref[axis : axis + 1, :] + shift) - two(radius_i * cols[axis])
    return diff * diff


def box_kernels(xs, ys, zs, radius_t, radius_i, col_ref, row_ref, tab_ref):
    cols = columns(col_ref)
    for n, shift in enumerate(xs):
        tab_ref[n] = square_of(0, shift, radius_t, radius_i, cols, row_ref)
    zsq = len(xs)
    for n, shift in enumerate(zs):
        tab_ref[zsq + n] = square_of(2, shift, radius_t, radius_i, cols, row_ref) + SOFTEN
    start = zsq + len(zs)
    for b, shift in enumerate(ys):
        ysq = square_of(1, shift, radius_t, radius_i, cols, row_ref)
        for c in range(len(zs)):
            tab_ref[start + b * len(zs) + c] = ysq + tab_ref[zsq + c]
    for b in range(len(ys)):
        for c in range(len(zs)):
            for a in range(len(xs)):
                yield (a, b, c), lax.rsqrt(tab_ref[a] + tab_ref[start + b * len(zs) + c])


def bits(ids, low, axis, top=14):
    total = 0
    for level in range(5):
        place = 3 * level + axis
        if low <= place < top:
            total = total + (((ids >> place) & 1) << level)
    return total


def corner(leaf_id, low):
    return [bits(leaf_id, low, axis) for axis in range(3)]


def local_leaf(index):
    return ((index & 1) + ((index >> 3) & 1) * 2, (index >> 1) & 1, (index >> 2) & 1)


def peer_box(inner):
    return (((inner >> 2) & 1) * 4, (inner & 1) * 2 + ((inner >> 3) & 1) * 4, ((inner >> 1) & 1) * 2)


def leaf_kernel(offs, col_ref):
    total = SOFTEN
    for c in range(3):
        col = jnp.broadcast_to(col_ref[:, c : c + 1], (SUB, 128)) * 1.8
        diff = jnp.concatenate([col] * (POINTS // 128), axis=1) - offs[c : c + 1, :]
        total = total + diff * diff
    return lax.rsqrt(total)


def padded(map_ref, pad_ref, scale):
    pad_ref[...] = jnp.zeros_like(pad_ref)
    pad_ref[0:TERMS, 0:TERMS] = map_ref[...] * scale
    return split(pad_ref[...])


def leaf_equivalents(charges, kern, up):
    block = lax.broadcasted_iota(jnp.int32, (RHS, 256), 1) // SLOTS
    out = []
    for half in range(2):
        lanes = slice(half * 256, half * 256 + 256)
        own = charges[:, lanes]
        spread = split(jnp.concatenate([jnp.where(block == g, own, 0.0) for g in range(8)], axis=0))
        check = mm3(spread, (kern[0][:, lanes], kern[1][:, lanes]), dot_nt)
        out.append(mm3(split(check), up))
    return out


def pack(rows):
    low, high = rows[:, :128], rows[:, 128:]
    n = rows.shape[0]
    top = lax.broadcasted_iota(jnp.int32, (n, 128), 0) % 8 < 4
    first = jnp.where(top, low, pltpu.roll(high, 4, 0))
    second = jnp.where(top, pltpu.roll(low, n - 4, 0), high)
    tiles = []
    for m in range(n // 8):
        tiles += [first[8 * m : 8 * m + 8], second[8 * m : 8 * m + 8]]
    return jnp.concatenate(tiles, axis=0)


def unpack(tiles):
    n = tiles.shape[0] // 2
    first = jnp.concatenate([tiles[16 * m : 16 * m + 8] for m in range(n // 8)], axis=0)
    second = jnp.concatenate([tiles[16 * m + 8 : 16 * m + 16] for m in range(n // 8)], axis=0)
    top = lax.broadcasted_iota(jnp.int32, (n, 128), 0) % 8 < 4
    low = jnp.where(top, first, pltpu.roll(second, 4, 0))
    high = jnp.where(top, pltpu.roll(first, n - 4, 0), second)
    return jnp.concatenate([low, high], axis=1)


def tile_dot(tile, high, low, acc):
    a_high, a_low = split(tile)
    both = jnp.concatenate([a_high, a_low], axis=0)
    rest = SUB - 128
    front = dot(both, high[:128]) + dot(both, low[:128])
    back = dot(both[:, :rest], high[128:]) + dot(both[:, :rest], low[128:])
    return acc[0] + front, acc[1] + back


def tile_sum(acc):
    front = acc[0][:8] + acc[0][8:]
    back = acc[1][:8] + acc[1][8:]
    return front + pltpu.roll(back, 4, 0)


def head_kernel(
    off_hbm, q_hbm, counts_hbm, up_hbm, down_hbm, col_hbm, row_hbm,
    out_ref, halo_ref, up_ref, down_ref, col_ref, row_ref,
    off_ref, q_ref, counts_ref, pad_ref, tab_ref, sems,
):
    moves = [
        pltpu.make_async_copy(src, dst, sems.at[n])
        for n, (src, dst) in enumerate(
            (
                (q_hbm, q_ref),
                (off_hbm, off_ref),
                (counts_hbm, counts_ref),
                (up_hbm, up_ref),
                (col_hbm, col_ref),
                (row_hbm, row_ref),
                (down_hbm, down_ref),
            )
        )
    ]
    for move in moves:
        move.start()
    for move in moves[:-1]:
        move.wait()
    lane = lax.broadcasted_iota(jnp.int32, (8, POINTS), 1)
    limit = jnp.zeros((8, POINTS), jnp.int32)
    for g in range(LEAVES):
        limit = jnp.where(lane // SLOTS == g, counts_ref[g], limit)
    filled = (lane % SLOTS < limit)[0:1]
    charges = jnp.where(filled, q_ref[...], 0.0)
    halo_ref[0:RHS, :] = charges
    halo_ref[RHS:ROWS, :] = jnp.zeros((ROWS - RHS, POINTS), F32)
    halo_ref[RHS : RHS + 3, :] = off_ref[...]
    kern = split(leaf_kernel(off_ref[...], col_ref))
    up = padded(up_ref, pad_ref, 18.0 / TERMS)
    up = (up[0][:, :], up[1][:, :])
    halves = leaf_equivalents(charges, kern, up)
    equiv = [split(h) for h in halves]
    acc = jnp.zeros((RHS, LANE), F32)
    for (x, y, z), kern in box_kernels(
        (1.5, 0.5, -0.5, -1.5), (0.5, -0.5), (0.5, -0.5), 6.0, 0.9, col_ref, row_ref, tab_ref
    ):
        half, g = (x >> 1), (x & 1) + 2 * y + 4 * z
        rows = slice(g * RHS, g * RHS + RHS)
        acc = acc + mm3((equiv[half][0][rows, :SUB], equiv[half][1][rows, :SUB]), split(kern))
    up60 = padded(up_ref, pad_ref, 60.0 / TERMS)
    out_ref[...] = pack(mm3(split(acc[:, :SUB]), up60))
    moves[-1].wait()


def group_up_kernel(x_ref, maps_ref, up_ref, out_ref, pad_ref):
    acc = (jnp.zeros((16, LANE), F32), jnp.zeros((16, LANE), F32))
    for e in range(INNER):
        acc = tile_dot(x_ref[8 * e : 8 * e + 8, :], maps_ref[e, 0], maps_ref[e, 1], acc)
    check = tile_sum(acc)
    both = jnp.concatenate([check, check], axis=0)
    equiv = mm3(split(both[:, :SUB]), padded(up_ref, pad_ref, 200.0 / TERMS))[:8]
    top = lax.broadcasted_iota(jnp.int32, (8, 128), 0) < 4
    tile = jnp.where(top, equiv[:, :128], pltpu.roll(equiv[:, 128:], 4, 0))
    for p in range(OUTER):
        out_ref[8 * p : 8 * p + 8, :] = tile


def box_order(rows):
    return jnp.concatenate(
        [rows[8 * k : 8 * k + 8] for k in (y * 4 + x * 2 + z for x in (0, 1) for z in (0, 1) for y in (0, 1))], axis=0
    )


def index_order(rows):
    return jnp.concatenate(
        [rows[8 * k : 8 * k + 8] for k in (x * 4 + z * 2 + y for y in (0, 1) for x in (0, 1) for z in (0, 1))], axis=0
    )


def peers_kernel(x_ref, col_ref, row_ref, out_ref, tab_ref, shifted_ref):
    equiv = jnp.concatenate([box_order(unpack(x_ref[...])), jnp.zeros((16, LANE), F32)], axis=0)
    shifted_ref[...] = jnp.zeros_like(shifted_ref)
    for q in range(4):
        high, low = split(pltpu.roll(equiv, 4 * q, 0) if q else equiv)
        shifted_ref[q, 0, RHS : RHS + 80, :] = high
        shifted_ref[q, 1, RHS : RHS + 80, :] = low
    cols = columns(col_ref)
    for dy in range(-3, 4):
        tab_ref[dy + 3] = square_of(1, 2.0 * dy, 3.0, 3.0, cols, row_ref) + SOFTEN
    row = lax.broadcasted_iota(jnp.int32, (RHS, 128), 0)
    lane = lax.broadcasted_iota(jnp.int32, (RHS, 128), 1)
    px, pz, py = row >> 5, (row >> 4) & 1, (row >> 2) & 3
    dest = (py & 1) + pz * 2 + px * 4 + (py >> 1) * 8

    def step(turn, acc):
        dx = turn // 3 - 1
        dz = turn % 3 - 1
        sx, sy, sz = px - dx, py - (lane - 3), pz - dz
        inside = (sx >= 0) & (sx < 2) & (sy >= 0) & (sy < 4) & (sz >= 0) & (sz < 2)
        source = (sy & 1) + sz * 2 + sx * 4 + (sy >> 1) * 8
        mask = (inside & (jnp.abs(source - dest) >= 2)).astype(F32)
        plane = square_of(0, dx.astype(F32) * 4.0, 3.0, 3.0, cols, row_ref)
        plane = plane + square_of(2, dz.astype(F32) * 2.0, 3.0, 3.0, cols, row_ref)
        tab_ref[7] = plane
        for dy in range(-3, 4):
            q = dy % 4
            start = pl.multiple_of(RHS - (dx * 2 + dz) * 16 - 4 * (dy - q), 16)
            keep = two(jnp.broadcast_to(mask[:, dy + 3 : dy + 4], (RHS, 128))).astype(BF)
            high = shifted_ref[q, 0, pl.ds(start, RHS), :] * keep
            low = shifted_ref[q, 1, pl.ds(start, RHS), :] * keep
            kern = split(lax.rsqrt(tab_ref[7] + tab_ref[dy + 3]))
            acc = acc + mm3((high[:, :SUB], low[:, :SUB]), kern)
        return acc

    out_ref[...] = index_order(lax.fori_loop(0, 9, step, jnp.zeros((RHS, LANE), F32)))


def local_kernel(x_ref, peers_ref, down_ref, col_ref, row_ref, out_ref, pad_ref, tab_ref):
    outer = lax.axis_index("outer")
    own = [p.astype(F32) for p in corner(outer * 256, 8)]
    cols = columns(col_ref)
    for n in range(4):
        tab_ref[n] = square_of(2, own[2] - 4.0 * n, 10.0, 20.0, cols, row_ref) + SOFTEN
    for x in range(4):
        xsq = square_of(0, own[0] - 8.0 * x, 10.0, 20.0, cols, row_ref)
        for y in range(2):
            tab_ref[4 + x * 2 + y] = xsq + square_of(1, own[1] - 8.0 * y, 10.0, 20.0, cols, row_ref)
    acc = (jnp.zeros((16, LANE), F32), jnp.zeros((16, LANE), F32))
    for p in range(OUTER):
        z, x, y = (p & 1) + ((p >> 3) & 1) * 2, ((p >> 1) & 1) + ((p >> 4) & 1) * 2, (p >> 2) & 1
        weight = (jnp.abs(p - outer) >= 2).astype(F32)
        kern = split(lax.rsqrt(tab_ref[4 + x * 2 + y] + tab_ref[z]))
        acc = tile_dot(x_ref[8 * p : 8 * p + 8, :] * weight, kern[0], kern[1], acc)
    check = tile_sum(acc)
    both = jnp.concatenate([check, check], axis=0)
    group = mm3(split(both[:, :SUB]), padded(down_ref, pad_ref, 200.0 / TERMS))[:8]
    pieces = jnp.concatenate(split(group[:, :SUB]), axis=0)
    top = lax.broadcasted_iota(jnp.int32, (8, LANE), 0) < 4
    found = [None] * INNER
    for (x, y, z), kern in box_kernels(
        (-2.0, 2.0), (-3.0, -1.0, 1.0, 3.0), (-1.0, 1.0), 3.0, 20.0, col_ref, row_ref, tab_ref
    ):
        high, low = split(kern)
        part = dot(pieces, high) + dot(pieces, low)
        found[(y & 1) + z * 2 + x * 4 + (y >> 1) * 8] = part[:8] + part[8:]
    merged = [jnp.where(top, found[2 * m], pltpu.roll(found[2 * m + 1], 4, 0)) for m in range(INNER // 2)]
    total = jnp.concatenate(merged, axis=0) + peers_ref[...]
    out_ref[...] = pack(mm3(split(total[:, :SUB]), padded(down_ref, pad_ref, 60.0 / TERMS)))


def up_maps_kernel(flow_ref, col_ref, row_ref, out_ref, tab_ref):
    for (x, y, z), kern in box_kernels(
        (2.0, -2.0), (3.0, 1.0, -1.0, -3.0), (1.0, -1.0), 20.0, 3.0, col_ref, row_ref, tab_ref
    ):
        d = (y & 1) + z * 2 + x * 4 + (y >> 1) * 8
        high, low = split(kern)
        out_ref[d, 0, :, :] = high
        out_ref[d, 1, :, :] = low


def operator_kernel(own_ref, down_ref, col_ref, row_ref, w_ref, m_ref, pad_ref, tab_ref):
    off = own_ref[RHS : RHS + 3, :]
    down = padded(down_ref, pad_ref, 18.0 / TERMS)
    down = (down[0][:, :SUB], down[1][:, :SUB])
    weights = split(mm3(down, split(leaf_kernel(off, col_ref))))
    w_ref[0, :, :] = weights[0]
    w_ref[1, :, :] = weights[1]
    block = lax.broadcasted_iota(jnp.int32, (SUB, 256), 1) // SLOTS
    found = [jnp.zeros((SUB, 256), F32)] * 2
    for (x, y, z), kern in box_kernels(
        (-1.5, -0.5, 0.5, 1.5), (-0.5, 0.5), (-0.5, 0.5), 0.9, 6.0, col_ref, row_ref, tab_ref
    ):
        half, g = (x >> 1), (x & 1) + 2 * y + 4 * z
        lanes = slice(half * 256, half * 256 + 256)
        own = (weights[0][:, lanes], weights[1][:, lanes])
        found[half] = jnp.where(block == g, mm3(split(kern[:, :SUB]), own), found[half])
    for half in range(2):
        lanes = slice(half * 256, half * 256 + 256)
        m_high, m_low = split(found[half])
        m_ref[0, :, lanes] = m_high
        m_ref[1, :, lanes] = m_low


def near_kernel(near_ref, left_ref, own_ref, right_ref, out_ref, mask_ref, high_ref, low_ref):
    offs = jnp.concatenate([own_ref[RHS:ROWS, :], jnp.zeros((120, POINTS), F32)], axis=0).T
    inner = lax.axis_index("inner")
    device = lax.axis_index("outer") * INNER + inner
    base = (device - 1) * LEAVES
    total = 3 * POINTS
    lane = lax.broadcasted_iota(jnp.int32, (LEAVES, total), 1) // SLOTS
    found = jnp.zeros((LEAVES, total), F32)
    near = near_ref[...] - base
    for k in range(12):
        found = jnp.where(lane == near[:, k : k + 1], 1.0, found)
    mask_ref[...] = found
    leaf = lax.broadcasted_iota(jnp.int32, (1, POINTS), 1) // SLOTS
    within = local_leaf(leaf)
    own_box = corner(device * LEAVES, 4)
    sources = []
    for c in range(3):
        lanes = []
        for side, ref in ((-1, left_ref), (0, own_ref), (1, right_ref)):
            box = corner((device + side) * LEAVES, 4)[c] - own_box[c]
            lanes.append(ref[RHS + c : RHS + c + 1, :] + (box + within[c]).astype(F32))
        sources.append(jnp.concatenate(lanes, axis=1))
    for g in range(LEAVES):
        rows = slice(g * SLOTS, g * SLOTS + SLOTS)
        place = local_leaf(g)
        dist = SOFTEN
        for c in range(3):
            diff = (offs[rows, c : c + 1] + float(place[c])) - sources[c]
            dist = dist + diff * diff
        k_high, k_low = split(lax.rsqrt(dist) * mask_ref[g : g + 1, :])
        high_ref[rows, :] = k_high
        low_ref[rows, :] = k_low
    charges = jnp.concatenate([r[0:RHS, :] for r in (left_ref, own_ref, right_ref)], axis=1)
    q_high, q_low = split(charges)
    both = jnp.concatenate([q_high, q_low], axis=0)
    res = dot_nt(high_ref[...], both)
    res = res + jnp.concatenate([dot_nt(low_ref[...], q_high), jnp.zeros((POINTS, RHS), F32)], axis=1)
    flipped = res.T
    out_ref[...] = flipped[:RHS] + flipped[RHS:]


def far_kernel(far_ref, left_ref, own_ref, right_ref, w_ref, up_ref, near_ref, col_ref, row_ref, out_ref, pad_ref, e_ref, dl_ref, xtab_ref, tab_ref):
    inner = lax.axis_index("inner")
    device = lax.axis_index("outer") * INNER + inner
    up = padded(up_ref, pad_ref, 18.0 / TERMS)
    for side, ref in enumerate((left_ref, own_ref, right_ref)):
        kern = split(leaf_kernel(ref[RHS : RHS + 3, :], col_ref))
        halves = leaf_equivalents(ref[0:RHS, :], kern, up)
        for half in range(2):
            e_high, e_low = split(halves[half])
            for g in range(8):
                start = ((side * 2 + half) * 8 + g) * 2 * RHS
                e_ref[start : start + RHS, :] = e_high[g * RHS : g * RHS + RHS]
                e_ref[start + RHS : start + 2 * RHS, :] = e_low[g * RHS : g * RHS + RHS]
    first = (device - 1) * LEAVES
    boxes = [corner((device + side) * LEAVES, 4) for side in (-1, 0, 1)]
    boxes = [[(boxes[1][c] - box[c]).astype(F32) for c in range(3)] for box in boxes]
    cols = columns(col_ref)
    for side in range(3):
        for n in range(7):
            xtab_ref[side * 7 + n] = square_of(0, boxes[side][0] + (n - 3.0), 0.9, 1.8, cols, row_ref)
        for c in range(3):
            tab_ref[27 + c] = square_of(2, boxes[side][2] + (c - 1.0), 0.9, 1.8, cols, row_ref) + SOFTEN
        for b in range(3):
            ysq = square_of(1, boxes[side][1] + (b - 1.0), 0.9, 1.8, cols, row_ref)
            for c in range(3):
                tab_ref[side * 9 + b * 3 + c] = ysq + tab_ref[27 + c]

    def one_leaf(g, carry):
        own = local_leaf(g)
        acc = jnp.zeros((RHS, LANE), F32)
        for k in range(12):
            window = far_ref[g, k] - first
            side = window >> 4
            place = local_leaf(window & 15)
            x = side * 7 + 3 + own[0] - place[0]
            yz = side * 9 + 4 + (own[1] - place[1]) * 3 + own[2] - place[2]
            k_high, k_low = split(lax.rsqrt(xtab_ref[x] + tab_ref[yz]))
            start = pl.multiple_of(window * (2 * RHS), 2 * RHS)
            equiv = e_ref[pl.ds(start, 2 * RHS), :][:, :SUB]
            wide = dot(equiv, k_high)
            acc = acc + wide[:RHS] + wide[RHS:] + dot(equiv[:RHS], k_low)
        high, low = split(acc)
        start = pl.multiple_of(g * RHS, RHS)
        dl_ref[0, pl.ds(start, RHS), :] = high
        dl_ref[1, pl.ds(start, RHS), :] = low
        return carry

    lax.fori_loop(0, LEAVES, one_leaf, 0)
    block = lax.broadcasted_iota(jnp.int32, (RHS, 256), 1) // SLOTS
    for half in range(2):
        lanes = slice(half * 256, half * 256 + 256)
        rows = slice(half * 8 * RHS, (half + 1) * 8 * RHS)
        local = (dl_ref[0, rows, :][:, :SUB], dl_ref[1, rows, :][:, :SUB])
        res = mm3(local, (w_ref[0, :, lanes], w_ref[1, :, lanes]))
        acc = near_ref[:, lanes]
        for g in range(8):
            acc = acc + jnp.where(block == g, res[g * RHS : (g + 1) * RHS], 0.0)
        out_ref[:, lanes] = acc


def tail_kernel(x_ref, base_ref, m_ref, out_ref):
    local = split(unpack(x_ref[...])[:, :SUB])
    out_ref[...] = base_ref[...] + mm3(local, (m_ref[0], m_ref[1]))


VM = pl.BlockSpec(memory_space=pltpu.VMEM)
SM = pl.BlockSpec(memory_space=pltpu.SMEM)


def call(kernel, name, outs, specs, scratch, vmem, *args):
    return pl.pallas_call(
        kernel,
        name=name,
        out_shape=outs,
        in_specs=specs,
        out_specs=jax.tree.map(lambda _: VM, outs),
        scratch_shapes=scratch,
        compiler_params=pltpu.CompilerParams(vmem_limit_bytes=vmem * 1024 * 1024),
        cost_estimate=pl.CostEstimate(flops=1000, bytes_accessed=1000, transcendentals=0),
    )(*args)


def tie(value, *others):
    return lax.optimization_barrier((value,) + others)[0]


def shards(offsets, charges, counts, near, far, upward, downward):
    col_np, row_np = sphere_tables()
    sds = jax.ShapeDtypeStruct
    pad = pltpu.VMEM((SUB, LANE), F32)
    flow = sds((2 * RHS, 128), F32)
    square = sds((TERMS, TERMS), F32)

    def tables(n):
        return pltpu.VMEM((n, SUB, LANE), F32)

    def maps(n):
        return sds((n, 2, SUB, LANE), BF)

    inputs = (offsets, charges, counts, upward, downward, jnp.asarray(col_np), jnp.asarray(row_np))
    dev_equiv, own, upward, downward, col, row = call(
        head_kernel, "leaf_and_device_equiv",
        (flow, sds((ROWS, POINTS), F32), square, square, sds((SUB, 128), F32), sds((8, LANE), F32)),
        [pl.BlockSpec(memory_space=pltpu.HBM)] * 7,
        [
            pltpu.VMEM((3, POINTS), F32),
            pltpu.VMEM((RHS, POINTS), F32),
            pltpu.SMEM((LEAVES,), jnp.int32),
            pad,
            tables(10),
            pltpu.SemaphoreType.DMA((7,)),
        ],
        16, *(pltpu.with_memory_space_constraint(a, pltpu.HBM) for a in inputs),
    )
    peers_equiv = lax.all_to_all(dev_equiv, "inner", 0, 0, tiled=True)
    up_maps = call(up_maps_kernel, "up_maps", maps(INNER), [VM, VM, VM], [tables(14)], 12, dev_equiv, col, row)
    ends = INNER - 1
    left = lax.ppermute(own, "inner", [(i, i + 1) for i in range(ends)])
    right = lax.ppermute(own, "inner", [(i + 1, i) for i in range(ends)])
    group_equiv = call(
        group_up_kernel, "group_equiv", sds((8 * OUTER, 128), F32), [VM, VM, VM], [pad], 6,
        peers_equiv, up_maps, upward,
    )
    groups = lax.all_to_all(group_equiv, "outer", 0, 0, tiled=True)
    peers_part = call(
        peers_kernel, "device_to_device", sds((RHS, LANE), F32), [VM, VM, VM],
        [tables(8), pltpu.VMEM((4, 2, 3 * RHS, LANE), BF)], 6, peers_equiv, col, row,
    )
    groups = tie(groups, peers_part)
    local = call(
        local_kernel, "group_and_device_local", flow, [VM, VM, VM, VM, VM], [pad, tables(14)], 8,
        groups, peers_part, downward, col, row,
    )
    dev_local = lax.all_to_all(local, "inner", 0, 0, tiled=True)
    weights, evaluate = call(
        operator_kernel, "evaluation_maps", (sds((2, SUB, POINTS), BF), sds((2, SUB, POINTS), BF)),
        [VM, VM, VM, VM], [pad, tables(10)], 12, own, downward, col, row,
    )
    near_part = call(
        near_kernel, "near_field", sds((RHS, POINTS), F32), [VM, VM, VM, VM],
        [pltpu.VMEM((LEAVES, 3 * POINTS), F32), pltpu.VMEM((POINTS, 3 * POINTS), BF), pltpu.VMEM((POINTS, 3 * POINTS), BF)],
        14, near, left, own, right,
    )
    base = call(
        far_kernel, "far_field", sds((RHS, POINTS), F32), [SM, VM, VM, VM, VM, VM, VM, VM, VM],
        [
            pad,
            pltpu.VMEM((3 * LEAVES * 2 * RHS, LANE), BF),
            pltpu.VMEM((2, LEAVES * RHS, LANE), BF),
            tables(21),
            tables(30),
        ],
        24, far, left, own, right, weights, upward, near_part, col, row,
    )
    return call(tail_kernel, "potential", sds((RHS, POINTS), F32), [VM, VM, VM], [], 4, dev_local, base, evaluate)


def solution(mesh):
    both = ("outer", "inner")
    in_specs = (P(None, both), P(None, both), P(both), P(both, None), P(both, None), P(), P())
    return jax.shard_map(shards, mesh=mesh, in_specs=in_specs, out_specs=P(None, both), check_vma=False)
```

```python
import functools

import jax
import jax.numpy as jnp
import numpy as np
from jax import lax
from jax.experimental import pallas as pl
from jax.experimental.pallas import tpu as pltpu
from jax.sharding import PartitionSpec as P

SOFTEN = 0.25
GOLDEN = 2.399963229728653
RHS = 64
TERMS = 165
SUB = 176
LANE = 256
LEAVES = 16
SLOTS = 32
POINTS = LEAVES * SLOTS
ROWS = 72
INNER = 16
OUTER = 32
PART = RHS // INNER
BF = jnp.bfloat16
F32 = jnp.float32


def sphere_tables():
    steps = np.arange(TERMS, dtype=np.float32)
    height = (np.float32(1.0) - (np.float32(2.0) * steps + np.float32(1.0)) / np.float32(TERMS)).astype(np.float32)
    radial = np.sqrt(np.maximum(np.float32(1.0) - height * height, np.float32(0.0))).astype(np.float32)
    angle = (steps * np.float32(GOLDEN)).astype(np.float32)
    dirs = np.stack([radial * np.cos(angle), radial * np.sin(angle), height]).astype(np.float32)
    col = np.zeros((SUB, 128), np.float32)
    col[:TERMS, :3] = dirs.T
    row = np.zeros((8, LANE), np.float32)
    row[:3, :TERMS] = dirs
    return col, row


def split(x):
    high = x.astype(BF)
    return high, (x - high.astype(F32)).astype(BF)


def dot(a, b):
    return jnp.dot(a, b, preferred_element_type=F32)


def dot_nt(a, b):
    return lax.dot_general(a, b, (((1,), (1,)), ((), ())), preferred_element_type=F32)


def mm3(a, b, f=dot):
    return f(a[0], b[0]) + f(a[1], b[0]) + f(a[0], b[1])


def columns(col_ref):
    return [jnp.broadcast_to(col_ref[:, c : c + 1], (SUB, 128)) for c in range(3)]


def two(x):
    return jnp.concatenate([x, x], axis=1)


def square_of(axis, shift, radius_t, radius_i, cols, row_ref):
    diff = (radius_t * row_ref[axis : axis + 1, :] + shift) - two(radius_i * cols[axis])
    return diff * diff


def box_kernels(xs, ys, zs, radius_t, radius_i, col_ref, row_ref, tab_ref):
    cols = columns(col_ref)
    for n, shift in enumerate(xs):
        tab_ref[n] = square_of(0, shift, radius_t, radius_i, cols, row_ref)
    zsq = len(xs)
    for n, shift in enumerate(zs):
        tab_ref[zsq + n] = square_of(2, shift, radius_t, radius_i, cols, row_ref) + SOFTEN
    start = zsq + len(zs)
    for b, shift in enumerate(ys):
        ysq = square_of(1, shift, radius_t, radius_i, cols, row_ref)
        for c in range(len(zs)):
            tab_ref[start + b * len(zs) + c] = ysq + tab_ref[zsq + c]
    for b in range(len(ys)):
        for c in range(len(zs)):
            for a in range(len(xs)):
                yield (a, b, c), lax.rsqrt(tab_ref[a] + tab_ref[start + b * len(zs) + c])


def bits(ids, low, axis, top=14):
    total = 0
    for level in range(5):
        place = 3 * level + axis
        if low <= place < top:
            total = total + (((ids >> place) & 1) << level)
    return total


def corner(leaf_id, low):
    return [bits(leaf_id, low, axis) for axis in range(3)]


def local_leaf(index):
    return ((index & 1) + ((index >> 3) & 1) * 2, (index >> 1) & 1, (index >> 2) & 1)


def peer_box(inner):
    return (((inner >> 2) & 1) * 4, (inner & 1) * 2 + ((inner >> 3) & 1) * 4, ((inner >> 1) & 1) * 2)


def leaf_kernel(offs, col_ref):
    total = SOFTEN
    for c in range(3):
        col = jnp.broadcast_to(col_ref[:, c : c + 1], (SUB, 128)) * 1.8
        diff = jnp.concatenate([col] * (POINTS // 128), axis=1) - offs[c : c + 1, :]
        total = total + diff * diff
    return lax.rsqrt(total)


def padded(map_ref, pad_ref, scale):
    pad_ref[...] = jnp.zeros_like(pad_ref)
    pad_ref[0:TERMS, 0:TERMS] = map_ref[...] * scale
    return split(pad_ref[...])


def leaf_equivalents(charges, kern, up):
    block = lax.broadcasted_iota(jnp.int32, (RHS, 256), 1) // SLOTS
    keep = [(block == g).astype(F32).astype(BF) for g in range(8)]
    pieces = split(charges)
    out = []
    for half in range(2):
        lanes = slice(half * 256, half * 256 + 256)
        spread = [jnp.concatenate([piece[:, lanes] * keep[g] for g in range(8)], axis=0) for piece in pieces]
        check = mm3(spread, (kern[0][:, lanes], kern[1][:, lanes]), dot_nt)
        out.append(mm3(split(check), up))
    return out


def store_equivalents(halves, e_ref, first):
    for half in range(2):
        e_high, e_low = split(halves[half])
        for g in range(8):
            start = first + (half * 8 + g) * 2 * RHS
            e_ref[start : start + RHS, :] = e_high[g * RHS : g * RHS + RHS]
            e_ref[start + RHS : start + 2 * RHS, :] = e_low[g * RHS : g * RHS + RHS]


def pack(rows):
    low, high = rows[:, :128], rows[:, 128:]
    n = rows.shape[0]
    top = lax.broadcasted_iota(jnp.int32, (n, 128), 0) % 8 < 4
    first = jnp.where(top, low, pltpu.roll(high, 4, 0))
    second = jnp.where(top, pltpu.roll(low, n - 4, 0), high)
    tiles = []
    for m in range(n // 8):
        tiles += [first[8 * m : 8 * m + 8], second[8 * m : 8 * m + 8]]
    return jnp.concatenate(tiles, axis=0)


def unpack(tiles):
    n = tiles.shape[0] // 2
    first = jnp.concatenate([tiles[16 * m : 16 * m + 8] for m in range(n // 8)], axis=0)
    second = jnp.concatenate([tiles[16 * m + 8 : 16 * m + 16] for m in range(n // 8)], axis=0)
    top = lax.broadcasted_iota(jnp.int32, (n, 128), 0) % 8 < 4
    low = jnp.where(top, first, pltpu.roll(second, 4, 0))
    high = jnp.where(top, pltpu.roll(first, n - 4, 0), second)
    return jnp.concatenate([low, high], axis=1)


def tile_dot(tile, high, low, acc):
    a_high, a_low = split(tile)
    both = jnp.concatenate([a_high, a_low], axis=0)
    rest = SUB - 128
    front = dot(both, high[:128]) + dot(both, low[:128])
    back = dot(both[:, :rest], high[128:]) + dot(both[:, :rest], low[128:])
    return acc[0] + front, acc[1] + back


def tile_sum(acc):
    front = acc[0][:8] + acc[0][8:]
    back = acc[1][:8] + acc[1][8:]
    return front + pltpu.roll(back, 4, 0)


def head_kernel(
    off_hbm, q_hbm, counts_hbm, up_hbm, down_hbm, col_hbm, row_hbm,
    out_ref, halo_ref, up_ref, down_ref, col_ref, row_ref, e_hbm,
    off_ref, q_ref, counts_ref, pad_ref, tab_ref, e_ref, sems,
):
    moves = [
        pltpu.make_async_copy(src, dst, sems.at[n])
        for n, (src, dst) in enumerate(
            (
                (q_hbm, q_ref),
                (off_hbm, off_ref),
                (counts_hbm, counts_ref),
                (up_hbm, up_ref),
                (col_hbm, col_ref),
                (row_hbm, row_ref),
                (down_hbm, down_ref),
            )
        )
    ]
    for move in moves:
        move.start()
    for move in moves[:-1]:
        move.wait()
    lane = lax.broadcasted_iota(jnp.int32, (8, POINTS), 1)
    limit = jnp.zeros((8, POINTS), jnp.int32)
    for g in range(LEAVES):
        limit = jnp.where(lane // SLOTS == g, counts_ref[g], limit)
    filled = (lane % SLOTS < limit)[0:1]
    charges = jnp.where(filled, q_ref[...], 0.0)
    halo_ref[0:RHS, :] = charges
    halo_ref[RHS:ROWS, :] = jnp.zeros((ROWS - RHS, POINTS), F32)
    halo_ref[RHS : RHS + 3, :] = off_ref[...]
    kern = split(leaf_kernel(off_ref[...], col_ref))
    up = padded(up_ref, pad_ref, 18.0 / TERMS)
    up = (up[0][:, :], up[1][:, :])
    halves = leaf_equivalents(charges, kern, up)
    store_equivalents(halves, e_ref, 0)
    e_move = pltpu.make_async_copy(e_ref, e_hbm, sems.at[7])
    e_move.start()
    acc = jnp.zeros((RHS, LANE), F32)
    for (x, y, z), kern in box_kernels(
        (1.5, 0.5, -0.5, -1.5), (0.5, -0.5), (0.5, -0.5), 6.0, 0.9, col_ref, row_ref, tab_ref
    ):
        start = ((x >> 1) * 8 + (x & 1) + 2 * y + 4 * z) * 2 * RHS
        high, low = split(kern)
        wide = dot(e_ref[start : start + 2 * RHS, :][:, :SUB], high)
        acc = acc + wide[:RHS] + wide[RHS:] + dot(e_ref[start : start + RHS, :][:, :SUB], low)
    up60 = padded(up_ref, pad_ref, 60.0 / TERMS)
    out_ref[...] = pack(mm3(split(acc[:, :SUB]), up60))
    moves[-1].wait()
    e_move.wait()


def group_up_kernel(x_ref, maps_ref, up_ref, out_hbm, pad_ref, out_ref, sem):
    acc = (jnp.zeros((16, LANE), F32), jnp.zeros((16, LANE), F32))
    for e in range(INNER):
        acc = tile_dot(x_ref[8 * e : 8 * e + 8, :], maps_ref[e, 0], maps_ref[e, 1], acc)
    check = tile_sum(acc)
    both = jnp.concatenate([check, check], axis=0)
    equiv = mm3(split(both[:, :SUB]), padded(up_ref, pad_ref, 200.0 / TERMS))[:8]
    top = lax.broadcasted_iota(jnp.int32, (8, 128), 0) < 4
    tile = jnp.where(top, equiv[:, :128], pltpu.roll(equiv[:, 128:], 4, 0))
    for p in range(OUTER):
        out_ref[8 * p : 8 * p + 8, :] = tile
    move = pltpu.make_async_copy(out_ref, out_hbm, sem)
    move.start()
    move.wait()


def box_order(rows):
    return jnp.concatenate(
        [rows[8 * k : 8 * k + 8] for k in (y * 4 + x * 2 + z for x in (0, 1) for z in (0, 1) for y in (0, 1))], axis=0
    )


def index_order(rows):
    return jnp.concatenate(
        [rows[8 * k : 8 * k + 8] for k in (x * 4 + z * 2 + y for y in (0, 1) for x in (0, 1) for z in (0, 1))], axis=0
    )


def peers_kernel(x_ref, col_ref, row_ref, out_ref, tab_ref, shifted_ref):
    equiv = jnp.concatenate([box_order(unpack(x_ref[...])), jnp.zeros((16, LANE), F32)], axis=0)
    shifted_ref[...] = jnp.zeros_like(shifted_ref)
    for q in range(4):
        high, low = split(pltpu.roll(equiv, 4 * q, 0) if q else equiv)
        shifted_ref[q, 0, RHS : RHS + 80, :] = high
        shifted_ref[q, 1, RHS : RHS + 80, :] = low
    cols = columns(col_ref)
    for dy in range(-3, 4):
        tab_ref[dy + 3] = square_of(1, 2.0 * dy, 3.0, 3.0, cols, row_ref) + SOFTEN
    row = lax.broadcasted_iota(jnp.int32, (RHS, 128), 0)
    lane = lax.broadcasted_iota(jnp.int32, (RHS, 128), 1)
    px, pz, py = row >> 5, (row >> 4) & 1, (row >> 2) & 3
    dest = (py & 1) + pz * 2 + px * 4 + (py >> 1) * 8

    def valid(dx, dz):
        sx, sy, sz = px - dx, py - (lane - 3), pz - dz
        inside = (sx >= 0) & (sx < 2) & (sy >= 0) & (sy < 4) & (sz >= 0) & (sz < 2)
        source = (sy & 1) + sz * 2 + sx * 4 + (sy >> 1) * 8
        return (inside & (jnp.abs(source - dest) >= 2)).astype(F32)

    def moved(dx, dy, dz, mask):
        q = dy % 4
        start = pl.multiple_of(RHS - (dx * 2 + dz) * 16 - 4 * (dy - q), 16)
        keep = two(jnp.broadcast_to(mask[:, dy + 3 : dy + 4], (RHS, 128))).astype(BF)
        rows = [(shifted_ref[q, n, pl.ds(start, RHS), :] * keep)[:, :SUB] for n in range(2)]
        return rows

    def both_ways(dx, dz, steps, acc):
        plane = square_of(0, dx.astype(F32) * 4.0, 3.0, 3.0, cols, row_ref)
        tab_ref[7] = plane + square_of(2, dz.astype(F32) * 2.0, 3.0, 3.0, cols, row_ref)
        ahead, behind = valid(dx, dz), valid(-dx, -dz)
        forward, backward = acc
        for dy in steps:
            kern = split(lax.rsqrt(tab_ref[7] + tab_ref[dy + 3]))
            forward = forward + mm3(moved(dx, dy, dz, ahead), kern)
            kern = (kern[0][:, :SUB], kern[1][:, :SUB])
            backward = backward + mm3(moved(-dx, -dy, -dz, behind), kern, dot_nt)
        return forward, backward

    zero = jnp.int32(0)
    acc = both_ways(zero, zero, (1, 2, 3), (jnp.zeros((RHS, LANE), F32), jnp.zeros((RHS, SUB), F32)))
    acc = lax.fori_loop(5, 9, lambda n, acc: both_ways(n // 3 - 1, n % 3 - 1, range(-3, 4), acc), acc)
    back = jnp.concatenate([acc[1], jnp.zeros((RHS, LANE - SUB), F32)], axis=1)
    out_ref[...] = index_order(acc[0] + back)


def local_kernel(x_ref, peers_ref, down_ref, col_ref, row_ref, out_ref, pad_ref, tab_ref):
    outer = lax.axis_index("outer")
    own = [p.astype(F32) for p in corner(outer * 256, 8)]
    cols = columns(col_ref)
    for n in range(4):
        tab_ref[n] = square_of(2, own[2] - 4.0 * n, 10.0, 20.0, cols, row_ref) + SOFTEN
    for x in range(4):
        xsq = square_of(0, own[0] - 8.0 * x, 10.0, 20.0, cols, row_ref)
        for y in range(2):
            tab_ref[4 + x * 2 + y] = xsq + square_of(1, own[1] - 8.0 * y, 10.0, 20.0, cols, row_ref)
    acc = (jnp.zeros((16, LANE), F32), jnp.zeros((16, LANE), F32))
    for p in range(OUTER):
        z, x, y = (p & 1) + ((p >> 3) & 1) * 2, ((p >> 1) & 1) + ((p >> 4) & 1) * 2, (p >> 2) & 1
        weight = (jnp.abs(p - outer) >= 2).astype(F32)
        kern = split(lax.rsqrt(tab_ref[4 + x * 2 + y] + tab_ref[z]))
        acc = tile_dot(x_ref[8 * p : 8 * p + 8, :] * weight, kern[0], kern[1], acc)
    check = tile_sum(acc)
    both = jnp.concatenate([check, check], axis=0)
    group = mm3(split(both[:, :SUB]), padded(down_ref, pad_ref, 200.0 / TERMS))[:8]
    pieces = jnp.concatenate(split(group[:, :SUB]), axis=0)
    top = lax.broadcasted_iota(jnp.int32, (8, LANE), 0) < 4
    found = [None] * INNER
    for (x, y, z), kern in box_kernels(
        (-2.0, 2.0), (-3.0, -1.0, 1.0, 3.0), (-1.0, 1.0), 3.0, 20.0, col_ref, row_ref, tab_ref
    ):
        high, low = split(kern)
        part = dot(pieces, high) + dot(pieces, low)
        found[(y & 1) + z * 2 + x * 4 + (y >> 1) * 8] = part[:8] + part[8:]
    merged = [jnp.where(top, found[2 * m], pltpu.roll(found[2 * m + 1], 4, 0)) for m in range(INNER // 2)]
    total = jnp.concatenate(merged, axis=0) + peers_ref[...]
    out_ref[...] = pack(mm3(split(total[:, :SUB]), padded(down_ref, pad_ref, 60.0 / TERMS)))


def operator_kernel(
    flow_ref, off_ref, down_ref, col_ref, row_ref, up_ref, w_hbm, m_hbm, w_ref, m_ref, pad_ref, tab_ref, sems
):
    kern = split(leaf_kernel(off_ref[RHS : RHS + 3, :], col_ref))
    down = padded(down_ref, pad_ref, 18.0 / TERMS)
    down = (down[0][:, :SUB], down[1][:, :SUB])
    weights = split(mm3(down, kern))
    w_ref[0, :, :] = weights[0]
    w_ref[1, :, :] = weights[1]
    w_move = pltpu.make_async_copy(w_ref, w_hbm, sems.at[0])
    w_move.start()
    block = lax.broadcasted_iota(jnp.int32, (SUB, 256), 1) // SLOTS
    found = [jnp.zeros((SUB, 256), F32)] * 2
    for (x, y, z), kern in box_kernels(
        (-1.5, -0.5, 0.5, 1.5), (-0.5, 0.5), (-0.5, 0.5), 0.9, 6.0, col_ref, row_ref, tab_ref
    ):
        half, g = (x >> 1), (x & 1) + 2 * y + 4 * z
        lanes = slice(half * 256, half * 256 + 256)
        own = (weights[0][:, lanes], weights[1][:, lanes])
        found[half] = jnp.where(block == g, mm3(split(kern[:, :SUB]), own), found[half])
    for half in range(2):
        lanes = slice(half * 256, half * 256 + 256)
        m_high, m_low = split(found[half])
        m_ref[0, :, lanes] = m_high
        m_ref[1, :, lanes] = m_low
    m_move = pltpu.make_async_copy(m_ref, m_hbm, sems.at[1])
    m_move.start()
    for (x, y, z), kern in box_kernels(
        (2.0, -2.0), (3.0, 1.0, -1.0, -3.0), (1.0, -1.0), 20.0, 3.0, col_ref, row_ref, tab_ref
    ):
        e = (y & 1) + z * 2 + x * 4 + (y >> 1) * 8
        high, low = split(kern)
        up_ref[e, 0, :, :] = high
        up_ref[e, 1, :, :] = low
    w_move.wait()
    m_move.wait()


def near_field(near_ref, left_ref, own_ref, right_ref, out_ref, mask_ref, high_ref, low_ref):
    offs = jnp.concatenate([own_ref[RHS:ROWS, :], jnp.zeros((120, POINTS), F32)], axis=0).T
    inner = lax.axis_index("inner")
    device = lax.axis_index("outer") * INNER + inner
    base = (device - 1) * LEAVES
    total = 3 * POINTS
    lane = lax.broadcasted_iota(jnp.int32, (LEAVES, total), 1) // SLOTS
    found = jnp.zeros((LEAVES, total), F32)
    near = near_ref[...] - base
    for k in range(12):
        found = jnp.where(lane == near[:, k : k + 1], 1.0, found)
    mask_ref[...] = found
    leaf = lax.broadcasted_iota(jnp.int32, (1, POINTS), 1) // SLOTS
    within = local_leaf(leaf)
    own_box = corner(device * LEAVES, 4)
    sources = []
    for c in range(3):
        lanes = []
        for side, ref in ((-1, left_ref), (0, own_ref), (1, right_ref)):
            box = corner((device + side) * LEAVES, 4)[c] - own_box[c]
            lanes.append(ref[RHS + c : RHS + c + 1, :] + (box + within[c]).astype(F32))
        sources.append(jnp.concatenate(lanes, axis=1))
    for g in range(LEAVES):
        rows = slice(g * SLOTS, g * SLOTS + SLOTS)
        place = local_leaf(g)
        dist = SOFTEN
        for c in range(3):
            diff = (offs[rows, c : c + 1] + float(place[c])) - sources[c]
            dist = dist + diff * diff
        k_high, k_low = split(lax.rsqrt(dist) * mask_ref[g : g + 1, :])
        high_ref[rows, :] = k_high
        low_ref[rows, :] = k_low
    charges = jnp.concatenate([r[0:RHS, :] for r in (left_ref, own_ref, right_ref)], axis=1)
    q_high, q_low = split(charges)
    both = jnp.concatenate([q_high, q_low], axis=0)
    res = dot_nt(high_ref[...], both)
    res = res + jnp.concatenate([dot_nt(low_ref[...], q_high), jnp.zeros((POINTS, RHS), F32)], axis=1)
    flipped = res.T
    out_ref[...] = flipped[:RHS] + flipped[RHS:]


def field_kernel(
    far_ref, near_ref, own_ref, swap_ref, cross_ref, up_ref, col_ref, row_ref, w_hbm, m_hbm, e_hbm, out_ref, m_ref,
    pad_ref, e_ref, dl_ref, xtab_ref, tab_ref, w_ref, left_ref, right_ref, mask_ref, high_ref, low_ref, sems,
):
    middle = LEAVES * 2 * RHS
    moves = [
        pltpu.make_async_copy(e_hbm, e_ref.at[middle : 2 * middle], sems.at[0]),
        pltpu.make_async_copy(w_hbm, w_ref, sems.at[1]),
        pltpu.make_async_copy(m_hbm, m_ref, sems.at[2]),
    ]
    for move in moves:
        move.start()
    odd = lax.rem(lax.axis_index("inner"), 2) == 1
    left_ref[...] = jnp.where(odd, swap_ref[...], cross_ref[...])
    right_ref[...] = jnp.where(odd, cross_ref[...], swap_ref[...])
    near_field(near_ref, left_ref, own_ref, right_ref, out_ref, mask_ref, high_ref, low_ref)
    inner = lax.axis_index("inner")
    device = lax.axis_index("outer") * INNER + inner
    up = padded(up_ref, pad_ref, 18.0 / TERMS)
    for side, ref in ((0, left_ref), (2, right_ref)):
        kern = split(leaf_kernel(ref[RHS : RHS + 3, :], col_ref))
        store_equivalents(leaf_equivalents(ref[0:RHS, :], kern, up), e_ref, side * middle)
    for move in moves:
        move.wait()
    first = (device - 1) * LEAVES
    boxes = [corner((device + side) * LEAVES, 4) for side in (-1, 0, 1)]
    boxes = [[(boxes[1][c] - box[c]).astype(F32) for c in range(3)] for box in boxes]
    cols = columns(col_ref)
    for side in range(3):
        for n in range(7):
            xtab_ref[side * 7 + n] = square_of(0, boxes[side][0] + (n - 3.0), 0.9, 1.8, cols, row_ref)
        for c in range(3):
            tab_ref[27 + c] = square_of(2, boxes[side][2] + (c - 1.0), 0.9, 1.8, cols, row_ref) + SOFTEN
        for b in range(3):
            ysq = square_of(1, boxes[side][1] + (b - 1.0), 0.9, 1.8, cols, row_ref)
            for c in range(3):
                tab_ref[side * 9 + b * 3 + c] = ysq + tab_ref[27 + c]

    def one_leaf(g, carry):
        own = local_leaf(g)
        acc = jnp.zeros((RHS, LANE), F32)
        for k in range(12):
            window = far_ref[g, k] - first
            side = window >> 4
            place = local_leaf(window & 15)
            x = side * 7 + 3 + own[0] - place[0]
            yz = side * 9 + 4 + (own[1] - place[1]) * 3 + own[2] - place[2]
            k_high, k_low = split(lax.rsqrt(xtab_ref[x] + tab_ref[yz]))
            start = pl.multiple_of(window * (2 * RHS), 2 * RHS)
            equiv = e_ref[pl.ds(start, 2 * RHS), :][:, :SUB]
            wide = dot(equiv, k_high)
            acc = acc + wide[:RHS] + wide[RHS:] + dot(equiv[:RHS], k_low)
        high, low = split(acc)
        start = pl.multiple_of(g * RHS, RHS)
        dl_ref[0, pl.ds(start, RHS), :] = high
        dl_ref[1, pl.ds(start, RHS), :] = low
        return carry

    lax.fori_loop(0, LEAVES, one_leaf, 0)
    block = lax.broadcasted_iota(jnp.int32, (RHS, 256), 1) // SLOTS
    for half in range(2):
        lanes = slice(half * 256, half * 256 + 256)
        rows = slice(half * 8 * RHS, (half + 1) * 8 * RHS)
        local = (dl_ref[0, rows, :][:, :SUB], dl_ref[1, rows, :][:, :SUB])
        res = mm3(local, (w_ref[0, :, lanes], w_ref[1, :, lanes]))
        acc = out_ref[:, lanes]
        for g in range(8):
            acc = acc + jnp.where(block == g, res[g * RHS : (g + 1) * RHS], 0.0)
        out_ref[:, lanes] = acc


def tail_kernel(x_ref, base_ref, m_ref, out_ref):
    local = split(unpack(x_ref[...])[:, :SUB])
    out_ref[...] = base_ref[...] + mm3(local, (m_ref[0], m_ref[1]))


VM = pl.BlockSpec(memory_space=pltpu.VMEM)
SM = pl.BlockSpec(memory_space=pltpu.SMEM)
HB = pl.BlockSpec(memory_space=pltpu.HBM)


def call(kernel, name, outs, specs, scratch, vmem, *args, out_specs=None):
    return pl.pallas_call(
        kernel,
        name=name,
        out_shape=outs,
        in_specs=specs,
        out_specs=out_specs or jax.tree.map(lambda _: VM, outs),
        scratch_shapes=scratch,
        compiler_params=pltpu.CompilerParams(vmem_limit_bytes=vmem * 1024 * 1024),
        cost_estimate=pl.CostEstimate(flops=1000, bytes_accessed=1000, transcendentals=0),
    )(*args)


def in_hbm(x):
    return pltpu.with_memory_space_constraint(x, pltpu.HBM)


def tie(value, *others):
    return lax.optimization_barrier((value,) + others)[0]


def shards(offsets, charges, counts, near, far, upward, downward):
    col_np, row_np = sphere_tables()
    sds = jax.ShapeDtypeStruct
    pad = pltpu.VMEM((SUB, LANE), F32)
    flow = sds((2 * RHS, 128), F32)
    square = sds((TERMS, TERMS), F32)

    def tables(n):
        return pltpu.VMEM((n, SUB, LANE), F32)

    inputs = (offsets, charges, counts, upward, downward, jnp.asarray(col_np), jnp.asarray(row_np))
    equiv_rows = LEAVES * 2 * RHS
    dev_equiv, own, upward, downward, col, row, equiv = call(
        head_kernel, "leaf_and_device_equiv",
        (flow, sds((ROWS, POINTS), F32), square, square, sds((SUB, 128), F32), sds((8, LANE), F32), pltpu.HBM((equiv_rows, LANE), BF)),
        [HB] * 7,
        [
            pltpu.VMEM((3, POINTS), F32),
            pltpu.VMEM((RHS, POINTS), F32),
            pltpu.SMEM((LEAVES,), jnp.int32),
            pad,
            tables(10),
            pltpu.VMEM((equiv_rows, LANE), BF),
            pltpu.SemaphoreType.DMA((8,)),
        ],
        16, *map(in_hbm, inputs), out_specs=(VM, VM, VM, VM, VM, VM, HB),
    )
    peers_equiv = lax.all_to_all(dev_equiv, "inner", 0, 0, tiled=True)
    leaf_maps = pltpu.HBM((2, SUB, POINTS), BF)
    up_maps, weights, evaluate = call(
        operator_kernel, "evaluation_and_group_maps", (sds((INNER, 2, SUB, LANE), BF), leaf_maps, leaf_maps),
        [VM, VM, VM, VM, VM],
        [pltpu.VMEM((2, SUB, POINTS), BF), pltpu.VMEM((2, SUB, POINTS), BF), pad, tables(14), pltpu.SemaphoreType.DMA((2,))],
        14, dev_equiv, own, downward, col, row, out_specs=(VM, HB, HB),
    )
    swap = lax.ppermute(own, "inner", [(i, i ^ 1) for i in range(INNER)])
    cross = lax.ppermute(own, "inner", [(i, ((i + 1) ^ 1) - 1) for i in range(1, INNER - 1)])
    group_equiv = call(
        group_up_kernel, "group_equiv", pltpu.HBM((8 * OUTER, 128), F32), [VM, VM, VM],
        [pad, pltpu.VMEM((8 * OUTER, 128), F32), pltpu.SemaphoreType.DMA], 6,
        peers_equiv, up_maps, upward, out_specs=HB,
    )
    groups = lax.all_to_all(group_equiv, "outer", 0, 0, tiled=True)
    peers_part = call(
        peers_kernel, "device_to_device", sds((RHS, LANE), F32), [VM, VM, VM],
        [tables(8), pltpu.VMEM((4, 2, 3 * RHS, LANE), BF)], 6, peers_equiv, col, row,
    )
    groups = tie(groups, peers_part)
    local = call(
        local_kernel, "group_and_device_local", flow, [VM, VM, VM, VM, VM], [pad, tables(14)], 8,
        groups, peers_part, downward, col, row,
    )
    dev_local = lax.all_to_all(local, "inner", 0, 0, tiled=True)
    base, evaluate = call(
        field_kernel, "near_and_far_field", (sds((RHS, POINTS), F32), sds((2, SUB, POINTS), BF)),
        [SM, VM, VM, VM, VM, VM, VM, VM, HB, HB, HB],
        [
            pad,
            pltpu.VMEM((3 * LEAVES * 2 * RHS, LANE), BF),
            pltpu.VMEM((2, LEAVES * RHS, LANE), BF),
            tables(21),
            tables(30),
            pltpu.VMEM((2, SUB, POINTS), BF),
            pltpu.VMEM((ROWS, POINTS), F32),
            pltpu.VMEM((ROWS, POINTS), F32),
            pltpu.VMEM((LEAVES, 3 * POINTS), F32),
            pltpu.VMEM((POINTS, 3 * POINTS), BF),
            pltpu.VMEM((POINTS, 3 * POINTS), BF),
            pltpu.SemaphoreType.DMA((3,)),
        ],
        32, far, near, own, swap, cross, upward, col, row, in_hbm(weights), in_hbm(evaluate), in_hbm(equiv),
    )
    return call(tail_kernel, "potential", sds((RHS, POINTS), F32), [VM, VM, VM], [], 4, dev_local, base, evaluate)


def solution(mesh):
    both = ("outer", "inner")
    in_specs = (P(None, both), P(None, both), P(both), P(both, None), P(both, None), P(), P())
    return jax.shard_map(shards, mesh=mesh, in_specs=in_specs, out_specs=P(None, both), check_vma=False)
```

```python
import functools

import jax
import jax.numpy as jnp
import numpy as np
from jax import lax
from jax.experimental import pallas as pl
from jax.experimental.pallas import tpu as pltpu
from jax.sharding import PartitionSpec as P

SOFTEN = 0.25
GOLDEN = 2.399963229728653
RHS = 64
TERMS = 165
SUB = 176
LANE = 256
LEAVES = 16
SLOTS = 32
POINTS = LEAVES * SLOTS
ROWS = 72
INNER = 16
OUTER = 32
PART = RHS // INNER
BF = jnp.bfloat16
F32 = jnp.float32


def sphere_tables():
    steps = np.arange(TERMS, dtype=np.float32)
    height = (np.float32(1.0) - (np.float32(2.0) * steps + np.float32(1.0)) / np.float32(TERMS)).astype(np.float32)
    radial = np.sqrt(np.maximum(np.float32(1.0) - height * height, np.float32(0.0))).astype(np.float32)
    angle = (steps * np.float32(GOLDEN)).astype(np.float32)
    dirs = np.stack([radial * np.cos(angle), radial * np.sin(angle), height]).astype(np.float32)
    col = np.zeros((SUB, 128), np.float32)
    col[:TERMS, :3] = dirs.T
    row = np.zeros((8, LANE), np.float32)
    row[:3, :TERMS] = dirs
    return col, row


def split(x):
    high = x.astype(BF)
    return high, (x - high.astype(F32)).astype(BF)


def dot(a, b):
    return jnp.dot(a, b, preferred_element_type=F32)


def dot_nt(a, b):
    return lax.dot_general(a, b, (((1,), (1,)), ((), ())), preferred_element_type=F32)


def mm3(a, b, f=dot):
    return f(a[0], b[0]) + f(a[1], b[0]) + f(a[0], b[1])


def columns(col_ref):
    return [jnp.broadcast_to(col_ref[:, c : c + 1], (SUB, 128)) for c in range(3)]


def two(x):
    return jnp.concatenate([x, x], axis=1)


def square_of(axis, shift, radius_t, radius_i, cols, row_ref):
    diff = (radius_t * row_ref[axis : axis + 1, :] + shift) - two(radius_i * cols[axis])
    return diff * diff


def box_kernels(xs, ys, zs, radius_t, radius_i, col_ref, row_ref, tab_ref):
    cols = columns(col_ref)
    for n, shift in enumerate(xs):
        tab_ref[n] = square_of(0, shift, radius_t, radius_i, cols, row_ref)
    zsq = len(xs)
    for n, shift in enumerate(zs):
        tab_ref[zsq + n] = square_of(2, shift, radius_t, radius_i, cols, row_ref) + SOFTEN
    start = zsq + len(zs)
    for b, shift in enumerate(ys):
        ysq = square_of(1, shift, radius_t, radius_i, cols, row_ref)
        for c in range(len(zs)):
            tab_ref[start + b * len(zs) + c] = ysq + tab_ref[zsq + c]
    for b in range(len(ys)):
        for c in range(len(zs)):
            for a in range(len(xs)):
                yield (a, b, c), lax.rsqrt(tab_ref[a] + tab_ref[start + b * len(zs) + c])


def bits(ids, low, axis, top=14):
    total = 0
    for level in range(5):
        place = 3 * level + axis
        if low <= place < top:
            total = total + (((ids >> place) & 1) << level)
    return total


def corner(leaf_id, low):
    return [bits(leaf_id, low, axis) for axis in range(3)]


def local_leaf(index):
    return ((index & 1) + ((index >> 3) & 1) * 2, (index >> 1) & 1, (index >> 2) & 1)


def peer_box(inner):
    return (((inner >> 2) & 1) * 4, (inner & 1) * 2 + ((inner >> 3) & 1) * 4, ((inner >> 1) & 1) * 2)


def leaf_kernel(offs, col_ref):
    total = SOFTEN
    for c in range(3):
        col = jnp.broadcast_to(col_ref[:, c : c + 1], (SUB, 128)) * 1.8
        diff = jnp.concatenate([col] * (POINTS // 128), axis=1) - offs[c : c + 1, :]
        total = total + diff * diff
    return lax.rsqrt(total)


def padded(map_ref, pad_ref, scale):
    pad_ref[...] = jnp.zeros_like(pad_ref)
    pad_ref[0:TERMS, 0:TERMS] = map_ref[...] * scale
    return split(pad_ref[...])


def leaf_equivalents(charges, kern, up):
    block = lax.broadcasted_iota(jnp.int32, (RHS, 256), 1) // SLOTS
    keep = [(block == g).astype(F32).astype(BF) for g in range(8)]
    pieces = split(charges)
    out = []
    for half in range(2):
        lanes = slice(half * 256, half * 256 + 256)
        spread = [jnp.concatenate([piece[:, lanes] * keep[g] for g in range(8)], axis=0) for piece in pieces]
        check = mm3(spread, (kern[0][:, lanes], kern[1][:, lanes]), dot_nt)
        out.append(mm3(split(check), up))
    return out


def store_equivalents(halves, e_ref, first):
    for half in range(2):
        e_high, e_low = split(halves[half])
        for g in range(8):
            start = first + (half * 8 + g) * 2 * RHS
            e_ref[start : start + RHS, :] = e_high[g * RHS : g * RHS + RHS]
            e_ref[start + RHS : start + 2 * RHS, :] = e_low[g * RHS : g * RHS + RHS]


def pack(rows):
    low, high = rows[:, :128], rows[:, 128:]
    n = rows.shape[0]
    top = lax.broadcasted_iota(jnp.int32, (n, 128), 0) % 8 < 4
    first = jnp.where(top, low, pltpu.roll(high, 4, 0))
    second = jnp.where(top, pltpu.roll(low, n - 4, 0), high)
    tiles = []
    for m in range(n // 8):
        tiles += [first[8 * m : 8 * m + 8], second[8 * m : 8 * m + 8]]
    return jnp.concatenate(tiles, axis=0)


def unpack(tiles):
    n = tiles.shape[0] // 2
    first = jnp.concatenate([tiles[16 * m : 16 * m + 8] for m in range(n // 8)], axis=0)
    second = jnp.concatenate([tiles[16 * m + 8 : 16 * m + 16] for m in range(n // 8)], axis=0)
    top = lax.broadcasted_iota(jnp.int32, (n, 128), 0) % 8 < 4
    low = jnp.where(top, first, pltpu.roll(second, 4, 0))
    high = jnp.where(top, pltpu.roll(first, n - 4, 0), second)
    return jnp.concatenate([low, high], axis=1)


def tile_dot(tile, high, low, acc):
    a_high, a_low = split(tile)
    both = jnp.concatenate([a_high, a_low], axis=0)
    rest = SUB - 128
    front = dot(both, high[:128]) + dot(both, low[:128])
    back = dot(both[:, :rest], high[128:]) + dot(both[:, :rest], low[128:])
    return acc[0] + front, acc[1] + back


def tile_sum(acc):
    front = acc[0][:8] + acc[0][8:]
    back = acc[1][:8] + acc[1][8:]
    return front + pltpu.roll(back, 4, 0)


def head_kernel(
    off_hbm, q_hbm, counts_hbm, up_hbm, down_hbm, col_hbm, row_hbm,
    out_ref, halo_ref, up_ref, down_ref, col_ref, row_ref, e_hbm,
    off_ref, q_ref, counts_ref, pad_ref, tab_ref, e_ref, sems,
):
    moves = [
        pltpu.make_async_copy(src, dst, sems.at[n])
        for n, (src, dst) in enumerate(
            (
                (q_hbm, q_ref),
                (off_hbm, off_ref),
                (counts_hbm, counts_ref),
                (up_hbm, up_ref),
                (col_hbm, col_ref),
                (row_hbm, row_ref),
                (down_hbm, down_ref),
            )
        )
    ]
    for move in moves:
        move.start()
    for move in moves[:-1]:
        move.wait()
    lane = lax.broadcasted_iota(jnp.int32, (8, POINTS), 1)
    limit = jnp.zeros((8, POINTS), jnp.int32)
    for g in range(LEAVES):
        limit = jnp.where(lane // SLOTS == g, counts_ref[g], limit)
    filled = (lane % SLOTS < limit)[0:1]
    charges = jnp.where(filled, q_ref[...], 0.0)
    halo_ref[0:RHS, :] = charges
    halo_ref[RHS:ROWS, :] = jnp.zeros((ROWS - RHS, POINTS), F32)
    halo_ref[RHS : RHS + 3, :] = off_ref[...]
    kern = split(leaf_kernel(off_ref[...], col_ref))
    up = padded(up_ref, pad_ref, 18.0 / TERMS)
    up = (up[0][:, :], up[1][:, :])
    halves = leaf_equivalents(charges, kern, up)
    store_equivalents(halves, e_ref, 0)
    e_move = pltpu.make_async_copy(e_ref, e_hbm, sems.at[7])
    e_move.start()
    acc = jnp.zeros((RHS, LANE), F32)
    for (x, y, z), kern in box_kernels(
        (1.5, 0.5, -0.5, -1.5), (0.5, -0.5), (0.5, -0.5), 6.0, 0.9, col_ref, row_ref, tab_ref
    ):
        start = ((x >> 1) * 8 + (x & 1) + 2 * y + 4 * z) * 2 * RHS
        high, low = split(kern)
        wide = dot(e_ref[start : start + 2 * RHS, :][:, :SUB], high)
        acc = acc + wide[:RHS] + wide[RHS:] + dot(e_ref[start : start + RHS, :][:, :SUB], low)
    up60 = padded(up_ref, pad_ref, 60.0 / TERMS)
    out_ref[...] = pack(mm3(split(acc[:, :SUB]), up60))
    moves[-1].wait()
    e_move.wait()


def group_up_kernel(x_ref, maps_ref, up_ref, out_hbm, pad_ref, out_ref, sem):
    acc = (jnp.zeros((16, LANE), F32), jnp.zeros((16, LANE), F32))
    for e in range(INNER):
        acc = tile_dot(x_ref[8 * e : 8 * e + 8, :], maps_ref[e, 0], maps_ref[e, 1], acc)
    check = tile_sum(acc)
    both = jnp.concatenate([check, check], axis=0)
    equiv = mm3(split(both[:, :SUB]), padded(up_ref, pad_ref, 200.0 / TERMS))[:8]
    top = lax.broadcasted_iota(jnp.int32, (8, 128), 0) < 4
    tile = jnp.where(top, equiv[:, :128], pltpu.roll(equiv[:, 128:], 4, 0))
    for p in range(OUTER):
        out_ref[8 * p : 8 * p + 8, :] = tile
    move = pltpu.make_async_copy(out_ref, out_hbm, sem)
    move.start()
    move.wait()


def box_order(rows):
    return jnp.concatenate(
        [rows[8 * k : 8 * k + 8] for k in (y * 4 + x * 2 + z for x in (0, 1) for z in (0, 1) for y in (0, 1))], axis=0
    )


def index_order(rows):
    return jnp.concatenate(
        [rows[8 * k : 8 * k + 8] for k in (x * 4 + z * 2 + y for y in (0, 1) for x in (0, 1) for z in (0, 1))], axis=0
    )


def peers_kernel(x_ref, col_ref, row_ref, out_ref, tab_ref, shifted_ref):
    equiv = jnp.concatenate([box_order(unpack(x_ref[...])), jnp.zeros((16, LANE), F32)], axis=0)
    shifted_ref[...] = jnp.zeros_like(shifted_ref)
    for q in range(4):
        high, low = split(pltpu.roll(equiv, 4 * q, 0) if q else equiv)
        shifted_ref[q, 0, RHS : RHS + 80, :] = high
        shifted_ref[q, 1, RHS : RHS + 80, :] = low
    cols = columns(col_ref)
    for dy in range(-3, 4):
        tab_ref[dy + 3] = square_of(1, 2.0 * dy, 3.0, 3.0, cols, row_ref) + SOFTEN
    row = lax.broadcasted_iota(jnp.int32, (RHS, 128), 0)
    lane = lax.broadcasted_iota(jnp.int32, (RHS, 128), 1)
    px, pz, py = row >> 5, (row >> 4) & 1, (row >> 2) & 3
    dest = (py & 1) + pz * 2 + px * 4 + (py >> 1) * 8

    def valid(dx, dz):
        sx, sy, sz = px - dx, py - (lane - 3), pz - dz
        inside = (sx >= 0) & (sx < 2) & (sy >= 0) & (sy < 4) & (sz >= 0) & (sz < 2)
        source = (sy & 1) + sz * 2 + sx * 4 + (sy >> 1) * 8
        return (inside & (jnp.abs(source - dest) >= 2)).astype(F32)

    def moved(dx, dy, dz, mask):
        q = dy % 4
        start = RHS - (dx * 2 + dz) * 16 - 4 * (dy - q)
        keep = two(jnp.broadcast_to(mask[:, dy + 3 : dy + 4], (RHS, 128))).astype(BF)
        rows = [(shifted_ref[q, n, start : start + RHS, :] * keep)[:, :SUB] for n in range(2)]
        return rows

    acc = (jnp.zeros((RHS, LANE), F32), jnp.zeros((RHS, SUB), F32))
    planes = [(0, 0, (1, 2, 3))] + [(dx, dz, range(-3, 4)) for dx, dz in ((0, 1), (1, -1), (1, 0), (1, 1))]
    for n, (dx, dz, steps) in enumerate(planes):
        plane = square_of(0, dx * 4.0, 3.0, 3.0, cols, row_ref)
        tab_ref[7 + n] = plane + square_of(2, dz * 2.0, 3.0, 3.0, cols, row_ref)
        ahead, behind = valid(dx, dz), valid(-dx, -dz)
        for dy in steps:
            kern = split(lax.rsqrt(tab_ref[7 + n] + tab_ref[dy + 3]))
            forward = acc[0] + mm3(moved(dx, dy, dz, ahead), kern)
            kern = (kern[0][:, :SUB], kern[1][:, :SUB])
            acc = (forward, acc[1] + mm3(moved(-dx, -dy, -dz, behind), kern, dot_nt))
    back = jnp.concatenate([acc[1], jnp.zeros((RHS, LANE - SUB), F32)], axis=1)
    out_ref[...] = index_order(acc[0] + back)


def local_kernel(x_ref, peers_ref, down_ref, col_ref, row_ref, up_hbm, out_ref, pad_ref, tab_ref, up_ref, sem):
    move = pltpu.make_async_copy(up_hbm, up_ref, sem)
    move.start()
    outer = lax.axis_index("outer")
    own = [p.astype(F32) for p in corner(outer * 256, 8)]
    cols = columns(col_ref)
    for n in range(4):
        tab_ref[n] = square_of(2, own[2] - 4.0 * n, 10.0, 20.0, cols, row_ref) + SOFTEN
    for x in range(4):
        xsq = square_of(0, own[0] - 8.0 * x, 10.0, 20.0, cols, row_ref)
        for y in range(2):
            tab_ref[4 + x * 2 + y] = xsq + square_of(1, own[1] - 8.0 * y, 10.0, 20.0, cols, row_ref)
    acc = (jnp.zeros((16, LANE), F32), jnp.zeros((16, LANE), F32))
    for p in range(OUTER):
        z, x, y = (p & 1) + ((p >> 3) & 1) * 2, ((p >> 1) & 1) + ((p >> 4) & 1) * 2, (p >> 2) & 1
        weight = (jnp.abs(p - outer) >= 2).astype(F32)
        kern = split(lax.rsqrt(tab_ref[4 + x * 2 + y] + tab_ref[z]))
        acc = tile_dot(x_ref[8 * p : 8 * p + 8, :] * weight, kern[0], kern[1], acc)
    check = tile_sum(acc)
    both = jnp.concatenate([check, check], axis=0)
    group = mm3(split(both[:, :SUB]), padded(down_ref, pad_ref, 200.0 / TERMS))[:8]
    pieces = jnp.concatenate(split(group[:, :SUB]), axis=0)
    top = lax.broadcasted_iota(jnp.int32, (8, SUB), 0) < 4
    move.wait()
    found = []
    for d in range(INNER):
        part = dot_nt(pieces, up_ref[d, 0][:, :SUB]) + dot_nt(pieces, up_ref[d, 1][:, :SUB])
        found.append(part[:8] + part[8:])
    merged = [jnp.where(top, found[2 * m], pltpu.roll(found[2 * m + 1], 4, 0)) for m in range(INNER // 2)]
    total = jnp.concatenate(merged, axis=0) + peers_ref[:, :SUB]
    out_ref[...] = pack(mm3(split(total), padded(down_ref, pad_ref, 60.0 / TERMS)))


def operator_kernel(
    flow_ref, off_ref, down_ref, col_ref, row_ref, up_ref, w_hbm, m_hbm, up_hbm, w_ref, m_ref, pad_ref, tab_ref, sems
):
    for (x, y, z), kern in box_kernels(
        (2.0, -2.0), (3.0, 1.0, -1.0, -3.0), (1.0, -1.0), 20.0, 3.0, col_ref, row_ref, tab_ref
    ):
        e = (y & 1) + z * 2 + x * 4 + (y >> 1) * 8
        high, low = split(kern)
        up_ref[e, 0, :, :] = high
        up_ref[e, 1, :, :] = low
    up_move = pltpu.make_async_copy(up_ref, up_hbm, sems.at[2])
    up_move.start()
    kern = split(leaf_kernel(off_ref[RHS : RHS + 3, :], col_ref))
    down = padded(down_ref, pad_ref, 18.0 / TERMS)
    down = (down[0][:, :SUB], down[1][:, :SUB])
    weights = split(mm3(down, kern))
    w_ref[0, :, :] = weights[0]
    w_ref[1, :, :] = weights[1]
    w_move = pltpu.make_async_copy(w_ref, w_hbm, sems.at[0])
    w_move.start()
    block = lax.broadcasted_iota(jnp.int32, (SUB, 256), 1) // SLOTS
    found = [jnp.zeros((SUB, 256), F32)] * 2
    for (x, y, z), kern in box_kernels(
        (-1.5, -0.5, 0.5, 1.5), (-0.5, 0.5), (-0.5, 0.5), 0.9, 6.0, col_ref, row_ref, tab_ref
    ):
        half, g = (x >> 1), (x & 1) + 2 * y + 4 * z
        lanes = slice(half * 256, half * 256 + 256)
        own = (weights[0][:, lanes], weights[1][:, lanes])
        found[half] = jnp.where(block == g, mm3(split(kern[:, :SUB]), own), found[half])
    for half in range(2):
        lanes = slice(half * 256, half * 256 + 256)
        m_high, m_low = split(found[half])
        m_ref[0, :, lanes] = m_high
        m_ref[1, :, lanes] = m_low
    m_move = pltpu.make_async_copy(m_ref, m_hbm, sems.at[1])
    m_move.start()
    up_move.wait()
    w_move.wait()
    m_move.wait()


def near_field(near_ref, left_ref, own_ref, right_ref, out_ref, mask_ref, high_ref, low_ref):
    offs = jnp.concatenate([own_ref[RHS:ROWS, :], jnp.zeros((120, POINTS), F32)], axis=0).T
    inner = lax.axis_index("inner")
    device = lax.axis_index("outer") * INNER + inner
    base = (device - 1) * LEAVES
    total = 3 * POINTS
    lane = lax.broadcasted_iota(jnp.int32, (LEAVES, total), 1) // SLOTS
    found = jnp.zeros((LEAVES, total), F32)
    near = near_ref[...] - base
    for k in range(12):
        found = jnp.where(lane == near[:, k : k + 1], 1.0, found)
    mask_ref[...] = found
    leaf = lax.broadcasted_iota(jnp.int32, (1, POINTS), 1) // SLOTS
    within = local_leaf(leaf)
    own_box = corner(device * LEAVES, 4)
    sources = []
    for c in range(3):
        lanes = []
        for side, ref in ((-1, left_ref), (0, own_ref), (1, right_ref)):
            box = corner((device + side) * LEAVES, 4)[c] - own_box[c]
            lanes.append(ref[RHS + c : RHS + c + 1, :] + (box + within[c]).astype(F32))
        sources.append(jnp.concatenate(lanes, axis=1))
    for g in range(LEAVES):
        rows = slice(g * SLOTS, g * SLOTS + SLOTS)
        place = local_leaf(g)
        dist = SOFTEN
        for c in range(3):
            diff = (offs[rows, c : c + 1] + float(place[c])) - sources[c]
            dist = dist + diff * diff
        k_high, k_low = split(lax.rsqrt(dist) * mask_ref[g : g + 1, :])
        high_ref[rows, :] = k_high
        low_ref[rows, :] = k_low
    charges = jnp.concatenate([r[0:RHS, :] for r in (left_ref, own_ref, right_ref)], axis=1)
    q_high, q_low = split(charges)
    both = jnp.concatenate([q_high, q_low], axis=0)
    res = dot_nt(high_ref[...], both)
    res = res + jnp.concatenate([dot_nt(low_ref[...], q_high), jnp.zeros((POINTS, RHS), F32)], axis=1)
    flipped = res.T
    out_ref[...] = flipped[:RHS] + flipped[RHS:]


def field_kernel(
    far_ref, near_ref, own_ref, swap_ref, cross_ref, up_ref, col_ref, row_ref, w_hbm, m_hbm, e_hbm, out_ref, m_ref,
    pad_ref, e_ref, dl_ref, xtab_ref, tab_ref, w_ref, left_ref, right_ref, mask_ref, high_ref, low_ref, sems,
):
    middle = LEAVES * 2 * RHS
    moves = [
        pltpu.make_async_copy(e_hbm, e_ref.at[middle : 2 * middle], sems.at[0]),
        pltpu.make_async_copy(w_hbm, w_ref, sems.at[1]),
        pltpu.make_async_copy(m_hbm, m_ref, sems.at[2]),
    ]
    for move in moves:
        move.start()
    odd = lax.rem(lax.axis_index("inner"), 2) == 1
    left_ref[...] = jnp.where(odd, swap_ref[...], cross_ref[...])
    right_ref[...] = jnp.where(odd, cross_ref[...], swap_ref[...])
    near_field(near_ref, left_ref, own_ref, right_ref, out_ref, mask_ref, high_ref, low_ref)
    inner = lax.axis_index("inner")
    device = lax.axis_index("outer") * INNER + inner
    up = padded(up_ref, pad_ref, 18.0 / TERMS)
    for side, ref in ((0, left_ref), (2, right_ref)):
        kern = split(leaf_kernel(ref[RHS : RHS + 3, :], col_ref))
        store_equivalents(leaf_equivalents(ref[0:RHS, :], kern, up), e_ref, side * middle)
    for move in moves:
        move.wait()
    first = (device - 1) * LEAVES
    boxes = [corner((device + side) * LEAVES, 4) for side in (-1, 0, 1)]
    boxes = [[(boxes[1][c] - box[c]).astype(F32) for c in range(3)] for box in boxes]
    cols = columns(col_ref)
    for side in range(3):
        for n in range(7):
            xtab_ref[side * 7 + n] = square_of(0, boxes[side][0] + (n - 3.0), 0.9, 1.8, cols, row_ref)
        for c in range(3):
            tab_ref[27 + c] = square_of(2, boxes[side][2] + (c - 1.0), 0.9, 1.8, cols, row_ref) + SOFTEN
        for b in range(3):
            ysq = square_of(1, boxes[side][1] + (b - 1.0), 0.9, 1.8, cols, row_ref)
            for c in range(3):
                tab_ref[side * 9 + b * 3 + c] = ysq + tab_ref[27 + c]

    def one_leaf(g, carry):
        own = local_leaf(g)
        wide = jnp.zeros((2 * RHS, LANE), F32)
        narrow = jnp.zeros((RHS, LANE), F32)
        rest = jnp.zeros((LANE - SUB, LANE), BF)
        for k in range(0, 12, 4):
            tops, lows, equivs = [], [], []
            for n in range(k, k + 4):
                window = far_ref[g, n] - first
                side = window >> 4
                place = local_leaf(window & 15)
                x = side * 7 + 3 + own[0] - place[0]
                yz = side * 9 + 4 + (own[1] - place[1]) * 3 + own[2] - place[2]
                k_high, k_low = split(lax.rsqrt(xtab_ref[x] + tab_ref[yz]))
                tops += [k_high, rest]
                lows += [k_low, rest]
                equivs.append(e_ref[pl.ds(pl.multiple_of(window * (2 * RHS), 2 * RHS), 2 * RHS), :])
            equiv = jnp.concatenate(equivs, axis=1)
            wide = wide + dot(equiv, jnp.concatenate(tops, axis=0))
            narrow = narrow + dot(equiv[:RHS], jnp.concatenate(lows, axis=0))
        acc = wide[:RHS] + wide[RHS:] + narrow
        high, low = split(acc)
        start = pl.multiple_of(g * RHS, RHS)
        dl_ref[0, pl.ds(start, RHS), :] = high
        dl_ref[1, pl.ds(start, RHS), :] = low
        return carry

    lax.fori_loop(0, LEAVES, one_leaf, 0)
    block = lax.broadcasted_iota(jnp.int32, (RHS, 256), 1) // SLOTS
    for half in range(2):
        lanes = slice(half * 256, half * 256 + 256)
        rows = slice(half * 8 * RHS, (half + 1) * 8 * RHS)
        local = (dl_ref[0, rows, :][:, :SUB], dl_ref[1, rows, :][:, :SUB])
        res = mm3(local, (w_ref[0, :, lanes], w_ref[1, :, lanes]))
        acc = out_ref[:, lanes]
        for g in range(8):
            acc = acc + jnp.where(block == g, res[g * RHS : (g + 1) * RHS], 0.0)
        out_ref[:, lanes] = acc


def tail_kernel(x_ref, base_ref, m_ref, out_ref):
    local = split(unpack(x_ref[...])[:, :SUB])
    out_ref[...] = base_ref[...] + mm3(local, (m_ref[0], m_ref[1]))


VM = pl.BlockSpec(memory_space=pltpu.VMEM)
SM = pl.BlockSpec(memory_space=pltpu.SMEM)
HB = pl.BlockSpec(memory_space=pltpu.HBM)


def call(kernel, name, outs, specs, scratch, vmem, *args, out_specs=None):
    return pl.pallas_call(
        kernel,
        name=name,
        out_shape=outs,
        in_specs=specs,
        out_specs=out_specs or jax.tree.map(lambda _: VM, outs),
        scratch_shapes=scratch,
        compiler_params=pltpu.CompilerParams(vmem_limit_bytes=vmem * 1024 * 1024),
        cost_estimate=pl.CostEstimate(flops=1000, bytes_accessed=1000, transcendentals=0),
    )(*args)


def in_hbm(x):
    return pltpu.with_memory_space_constraint(x, pltpu.HBM)


def tie(value, *others):
    return lax.optimization_barrier((value,) + others)[0]


def shards(offsets, charges, counts, near, far, upward, downward):
    col_np, row_np = sphere_tables()
    sds = jax.ShapeDtypeStruct
    pad = pltpu.VMEM((SUB, LANE), F32)
    flow = sds((2 * RHS, 128), F32)
    square = sds((TERMS, TERMS), F32)

    def tables(n):
        return pltpu.VMEM((n, SUB, LANE), F32)

    inputs = (offsets, charges, counts, upward, downward, jnp.asarray(col_np), jnp.asarray(row_np))
    equiv_rows = LEAVES * 2 * RHS
    dev_equiv, own, upward, downward, col, row, equiv = call(
        head_kernel, "leaf_and_device_equiv",
        (flow, sds((ROWS, POINTS), F32), square, square, sds((SUB, 128), F32), sds((8, LANE), F32), pltpu.HBM((equiv_rows, LANE), BF)),
        [HB] * 7,
        [
            pltpu.VMEM((3, POINTS), F32),
            pltpu.VMEM((RHS, POINTS), F32),
            pltpu.SMEM((LEAVES,), jnp.int32),
            pad,
            tables(10),
            pltpu.VMEM((equiv_rows, LANE), BF),
            pltpu.SemaphoreType.DMA((8,)),
        ],
        16, *map(in_hbm, inputs), out_specs=(VM, VM, VM, VM, VM, VM, HB),
    )
    peers_equiv = lax.all_to_all(dev_equiv, "inner", 0, 0, tiled=True)
    leaf_maps = pltpu.HBM((2, SUB, POINTS), BF)
    up_shape = (INNER, 2, SUB, LANE)
    up_maps, weights, evaluate, up_copy = call(
        operator_kernel, "evaluation_and_group_maps", (sds(up_shape, BF), leaf_maps, leaf_maps, pltpu.HBM(up_shape, BF)),
        [VM, VM, VM, VM, VM],
        [pltpu.VMEM((2, SUB, POINTS), BF), pltpu.VMEM((2, SUB, POINTS), BF), pad, tables(14), pltpu.SemaphoreType.DMA((3,))],
        14, dev_equiv, own, downward, col, row, out_specs=(VM, HB, HB, HB),
    )
    swap = lax.ppermute(own, "inner", [(i, i ^ 1) for i in range(INNER)])
    cross = lax.ppermute(own, "inner", [(i, ((i + 1) ^ 1) - 1) for i in range(1, INNER - 1)])
    group_equiv = call(
        group_up_kernel, "group_equiv", pltpu.HBM((8 * OUTER, 128), F32), [VM, VM, VM],
        [pad, pltpu.VMEM((8 * OUTER, 128), F32), pltpu.SemaphoreType.DMA], 6,
        peers_equiv, up_maps, upward, out_specs=HB,
    )
    groups = lax.all_to_all(group_equiv, "outer", 0, 0, tiled=True)
    peers_part = call(
        peers_kernel, "device_to_device", sds((RHS, LANE), F32), [VM, VM, VM],
        [tables(12), pltpu.VMEM((4, 2, 3 * RHS, LANE), BF)], 10, peers_equiv, col, row,
    )
    groups = tie(groups, peers_part)
    local = call(
        local_kernel, "group_and_device_local", flow, [VM, VM, VM, VM, VM, HB],
        [pad, tables(14), pltpu.VMEM(up_shape, BF), pltpu.SemaphoreType.DMA], 12,
        groups, peers_part, downward, col, row, in_hbm(up_copy),
    )
    dev_local = lax.all_to_all(local, "inner", 0, 0, tiled=True)
    base, evaluate = call(
        field_kernel, "near_and_far_field", (sds((RHS, POINTS), F32), sds((2, SUB, POINTS), BF)),
        [SM, VM, VM, VM, VM, VM, VM, VM, HB, HB, HB],
        [
            pad,
            pltpu.VMEM((3 * LEAVES * 2 * RHS, LANE), BF),
            pltpu.VMEM((2, LEAVES * RHS, LANE), BF),
            tables(21),
            tables(30),
            pltpu.VMEM((2, SUB, POINTS), BF),
            pltpu.VMEM((ROWS, POINTS), F32),
            pltpu.VMEM((ROWS, POINTS), F32),
            pltpu.VMEM((LEAVES, 3 * POINTS), F32),
            pltpu.VMEM((POINTS, 3 * POINTS), BF),
            pltpu.VMEM((POINTS, 3 * POINTS), BF),
            pltpu.SemaphoreType.DMA((3,)),
        ],
        32, far, near, own, swap, cross, upward, col, row, in_hbm(weights), in_hbm(evaluate), in_hbm(equiv),
    )
    return call(tail_kernel, "potential", sds((RHS, POINTS), F32), [VM, VM, VM], [], 4, dev_local, base, evaluate)


def solution(mesh):
    both = ("outer", "inner")
    in_specs = (P(None, both), P(None, both), P(both), P(both, None), P(both, None), P(), P())
    return jax.shard_map(shards, mesh=mesh, in_specs=in_specs, out_specs=P(None, both), check_vma=False)
```

```python
import functools

import jax
import jax.numpy as jnp
import numpy as np
from jax import lax
from jax.experimental import pallas as pl
from jax.experimental.pallas import tpu as pltpu
from jax.sharding import PartitionSpec as P

SOFTEN = 0.25
GOLDEN = 2.399963229728653
RHS = 64
TERMS = 165
SUB = 176
LANE = 256
LEAVES = 16
SLOTS = 32
POINTS = LEAVES * SLOTS
ROWS = 72
INNER = 16
EQUIV = LEAVES * RHS
HALO = EQUIV + 2 * ROWS
OUTER = 32
PART = RHS // INNER
BF = jnp.bfloat16
F32 = jnp.float32


def sphere_tables():
    steps = np.arange(TERMS, dtype=np.float32)
    height = (np.float32(1.0) - (np.float32(2.0) * steps + np.float32(1.0)) / np.float32(TERMS)).astype(np.float32)
    radial = np.sqrt(np.maximum(np.float32(1.0) - height * height, np.float32(0.0))).astype(np.float32)
    angle = (steps * np.float32(GOLDEN)).astype(np.float32)
    dirs = np.stack([radial * np.cos(angle), radial * np.sin(angle), height]).astype(np.float32)
    col = np.zeros((SUB, 128), np.float32)
    col[:TERMS, :3] = dirs.T
    row = np.zeros((8, LANE), np.float32)
    row[:3, :TERMS] = dirs
    return col, row


def split(x):
    high = x.astype(BF)
    return high, (x - high.astype(F32)).astype(BF)


def dot(a, b):
    return jnp.dot(a, b, preferred_element_type=F32)


def dot_nt(a, b):
    return lax.dot_general(a, b, (((1,), (1,)), ((), ())), preferred_element_type=F32)


def mm3(a, b, f=dot):
    return f(a[0], b[0]) + f(a[1], b[0]) + f(a[0], b[1])


def columns(col_ref):
    return [jnp.broadcast_to(col_ref[:, c : c + 1], (SUB, 128)) for c in range(3)]


def two(x):
    return jnp.concatenate([x, x], axis=1)


def square_of(axis, shift, radius_t, radius_i, cols, row_ref):
    diff = (radius_t * row_ref[axis : axis + 1, :] + shift) - two(radius_i * cols[axis])
    return diff * diff


def box_kernels(xs, ys, zs, radius_t, radius_i, col_ref, row_ref, tab_ref):
    cols = columns(col_ref)
    for n, shift in enumerate(xs):
        tab_ref[n] = square_of(0, shift, radius_t, radius_i, cols, row_ref)
    zsq = len(xs)
    for n, shift in enumerate(zs):
        tab_ref[zsq + n] = square_of(2, shift, radius_t, radius_i, cols, row_ref) + SOFTEN
    start = zsq + len(zs)
    for b, shift in enumerate(ys):
        ysq = square_of(1, shift, radius_t, radius_i, cols, row_ref)
        for c in range(len(zs)):
            tab_ref[start + b * len(zs) + c] = ysq + tab_ref[zsq + c]
    for b in range(len(ys)):
        for c in range(len(zs)):
            for a in range(len(xs)):
                yield (a, b, c), lax.rsqrt(tab_ref[a] + tab_ref[start + b * len(zs) + c])


def bits(ids, low, axis, top=14):
    total = 0
    for level in range(5):
        place = 3 * level + axis
        if low <= place < top:
            total = total + (((ids >> place) & 1) << level)
    return total


def corner(leaf_id, low):
    return [bits(leaf_id, low, axis) for axis in range(3)]


def local_leaf(index):
    return ((index & 1) + ((index >> 3) & 1) * 2, (index >> 1) & 1, (index >> 2) & 1)


def peer_box(inner):
    return (((inner >> 2) & 1) * 4, (inner & 1) * 2 + ((inner >> 3) & 1) * 4, ((inner >> 1) & 1) * 2)


def leaf_kernel(offs, col_ref):
    total = SOFTEN
    for c in range(3):
        col = jnp.broadcast_to(col_ref[:, c : c + 1], (SUB, 128)) * 1.8
        diff = jnp.concatenate([col] * (POINTS // 128), axis=1) - offs[c : c + 1, :]
        total = total + diff * diff
    return lax.rsqrt(total)


def padded(map_ref, pad_ref, scale):
    pad_ref[...] = jnp.zeros_like(pad_ref)
    pad_ref[0:TERMS, 0:TERMS] = map_ref[...] * scale
    return split(pad_ref[...])


def leaf_equivalents(charges, kern, up):
    block = lax.broadcasted_iota(jnp.int32, (RHS, 256), 1) // SLOTS
    keep = [(block == g).astype(F32).astype(BF) for g in range(8)]
    pieces = split(charges)
    out = []
    for half in range(2):
        lanes = slice(half * 256, half * 256 + 256)
        spread = [jnp.concatenate([piece[:, lanes] * keep[g] for g in range(8)], axis=0) for piece in pieces]
        high, low = kern[0][:, lanes], kern[1][:, lanes]
        spread = jnp.concatenate([spread[0], spread[1], spread[0]], axis=1)
        check = dot_nt(spread, jnp.concatenate([high, high, low], axis=1))
        out.append(mm3(split(check), up))
    return out


def store_equivalents(rows, e_ref, first):
    high, low = split(rows)
    e_ref[pl.ds(first, RHS), :] = high
    e_ref[pl.ds(first + RHS, RHS), :] = low


def pack(rows):
    low, high = rows[:, :128], rows[:, 128:]
    n = rows.shape[0]
    top = lax.broadcasted_iota(jnp.int32, (n, 128), 0) % 8 < 4
    first = jnp.where(top, low, pltpu.roll(high, 4, 0))
    second = jnp.where(top, pltpu.roll(low, n - 4, 0), high)
    tiles = []
    for m in range(n // 8):
        tiles += [first[8 * m : 8 * m + 8], second[8 * m : 8 * m + 8]]
    return jnp.concatenate(tiles, axis=0)


def unpack(tiles):
    n = tiles.shape[0] // 2
    first = jnp.concatenate([tiles[16 * m : 16 * m + 8] for m in range(n // 8)], axis=0)
    second = jnp.concatenate([tiles[16 * m + 8 : 16 * m + 16] for m in range(n // 8)], axis=0)
    top = lax.broadcasted_iota(jnp.int32, (n, 128), 0) % 8 < 4
    low = jnp.where(top, first, pltpu.roll(second, 4, 0))
    high = jnp.where(top, pltpu.roll(first, n - 4, 0), second)
    return jnp.concatenate([low, high], axis=1)


def tile_dot(tile, high, low, acc):
    a_high, a_low = split(tile)
    both = jnp.concatenate([a_high, a_low], axis=0)
    rest = SUB - 128
    front = dot(both, high[:128]) + dot(both, low[:128])
    back = dot(both[:, :rest], high[128:]) + dot(both[:, :rest], low[128:])
    return acc[0] + front, acc[1] + back


def tile_sum(acc):
    front = acc[0][:8] + acc[0][8:]
    back = acc[1][:8] + acc[1][8:]
    return front + pltpu.roll(back, 4, 0)


def head_kernel(
    off_hbm, q_hbm, counts_hbm, up_hbm, down_hbm, col_hbm, row_hbm,
    out_ref, halo_ref, up_ref, down_ref, col_ref, row_ref, beside_hbm,
    off_ref, q_ref, counts_ref, pad_ref, tab_ref, e_ref, beside_ref, sems,
):
    moves = [
        pltpu.make_async_copy(src, dst, sems.at[n])
        for n, (src, dst) in enumerate(
            (
                (q_hbm, q_ref),
                (off_hbm, off_ref),
                (counts_hbm, counts_ref),
                (up_hbm, up_ref),
                (col_hbm, col_ref),
                (row_hbm, row_ref),
                (down_hbm, down_ref),
            )
        )
    ]
    for move in moves:
        move.start()
    for move in moves[:-1]:
        move.wait()
    lane = lax.broadcasted_iota(jnp.int32, (8, POINTS), 1)
    limit = jnp.zeros((8, POINTS), jnp.int32)
    for g in range(LEAVES):
        limit = jnp.where(lane // SLOTS == g, counts_ref[g], limit)
    filled = (lane % SLOTS < limit)[0:1]
    charges = jnp.where(filled, q_ref[...], 0.0)
    halo_ref[0:RHS, :] = charges
    halo_ref[RHS:ROWS, :] = jnp.zeros((ROWS - RHS, POINTS), F32)
    halo_ref[RHS : RHS + 3, :] = off_ref[...]
    beside_ref[EQUIV : EQUIV + ROWS, :] = halo_ref[:, :256]
    beside_ref[EQUIV + ROWS : HALO, :] = halo_ref[:, 256:]
    kern = split(leaf_kernel(off_ref[...], col_ref))
    up = padded(up_ref, pad_ref, 18.0 / TERMS)
    up = (up[0][:, :], up[1][:, :])
    halves = leaf_equivalents(charges, kern, up)
    for half in range(2):
        beside_ref[half * 8 * RHS : (half + 1) * 8 * RHS, :] = halves[half]
        for g in range(8):
            store_equivalents(halves[half][g * RHS : (g + 1) * RHS], e_ref, (half * 8 + g) * 2 * RHS)
    e_move = pltpu.make_async_copy(beside_ref, beside_hbm, sems.at[7])
    e_move.start()
    acc = jnp.zeros((RHS, LANE), F32)
    for (x, y, z), kern in box_kernels(
        (1.5, 0.5, -0.5, -1.5), (0.5, -0.5), (0.5, -0.5), 6.0, 0.9, col_ref, row_ref, tab_ref
    ):
        start = ((x >> 1) * 8 + (x & 1) + 2 * y + 4 * z) * 2 * RHS
        high, low = split(kern)
        wide = dot(e_ref[start : start + 2 * RHS, :][:, :SUB], high)
        acc = acc + wide[:RHS] + wide[RHS:] + dot(e_ref[start : start + RHS, :][:, :SUB], low)
    up60 = padded(up_ref, pad_ref, 60.0 / TERMS)
    out_ref[...] = pack(mm3(split(acc[:, :SUB]), up60))
    moves[-1].wait()
    e_move.wait()


def group_up_kernel(x_ref, maps_ref, up_ref, out_hbm, pad_ref, out_ref, sem):
    acc = (jnp.zeros((16, LANE), F32), jnp.zeros((16, LANE), F32))
    for e in range(INNER):
        acc = tile_dot(x_ref[8 * e : 8 * e + 8, :], maps_ref[e, 0], maps_ref[e, 1], acc)
    check = tile_sum(acc)
    both = jnp.concatenate([check, check], axis=0)
    equiv = mm3(split(both[:, :SUB]), padded(up_ref, pad_ref, 200.0 / TERMS))[:8]
    top = lax.broadcasted_iota(jnp.int32, (8, 128), 0) < 4
    tile = jnp.where(top, equiv[:, :128], pltpu.roll(equiv[:, 128:], 4, 0))
    for p in range(OUTER):
        out_ref[8 * p : 8 * p + 8, :] = tile
    move = pltpu.make_async_copy(out_ref, out_hbm, sem)
    move.start()
    move.wait()


def box_order(rows):
    return jnp.concatenate(
        [rows[8 * k : 8 * k + 8] for k in (y * 4 + x * 2 + z for x in (0, 1) for z in (0, 1) for y in (0, 1))], axis=0
    )


def index_order(rows):
    return jnp.concatenate(
        [rows[8 * k : 8 * k + 8] for k in (x * 4 + z * 2 + y for y in (0, 1) for x in (0, 1) for z in (0, 1))], axis=0
    )


def peers_kernel(x_ref, col_ref, row_ref, out_ref, tab_ref, shifted_ref):
    equiv = jnp.concatenate([box_order(unpack(x_ref[...])), jnp.zeros((16, LANE), F32)], axis=0)
    shifted_ref[...] = jnp.zeros_like(shifted_ref)
    for q in range(4):
        high, low = split(pltpu.roll(equiv, 4 * q, 0) if q else equiv)
        shifted_ref[q, 0, RHS : RHS + 80, :] = high
        shifted_ref[q, 1, RHS : RHS + 80, :] = low
    cols = columns(col_ref)
    for dy in range(-3, 4):
        tab_ref[dy + 3] = square_of(1, 2.0 * dy, 3.0, 3.0, cols, row_ref) + SOFTEN
    row = lax.broadcasted_iota(jnp.int32, (RHS, 128), 0)
    lane = lax.broadcasted_iota(jnp.int32, (RHS, 128), 1)
    px, pz, py = row >> 5, (row >> 4) & 1, (row >> 2) & 3
    dest = (py & 1) + pz * 2 + px * 4 + (py >> 1) * 8

    def valid(dx, dz):
        sx, sy, sz = px - dx, py - (lane - 3), pz - dz
        inside = (sx >= 0) & (sx < 2) & (sy >= 0) & (sy < 4) & (sz >= 0) & (sz < 2)
        source = (sy & 1) + sz * 2 + sx * 4 + (sy >> 1) * 8
        return (inside & (jnp.abs(source - dest) >= 2)).astype(F32)

    def moved(dx, dy, dz, mask):
        q = dy % 4
        start = RHS - (dx * 2 + dz) * 16 - 4 * (dy - q)
        keep = two(jnp.broadcast_to(mask[:, dy + 3 : dy + 4], (RHS, 128))).astype(BF)
        rows = [(shifted_ref[q, n, start : start + RHS, :] * keep)[:, :SUB] for n in range(2)]
        return rows

    acc = (jnp.zeros((RHS, LANE), F32), jnp.zeros((RHS, SUB), F32))
    planes = [(0, 0, (1, 2, 3))] + [(dx, dz, range(-3, 4)) for dx, dz in ((0, 1), (1, -1), (1, 0), (1, 1))]
    for n, (dx, dz, steps) in enumerate(planes):
        plane = square_of(0, dx * 4.0, 3.0, 3.0, cols, row_ref)
        tab_ref[7 + n] = plane + square_of(2, dz * 2.0, 3.0, 3.0, cols, row_ref)
        ahead, behind = valid(dx, dz), valid(-dx, -dz)
        for dy in steps:
            kern = split(lax.rsqrt(tab_ref[7 + n] + tab_ref[dy + 3]))
            forward = acc[0] + mm3(moved(dx, dy, dz, ahead), kern)
            kern = (kern[0][:, :SUB], kern[1][:, :SUB])
            acc = (forward, acc[1] + mm3(moved(-dx, -dy, -dz, behind), kern, dot_nt))
    back = jnp.concatenate([acc[1], jnp.zeros((RHS, LANE - SUB), F32)], axis=1)
    out_ref[...] = index_order(acc[0] + back)


def local_kernel(x_ref, peers_ref, down_ref, col_ref, row_ref, out_ref, pad_ref, tab_ref):
    outer = lax.axis_index("outer")
    own = [p.astype(F32) for p in corner(outer * 256, 8)]
    cols = columns(col_ref)
    for n in range(4):
        tab_ref[n] = square_of(2, own[2] - 4.0 * n, 10.0, 20.0, cols, row_ref) + SOFTEN
    for x in range(4):
        xsq = square_of(0, own[0] - 8.0 * x, 10.0, 20.0, cols, row_ref)
        for y in range(2):
            tab_ref[4 + x * 2 + y] = xsq + square_of(1, own[1] - 8.0 * y, 10.0, 20.0, cols, row_ref)
    acc = (jnp.zeros((16, LANE), F32), jnp.zeros((16, LANE), F32))
    for p in range(OUTER):
        z, x, y = (p & 1) + ((p >> 3) & 1) * 2, ((p >> 1) & 1) + ((p >> 4) & 1) * 2, (p >> 2) & 1
        weight = (jnp.abs(p - outer) >= 2).astype(F32)
        kern = split(lax.rsqrt(tab_ref[4 + x * 2 + y] + tab_ref[z]))
        acc = tile_dot(x_ref[8 * p : 8 * p + 8, :] * weight, kern[0], kern[1], acc)
    check = tile_sum(acc)
    both = jnp.concatenate([check, check], axis=0)
    group = mm3(split(both[:, :SUB]), padded(down_ref, pad_ref, 200.0 / TERMS))[:8]
    pieces = jnp.concatenate(split(group[:, :SUB]), axis=0)
    top = lax.broadcasted_iota(jnp.int32, (8, LANE), 0) < 4
    found = [None] * INNER
    for (x, y, z), kern in box_kernels(
        (-2.0, 2.0), (-3.0, -1.0, 1.0, 3.0), (-1.0, 1.0), 3.0, 20.0, col_ref, row_ref, tab_ref
    ):
        high, low = split(kern)
        part = dot(pieces, high) + dot(pieces, low)
        found[(y & 1) + z * 2 + x * 4 + (y >> 1) * 8] = part[:8] + part[8:]
    merged = [jnp.where(top, found[2 * m], pltpu.roll(found[2 * m + 1], 4, 0)) for m in range(INNER // 2)]
    total = jnp.concatenate(merged, axis=0) + peers_ref[...]
    out_ref[...] = pack(mm3(split(total[:, :SUB]), padded(down_ref, pad_ref, 60.0 / TERMS)))


def operator_kernel(
    flow_ref, off_ref, down_ref, col_ref, row_ref, up_ref, w_hbm, m_hbm, w_ref, m_ref, pad_ref, tab_ref, sems
):
    for (x, y, z), kern in box_kernels(
        (2.0, -2.0), (3.0, 1.0, -1.0, -3.0), (1.0, -1.0), 20.0, 3.0, col_ref, row_ref, tab_ref
    ):
        e = (y & 1) + z * 2 + x * 4 + (y >> 1) * 8
        high, low = split(kern)
        up_ref[e, 0, :, :] = high
        up_ref[e, 1, :, :] = low
    kern = split(leaf_kernel(off_ref[RHS : RHS + 3, :], col_ref))
    down = padded(down_ref, pad_ref, 18.0 / TERMS)
    down = (down[0][:, :SUB], down[1][:, :SUB])
    weights = split(mm3(down, kern))
    w_ref[0, :, :] = weights[0]
    w_ref[1, :, :] = weights[1]
    w_move = pltpu.make_async_copy(w_ref, w_hbm, sems.at[0])
    w_move.start()
    block = lax.broadcasted_iota(jnp.int32, (SUB, 256), 1) // SLOTS
    found = [jnp.zeros((SUB, 256), F32)] * 2
    for (x, y, z), kern in box_kernels(
        (-1.5, -0.5, 0.5, 1.5), (-0.5, 0.5), (-0.5, 0.5), 0.9, 6.0, col_ref, row_ref, tab_ref
    ):
        half, g = (x >> 1), (x & 1) + 2 * y + 4 * z
        lanes = slice(half * 256, half * 256 + 256)
        own = (weights[0][:, lanes], weights[1][:, lanes])
        found[half] = jnp.where(block == g, mm3(split(kern[:, :SUB]), own), found[half])
    for half in range(2):
        lanes = slice(half * 256, half * 256 + 256)
        m_high, m_low = split(found[half])
        m_ref[0, :, lanes] = m_high
        m_ref[1, :, lanes] = m_low
    m_move = pltpu.make_async_copy(m_ref, m_hbm, sems.at[1])
    m_move.start()
    w_move.wait()
    m_move.wait()


def near_field(near_ref, left_ref, own_ref, right_ref, out_ref, mask_ref, high_ref, low_ref):
    offs = jnp.concatenate([own_ref[RHS:ROWS, :], jnp.zeros((120, POINTS), F32)], axis=0).T
    inner = lax.axis_index("inner")
    device = lax.axis_index("outer") * INNER + inner
    base = (device - 1) * LEAVES
    total = 3 * POINTS
    lane = lax.broadcasted_iota(jnp.int32, (LEAVES, total), 1) // SLOTS
    found = jnp.zeros((LEAVES, total), F32)
    near = near_ref[...] - base
    for k in range(12):
        found = jnp.where(lane == near[:, k : k + 1], 1.0, found)
    mask_ref[...] = found
    leaf = lax.broadcasted_iota(jnp.int32, (1, POINTS), 1) // SLOTS
    within = local_leaf(leaf)
    own_box = corner(device * LEAVES, 4)
    sources = []
    for c in range(3):
        lanes = []
        for side, ref in ((-1, left_ref), (0, own_ref), (1, right_ref)):
            box = corner((device + side) * LEAVES, 4)[c] - own_box[c]
            lanes.append(ref[RHS + c : RHS + c + 1, :] + (box + within[c]).astype(F32))
        sources.append(jnp.concatenate(lanes, axis=1))
    for g in range(LEAVES):
        rows = slice(g * SLOTS, g * SLOTS + SLOTS)
        place = local_leaf(g)
        dist = SOFTEN
        for c in range(3):
            diff = (offs[rows, c : c + 1] + float(place[c])) - sources[c]
            dist = dist + diff * diff
        k_high, k_low = split(lax.rsqrt(dist) * mask_ref[g : g + 1, :])
        high_ref[rows, :] = k_high
        low_ref[rows, :] = k_low
    charges = jnp.concatenate([r[0:RHS, :] for r in (left_ref, own_ref, right_ref)], axis=1)
    q_high, q_low = split(charges)
    both = jnp.concatenate([q_high, q_low], axis=0)
    res = dot_nt(high_ref[...], both)
    res = res + jnp.concatenate([dot_nt(low_ref[...], q_high), jnp.zeros((POINTS, RHS), F32)], axis=1)
    flipped = res.T
    out_ref[...] = flipped[:RHS] + flipped[RHS:]


def field_kernel(
    far_ref, near_ref, own_ref, col_ref, row_ref, own_hbm, swap_hbm, cross_hbm, w_hbm, m_hbm, out_ref, m_ref,
    e_ref, dl_ref, xtab_ref, tab_ref, w_ref, left_ref, right_ref, mask_ref, high_ref, low_ref,
    self_ref, swap_ref, cross_ref, sems,
):
    points, equivs = pl.ds(EQUIV, 2 * ROWS), pl.ds(0, EQUIV)
    moves = [
        pltpu.make_async_copy(src, dst, sems.at[n])
        for n, (src, dst) in enumerate(
            (
                (swap_hbm.at[points], swap_ref.at[points]),
                (cross_hbm.at[points], cross_ref.at[points]),
                (own_hbm.at[equivs], self_ref),
                (swap_hbm.at[equivs], swap_ref.at[equivs]),
                (cross_hbm.at[equivs], cross_ref.at[equivs]),
                (w_hbm, w_ref),
                (m_hbm, m_ref),
            )
        )
    ]
    for move in moves:
        move.start()
    inner = lax.axis_index("inner")
    device = lax.axis_index("outer") * INNER + inner
    odd = lax.rem(inner, 2) == 1
    first = (device - 1) * LEAVES
    boxes = [corner((device + side) * LEAVES, 4) for side in (-1, 0, 1)]
    boxes = [[(boxes[1][c] - box[c]).astype(F32) for c in range(3)] for box in boxes]
    cols = columns(col_ref)
    for side in range(3):
        for n in range(7):
            xtab_ref[side * 7 + n] = square_of(0, boxes[side][0] + (n - 3.0), 0.9, 1.8, cols, row_ref)
        for c in range(3):
            tab_ref[27 + c] = square_of(2, boxes[side][2] + (c - 1.0), 0.9, 1.8, cols, row_ref) + SOFTEN
        for b in range(3):
            ysq = square_of(1, boxes[side][1] + (b - 1.0), 0.9, 1.8, cols, row_ref)
            for c in range(3):
                tab_ref[side * 9 + b * 3 + c] = ysq + tab_ref[27 + c]
    moves[0].wait()
    moves[1].wait()
    for half in range(2):
        lanes = slice(half * 256, half * 256 + 256)
        rows = slice(EQUIV + half * ROWS, EQUIV + (half + 1) * ROWS)
        swap, cross = swap_ref[rows, :], cross_ref[rows, :]
        left_ref[:, lanes] = jnp.where(odd, swap, cross)
        right_ref[:, lanes] = jnp.where(odd, cross, swap)
    near_field(near_ref, left_ref, own_ref, right_ref, out_ref, mask_ref, high_ref, low_ref)
    for move in moves[2:]:
        move.wait()
    middle = 2 * EQUIV
    swap_at = pl.multiple_of(jnp.where(odd, 0, 2 * middle), 2 * RHS)
    cross_at = pl.multiple_of(jnp.where(odd, 2 * middle, 0), 2 * RHS)
    for ref, place in ((self_ref, middle), (swap_ref, swap_at), (cross_ref, cross_at)):
        for g in range(LEAVES):
            start = place + g * 2 * RHS
            if ref is not self_ref:
                start = pl.multiple_of(start, 2 * RHS)
            store_equivalents(ref[g * RHS : (g + 1) * RHS, :], e_ref, start)

    def one_leaf(g, carry):
        own = local_leaf(g)
        wide = jnp.zeros((2 * RHS, LANE), F32)
        narrow = jnp.zeros((RHS, LANE), F32)
        rest = jnp.zeros((LANE - SUB, LANE), BF)
        for k in range(0, 12, 4):
            tops, lows, equivs = [], [], []
            for n in range(k, k + 4):
                window = far_ref[g, n] - first
                side = window >> 4
                place = local_leaf(window & 15)
                x = side * 7 + 3 + own[0] - place[0]
                yz = side * 9 + 4 + (own[1] - place[1]) * 3 + own[2] - place[2]
                k_high, k_low = split(lax.rsqrt(xtab_ref[x] + tab_ref[yz]))
                tops += [k_high, rest]
                lows += [k_low, rest]
                equivs.append(e_ref[pl.ds(pl.multiple_of(window * (2 * RHS), 2 * RHS), 2 * RHS), :])
            equiv = jnp.concatenate(equivs, axis=1)
            wide = wide + dot(equiv, jnp.concatenate(tops, axis=0))
            narrow = narrow + dot(equiv[:RHS], jnp.concatenate(lows, axis=0))
        acc = wide[:RHS] + wide[RHS:] + narrow
        high, low = split(acc)
        start = pl.multiple_of(g * RHS, RHS)
        dl_ref[0, pl.ds(start, RHS), :] = high
        dl_ref[1, pl.ds(start, RHS), :] = low
        return carry

    lax.fori_loop(0, LEAVES, one_leaf, 0)
    block = lax.broadcasted_iota(jnp.int32, (RHS, 256), 1) // SLOTS
    for half in range(2):
        lanes = slice(half * 256, half * 256 + 256)
        rows = slice(half * 8 * RHS, (half + 1) * 8 * RHS)
        local = (dl_ref[0, rows, :][:, :SUB], dl_ref[1, rows, :][:, :SUB])
        res = mm3(local, (w_ref[0, :, lanes], w_ref[1, :, lanes]))
        acc = out_ref[:, lanes]
        for g in range(8):
            acc = acc + jnp.where(block == g, res[g * RHS : (g + 1) * RHS], 0.0)
        out_ref[:, lanes] = acc


def tail_kernel(x_ref, base_ref, m_ref, out_ref):
    local = split(unpack(x_ref[...])[:, :SUB])
    out_ref[...] = base_ref[...] + mm3(local, (m_ref[0], m_ref[1]))


VM = pl.BlockSpec(memory_space=pltpu.VMEM)
SM = pl.BlockSpec(memory_space=pltpu.SMEM)
HB = pl.BlockSpec(memory_space=pltpu.HBM)


def call(kernel, name, outs, specs, scratch, vmem, *args, out_specs=None):
    return pl.pallas_call(
        kernel,
        name=name,
        out_shape=outs,
        in_specs=specs,
        out_specs=out_specs or jax.tree.map(lambda _: VM, outs),
        scratch_shapes=scratch,
        compiler_params=pltpu.CompilerParams(vmem_limit_bytes=vmem * 1024 * 1024),
        cost_estimate=pl.CostEstimate(flops=1000, bytes_accessed=1000, transcendentals=0),
    )(*args)


def in_hbm(x):
    return pltpu.with_memory_space_constraint(x, pltpu.HBM)


def tie(value, *others):
    return lax.optimization_barrier((value,) + others)[0]


def shards(offsets, charges, counts, near, far, upward, downward):
    col_np, row_np = sphere_tables()
    sds = jax.ShapeDtypeStruct
    pad = pltpu.VMEM((SUB, LANE), F32)
    flow = sds((2 * RHS, 128), F32)
    square = sds((TERMS, TERMS), F32)

    def tables(n):
        return pltpu.VMEM((n, SUB, LANE), F32)

    inputs = (offsets, charges, counts, upward, downward, jnp.asarray(col_np), jnp.asarray(row_np))
    dev_equiv, own, upward, downward, col, row, beside = call(
        head_kernel, "leaf_and_device_equiv",
        (flow, sds((ROWS, POINTS), F32), square, square, sds((SUB, 128), F32), sds((8, LANE), F32), pltpu.HBM((HALO, LANE), F32)),
        [HB] * 7,
        [
            pltpu.VMEM((3, POINTS), F32),
            pltpu.VMEM((RHS, POINTS), F32),
            pltpu.SMEM((LEAVES,), jnp.int32),
            pad,
            tables(10),
            pltpu.VMEM((2 * EQUIV, LANE), BF),
            pltpu.VMEM((HALO, LANE), F32),
            pltpu.SemaphoreType.DMA((8,)),
        ],
        16, *map(in_hbm, inputs), out_specs=(VM, VM, VM, VM, VM, VM, HB),
    )
    peers_equiv = lax.all_to_all(dev_equiv, "inner", 0, 0, tiled=True)
    leaf_maps = pltpu.HBM((2, SUB, POINTS), BF)
    up_maps, weights, evaluate = call(
        operator_kernel, "evaluation_and_group_maps", (sds((INNER, 2, SUB, LANE), BF), leaf_maps, leaf_maps),
        [VM, VM, VM, VM, VM],
        [pltpu.VMEM((2, SUB, POINTS), BF), pltpu.VMEM((2, SUB, POINTS), BF), pad, tables(14), pltpu.SemaphoreType.DMA((2,))],
        14, dev_equiv, own, downward, col, row, out_specs=(VM, HB, HB),
    )
    swap = lax.ppermute(beside, "inner", [(i, i ^ 1) for i in range(INNER)])
    cross = lax.ppermute(beside, "inner", [(i, ((i + 1) ^ 1) - 1) for i in range(1, INNER - 1)])
    group_equiv = call(
        group_up_kernel, "group_equiv", pltpu.HBM((8 * OUTER, 128), F32), [VM, VM, VM],
        [pad, pltpu.VMEM((8 * OUTER, 128), F32), pltpu.SemaphoreType.DMA], 6,
        peers_equiv, up_maps, upward, out_specs=HB,
    )
    groups = lax.all_to_all(group_equiv, "outer", 0, 0, tiled=True)
    peers_part = call(
        peers_kernel, "device_to_device", sds((RHS, LANE), F32), [VM, VM, VM],
        [tables(12), pltpu.VMEM((4, 2, 3 * RHS, LANE), BF)], 10, peers_equiv, col, row,
    )
    groups = tie(groups, peers_part)
    local = call(
        local_kernel, "group_and_device_local", flow, [VM, VM, VM, VM, VM], [pad, tables(14)], 8,
        groups, peers_part, downward, col, row,
    )
    dev_local = lax.all_to_all(local, "inner", 0, 0, tiled=True)
    base, evaluate = call(
        field_kernel, "near_and_far_field", (sds((RHS, POINTS), F32), sds((2, SUB, POINTS), BF)),
        [SM, VM, VM, VM, VM, HB, HB, HB, HB, HB],
        [
            pltpu.VMEM((6 * EQUIV, LANE), BF),
            pltpu.VMEM((2, EQUIV, LANE), BF),
            tables(21),
            tables(30),
            pltpu.VMEM((2, SUB, POINTS), BF),
            pltpu.VMEM((ROWS, POINTS), F32),
            pltpu.VMEM((ROWS, POINTS), F32),
            pltpu.VMEM((LEAVES, 3 * POINTS), F32),
            pltpu.VMEM((POINTS, 3 * POINTS), BF),
            pltpu.VMEM((POINTS, 3 * POINTS), BF),
            pltpu.VMEM((EQUIV, LANE), F32),
            pltpu.VMEM((HALO, LANE), F32),
            pltpu.VMEM((HALO, LANE), F32),
            pltpu.SemaphoreType.DMA((7,)),
        ],
        36, far, near, own, col, row, *map(in_hbm, (beside, swap, cross, weights, evaluate)),
    )
    return call(tail_kernel, "potential", sds((RHS, POINTS), F32), [VM, VM, VM], [], 4, dev_local, base, evaluate)


def solution(mesh):
    both = ("outer", "inner")
    in_specs = (P(None, both), P(None, both), P(both), P(both, None), P(both, None), P(), P())
    return jax.shard_map(shards, mesh=mesh, in_specs=in_specs, out_specs=P(None, both), check_vma=False)
```

```python
import functools

import jax
import jax.numpy as jnp
import numpy as np
from jax import lax
from jax.experimental import pallas as pl
from jax.experimental.pallas import tpu as pltpu
from jax.sharding import PartitionSpec as P

SOFTEN = 0.25
GOLDEN = 2.399963229728653
RHS = 64
TERMS = 165
SUB = 176
LANE = 256
LEAVES = 16
SLOTS = 32
POINTS = LEAVES * SLOTS
ROWS = 72
INNER = 16
OUTER = 32
PART = RHS // INNER
BF = jnp.bfloat16
F32 = jnp.float32


def sphere_tables():
    steps = np.arange(TERMS, dtype=np.float32)
    height = (np.float32(1.0) - (np.float32(2.0) * steps + np.float32(1.0)) / np.float32(TERMS)).astype(np.float32)
    radial = np.sqrt(np.maximum(np.float32(1.0) - height * height, np.float32(0.0))).astype(np.float32)
    angle = (steps * np.float32(GOLDEN)).astype(np.float32)
    dirs = np.stack([radial * np.cos(angle), radial * np.sin(angle), height]).astype(np.float32)
    col = np.zeros((SUB, 128), np.float32)
    col[:TERMS, :3] = dirs.T
    row = np.zeros((8, LANE), np.float32)
    row[:3, :TERMS] = dirs
    return col, row


def split(x):
    high = x.astype(BF)
    return high, (x - high.astype(F32)).astype(BF)


def dot(a, b):
    return jnp.dot(a, b, preferred_element_type=F32)


def dot_nt(a, b):
    return lax.dot_general(a, b, (((1,), (1,)), ((), ())), preferred_element_type=F32)


def mm3(a, b, f=dot):
    return f(a[0], b[0]) + f(a[1], b[0]) + f(a[0], b[1])


def columns(col_ref):
    return [jnp.broadcast_to(col_ref[:, c : c + 1], (SUB, 128)) for c in range(3)]


def two(x):
    return jnp.concatenate([x, x], axis=1)


def square_of(axis, shift, radius_t, radius_i, cols, row_ref):
    diff = (radius_t * row_ref[axis : axis + 1, :] + shift) - two(radius_i * cols[axis])
    return diff * diff


def box_kernels(xs, ys, zs, radius_t, radius_i, col_ref, row_ref, tab_ref):
    cols = columns(col_ref)
    for n, shift in enumerate(xs):
        tab_ref[n] = square_of(0, shift, radius_t, radius_i, cols, row_ref)
    zsq = len(xs)
    for n, shift in enumerate(zs):
        tab_ref[zsq + n] = square_of(2, shift, radius_t, radius_i, cols, row_ref) + SOFTEN
    start = zsq + len(zs)
    for b, shift in enumerate(ys):
        ysq = square_of(1, shift, radius_t, radius_i, cols, row_ref)
        for c in range(len(zs)):
            tab_ref[start + b * len(zs) + c] = ysq + tab_ref[zsq + c]
    for b in range(len(ys)):
        for c in range(len(zs)):
            for a in range(len(xs)):
                yield (a, b, c), lax.rsqrt(tab_ref[a] + tab_ref[start + b * len(zs) + c])


def bits(ids, low, axis, top=14):
    total = 0
    for level in range(5):
        place = 3 * level + axis
        if low <= place < top:
            total = total + (((ids >> place) & 1) << level)
    return total


def corner(leaf_id, low):
    return [bits(leaf_id, low, axis) for axis in range(3)]


def local_leaf(index):
    return ((index & 1) + ((index >> 3) & 1) * 2, (index >> 1) & 1, (index >> 2) & 1)


def peer_box(inner):
    return (((inner >> 2) & 1) * 4, (inner & 1) * 2 + ((inner >> 3) & 1) * 4, ((inner >> 1) & 1) * 2)


def leaf_kernel(offs, col_ref):
    total = SOFTEN
    for c in range(3):
        col = jnp.broadcast_to(col_ref[:, c : c + 1], (SUB, 128)) * 1.8
        diff = jnp.concatenate([col] * (POINTS // 128), axis=1) - offs[c : c + 1, :]
        total = total + diff * diff
    return lax.rsqrt(total)


def padded(map_ref, pad_ref, scale):
    pad_ref[...] = jnp.zeros_like(pad_ref)
    pad_ref[0:TERMS, 0:TERMS] = map_ref[...] * scale
    return split(pad_ref[...])


def leaf_equivalents(charges, kern, up):
    block = lax.broadcasted_iota(jnp.int32, (RHS, 256), 1) // SLOTS
    keep = [(block == g).astype(F32).astype(BF) for g in range(8)]
    pieces = split(charges)
    out = []
    for half in range(2):
        lanes = slice(half * 256, half * 256 + 256)
        spread = [jnp.concatenate([piece[:, lanes] * keep[g] for g in range(8)], axis=0) for piece in pieces]
        high, low = kern[0][:, lanes], kern[1][:, lanes]
        spread = jnp.concatenate([spread[0], spread[1], spread[0]], axis=1)
        check = dot_nt(spread, jnp.concatenate([high, high, low], axis=1))
        out.append(mm3(split(check), up))
    return out


def store_equivalents(halves, e_ref, first):
    for half in range(2):
        e_high, e_low = split(halves[half])
        for g in range(8):
            start = first + (half * 8 + g) * 2 * RHS
            e_ref[start : start + RHS, :] = e_high[g * RHS : g * RHS + RHS]
            e_ref[start + RHS : start + 2 * RHS, :] = e_low[g * RHS : g * RHS + RHS]


def pack(rows):
    low, high = rows[:, :128], rows[:, 128:]
    n = rows.shape[0]
    top = lax.broadcasted_iota(jnp.int32, (n, 128), 0) % 8 < 4
    first = jnp.where(top, low, pltpu.roll(high, 4, 0))
    second = jnp.where(top, pltpu.roll(low, n - 4, 0), high)
    tiles = []
    for m in range(n // 8):
        tiles += [first[8 * m : 8 * m + 8], second[8 * m : 8 * m + 8]]
    return jnp.concatenate(tiles, axis=0)


def unpack(tiles):
    n = tiles.shape[0] // 2
    first = jnp.concatenate([tiles[16 * m : 16 * m + 8] for m in range(n // 8)], axis=0)
    second = jnp.concatenate([tiles[16 * m + 8 : 16 * m + 16] for m in range(n // 8)], axis=0)
    top = lax.broadcasted_iota(jnp.int32, (n, 128), 0) % 8 < 4
    low = jnp.where(top, first, pltpu.roll(second, 4, 0))
    high = jnp.where(top, pltpu.roll(first, n - 4, 0), second)
    return jnp.concatenate([low, high], axis=1)


def tile_dot(tile, high, low, acc):
    a_high, a_low = split(tile)
    both = jnp.concatenate([a_high, a_low], axis=0)
    rest = SUB - 128
    front = dot(both, high[:128]) + dot(both, low[:128])
    back = dot(both[:, :rest], high[128:]) + dot(both[:, :rest], low[128:])
    return acc[0] + front, acc[1] + back


def tile_sum(acc):
    front = acc[0][:8] + acc[0][8:]
    back = acc[1][:8] + acc[1][8:]
    return front + pltpu.roll(back, 4, 0)


def head_kernel(
    off_hbm, q_hbm, counts_hbm, up_hbm, down_hbm, col_hbm, row_hbm,
    out_ref, halo_ref, up_ref, down_ref, col_ref, row_ref, e_hbm,
    off_ref, q_ref, counts_ref, pad_ref, tab_ref, e_ref, sems,
):
    moves = [
        pltpu.make_async_copy(src, dst, sems.at[n])
        for n, (src, dst) in enumerate(
            (
                (q_hbm, q_ref),
                (off_hbm, off_ref),
                (counts_hbm, counts_ref),
                (up_hbm, up_ref),
                (col_hbm, col_ref),
                (row_hbm, row_ref),
                (down_hbm, down_ref),
            )
        )
    ]
    for move in moves:
        move.start()
    for move in moves[:-1]:
        move.wait()
    lane = lax.broadcasted_iota(jnp.int32, (8, POINTS), 1)
    limit = jnp.zeros((8, POINTS), jnp.int32)
    for g in range(LEAVES):
        limit = jnp.where(lane // SLOTS == g, counts_ref[g], limit)
    filled = (lane % SLOTS < limit)[0:1]
    charges = jnp.where(filled, q_ref[...], 0.0)
    halo_ref[0:RHS, :] = charges
    halo_ref[RHS:ROWS, :] = jnp.zeros((ROWS - RHS, POINTS), F32)
    halo_ref[RHS : RHS + 3, :] = off_ref[...]
    kern = split(leaf_kernel(off_ref[...], col_ref))
    up = padded(up_ref, pad_ref, 18.0 / TERMS)
    up = (up[0][:, :], up[1][:, :])
    halves = leaf_equivalents(charges, kern, up)
    store_equivalents(halves, e_ref, 0)
    e_move = pltpu.make_async_copy(e_ref, e_hbm, sems.at[7])
    e_move.start()
    acc = jnp.zeros((RHS, LANE), F32)
    for (x, y, z), kern in box_kernels(
        (1.5, 0.5, -0.5, -1.5), (0.5, -0.5), (0.5, -0.5), 6.0, 0.9, col_ref, row_ref, tab_ref
    ):
        start = ((x >> 1) * 8 + (x & 1) + 2 * y + 4 * z) * 2 * RHS
        high, low = split(kern)
        wide = dot(e_ref[start : start + 2 * RHS, :][:, :SUB], high)
        acc = acc + wide[:RHS] + wide[RHS:] + dot(e_ref[start : start + RHS, :][:, :SUB], low)
    up60 = padded(up_ref, pad_ref, 60.0 / TERMS)
    out_ref[...] = pack(mm3(split(acc[:, :SUB]), up60))
    moves[-1].wait()
    e_move.wait()


def group_up_kernel(x_ref, maps_ref, up_ref, out_hbm, pad_ref, out_ref, sem):
    acc = (jnp.zeros((16, LANE), F32), jnp.zeros((16, LANE), F32))
    for e in range(INNER):
        acc = tile_dot(x_ref[8 * e : 8 * e + 8, :], maps_ref[e, 0], maps_ref[e, 1], acc)
    check = tile_sum(acc)
    both = jnp.concatenate([check, check], axis=0)
    equiv = mm3(split(both[:, :SUB]), padded(up_ref, pad_ref, 200.0 / TERMS))[:8]
    top = lax.broadcasted_iota(jnp.int32, (8, 128), 0) < 4
    tile = jnp.where(top, equiv[:, :128], pltpu.roll(equiv[:, 128:], 4, 0))
    for p in range(OUTER):
        out_ref[8 * p : 8 * p + 8, :] = tile
    move = pltpu.make_async_copy(out_ref, out_hbm, sem)
    move.start()
    move.wait()


def box_order(rows):
    return jnp.concatenate(
        [rows[8 * k : 8 * k + 8] for k in (y * 4 + x * 2 + z for x in (0, 1) for z in (0, 1) for y in (0, 1))], axis=0
    )


def index_order(rows):
    return jnp.concatenate(
        [rows[8 * k : 8 * k + 8] for k in (x * 4 + z * 2 + y for y in (0, 1) for x in (0, 1) for z in (0, 1))], axis=0
    )


def peers_kernel(x_ref, col_ref, row_ref, out_ref, tab_ref, shifted_ref):
    equiv = jnp.concatenate([box_order(unpack(x_ref[...])), jnp.zeros((16, LANE), F32)], axis=0)
    shifted_ref[...] = jnp.zeros_like(shifted_ref)
    for q in range(4):
        high, low = split(pltpu.roll(equiv, 4 * q, 0) if q else equiv)
        shifted_ref[q, 0, RHS : RHS + 80, :] = high
        shifted_ref[q, 1, RHS : RHS + 80, :] = low
    cols = columns(col_ref)
    for dy in range(-3, 4):
        tab_ref[dy + 3] = square_of(1, 2.0 * dy, 3.0, 3.0, cols, row_ref) + SOFTEN
    row = lax.broadcasted_iota(jnp.int32, (RHS, 128), 0)
    lane = lax.broadcasted_iota(jnp.int32, (RHS, 128), 1)
    px, pz, py = row >> 5, (row >> 4) & 1, (row >> 2) & 3
    dest = (py & 1) + pz * 2 + px * 4 + (py >> 1) * 8

    def valid(dx, dz):
        sx, sy, sz = px - dx, py - (lane - 3), pz - dz
        inside = (sx >= 0) & (sx < 2) & (sy >= 0) & (sy < 4) & (sz >= 0) & (sz < 2)
        source = (sy & 1) + sz * 2 + sx * 4 + (sy >> 1) * 8
        return (inside & (jnp.abs(source - dest) >= 2)).astype(F32)

    def moved(dx, dy, dz, mask):
        q = dy % 4
        start = RHS - (dx * 2 + dz) * 16 - 4 * (dy - q)
        keep = two(jnp.broadcast_to(mask[:, dy + 3 : dy + 4], (RHS, 128))).astype(BF)
        rows = [(shifted_ref[q, n, start : start + RHS, :] * keep)[:, :SUB] for n in range(2)]
        return rows

    acc = (jnp.zeros((RHS, LANE), F32), jnp.zeros((RHS, SUB), F32))
    planes = [(0, 0, (1, 2, 3))] + [(dx, dz, range(-3, 4)) for dx, dz in ((0, 1), (1, -1), (1, 0), (1, 1))]
    for n, (dx, dz, steps) in enumerate(planes):
        plane = square_of(0, dx * 4.0, 3.0, 3.0, cols, row_ref)
        tab_ref[7 + n] = plane + square_of(2, dz * 2.0, 3.0, 3.0, cols, row_ref)
        ahead, behind = valid(dx, dz), valid(-dx, -dz)
        for dy in steps:
            kern = split(lax.rsqrt(tab_ref[7 + n] + tab_ref[dy + 3]))
            forward = acc[0] + mm3(moved(dx, dy, dz, ahead), kern)
            kern = (kern[0][:, :SUB], kern[1][:, :SUB])
            acc = (forward, acc[1] + mm3(moved(-dx, -dy, -dz, behind), kern, dot_nt))
    back = jnp.concatenate([acc[1], jnp.zeros((RHS, LANE - SUB), F32)], axis=1)
    out_ref[...] = index_order(acc[0] + back)


def local_kernel(x_ref, peers_ref, down_ref, col_ref, row_ref, out_ref, pad_ref, tab_ref):
    outer = lax.axis_index("outer")
    own = [p.astype(F32) for p in corner(outer * 256, 8)]
    cols = columns(col_ref)
    for n in range(4):
        tab_ref[n] = square_of(2, own[2] - 4.0 * n, 10.0, 20.0, cols, row_ref) + SOFTEN
    for x in range(4):
        xsq = square_of(0, own[0] - 8.0 * x, 10.0, 20.0, cols, row_ref)
        for y in range(2):
            tab_ref[4 + x * 2 + y] = xsq + square_of(1, own[1] - 8.0 * y, 10.0, 20.0, cols, row_ref)
    acc = (jnp.zeros((16, LANE), F32), jnp.zeros((16, LANE), F32))
    for p in range(OUTER):
        z, x, y = (p & 1) + ((p >> 3) & 1) * 2, ((p >> 1) & 1) + ((p >> 4) & 1) * 2, (p >> 2) & 1
        weight = (jnp.abs(p - outer) >= 2).astype(F32)
        kern = split(lax.rsqrt(tab_ref[4 + x * 2 + y] + tab_ref[z]))
        acc = tile_dot(x_ref[8 * p : 8 * p + 8, :] * weight, kern[0], kern[1], acc)
    check = tile_sum(acc)
    both = jnp.concatenate([check, check], axis=0)
    group = mm3(split(both[:, :SUB]), padded(down_ref, pad_ref, 200.0 / TERMS))[:8]
    pieces = jnp.concatenate(split(group[:, :SUB]), axis=0)
    top = lax.broadcasted_iota(jnp.int32, (8, LANE), 0) < 4
    found = [None] * INNER
    for (x, y, z), kern in box_kernels(
        (-2.0, 2.0), (-3.0, -1.0, 1.0, 3.0), (-1.0, 1.0), 3.0, 20.0, col_ref, row_ref, tab_ref
    ):
        high, low = split(kern)
        part = dot(pieces, high) + dot(pieces, low)
        found[(y & 1) + z * 2 + x * 4 + (y >> 1) * 8] = part[:8] + part[8:]
    merged = [jnp.where(top, found[2 * m], pltpu.roll(found[2 * m + 1], 4, 0)) for m in range(INNER // 2)]
    total = jnp.concatenate(merged, axis=0) + peers_ref[...]
    out_ref[...] = pack(mm3(split(total[:, :SUB]), padded(down_ref, pad_ref, 60.0 / TERMS)))


def operator_kernel(
    flow_ref, off_ref, down_ref, col_ref, row_ref, up_ref, w_hbm, m_hbm, w_ref, m_ref, pad_ref, tab_ref, sems
):
    for (x, y, z), kern in box_kernels(
        (2.0, -2.0), (3.0, 1.0, -1.0, -3.0), (1.0, -1.0), 20.0, 3.0, col_ref, row_ref, tab_ref
    ):
        e = (y & 1) + z * 2 + x * 4 + (y >> 1) * 8
        high, low = split(kern)
        up_ref[e, 0, :, :] = high
        up_ref[e, 1, :, :] = low
    kern = split(leaf_kernel(off_ref[RHS : RHS + 3, :], col_ref))
    down = padded(down_ref, pad_ref, 18.0 / TERMS)
    down = (down[0][:, :SUB], down[1][:, :SUB])
    weights = split(mm3(down, kern))
    w_ref[0, :, :] = weights[0]
    w_ref[1, :, :] = weights[1]
    w_move = pltpu.make_async_copy(w_ref, w_hbm, sems.at[0])
    w_move.start()
    block = lax.broadcasted_iota(jnp.int32, (SUB, 256), 1) // SLOTS
    found = [jnp.zeros((SUB, 256), F32)] * 2
    for (x, y, z), kern in box_kernels(
        (-1.5, -0.5, 0.5, 1.5), (-0.5, 0.5), (-0.5, 0.5), 0.9, 6.0, col_ref, row_ref, tab_ref
    ):
        half, g = (x >> 1), (x & 1) + 2 * y + 4 * z
        lanes = slice(half * 256, half * 256 + 256)
        own = (weights[0][:, lanes], weights[1][:, lanes])
        found[half] = jnp.where(block == g, mm3(split(kern[:, :SUB]), own), found[half])
    for half in range(2):
        lanes = slice(half * 256, half * 256 + 256)
        m_high, m_low = split(found[half])
        m_ref[0, :, lanes] = m_high
        m_ref[1, :, lanes] = m_low
    m_move = pltpu.make_async_copy(m_ref, m_hbm, sems.at[1])
    m_move.start()
    w_move.wait()
    m_move.wait()


def near_field(near_ref, left_ref, own_ref, right_ref, out_ref, mask_ref, high_ref, low_ref):
    offs = jnp.concatenate([own_ref[RHS:ROWS, :], jnp.zeros((120, POINTS), F32)], axis=0).T
    inner = lax.axis_index("inner")
    device = lax.axis_index("outer") * INNER + inner
    base = (device - 1) * LEAVES
    total = 3 * POINTS
    lane = lax.broadcasted_iota(jnp.int32, (LEAVES, total), 1) // SLOTS
    found = jnp.zeros((LEAVES, total), F32)
    near = near_ref[...] - base
    for k in range(12):
        found = jnp.where(lane == near[:, k : k + 1], 1.0, found)
    mask_ref[...] = found
    leaf = lax.broadcasted_iota(jnp.int32, (1, POINTS), 1) // SLOTS
    within = local_leaf(leaf)
    own_box = corner(device * LEAVES, 4)
    sources = []
    for c in range(3):
        lanes = []
        for side, ref in ((-1, left_ref), (0, own_ref), (1, right_ref)):
            box = corner((device + side) * LEAVES, 4)[c] - own_box[c]
            lanes.append(ref[RHS + c : RHS + c + 1, :] + (box + within[c]).astype(F32))
        sources.append(jnp.concatenate(lanes, axis=1))
    for g in range(LEAVES):
        rows = slice(g * SLOTS, g * SLOTS + SLOTS)
        place = local_leaf(g)
        dist = SOFTEN
        for c in range(3):
            diff = (offs[rows, c : c + 1] + float(place[c])) - sources[c]
            dist = dist + diff * diff
        k_high, k_low = split(lax.rsqrt(dist) * mask_ref[g : g + 1, :])
        high_ref[rows, :] = k_high
        low_ref[rows, :] = k_low
    charges = jnp.concatenate([r[0:RHS, :] for r in (left_ref, own_ref, right_ref)], axis=1)
    q_high, q_low = split(charges)
    both = jnp.concatenate([q_high, q_low], axis=0)
    res = dot_nt(high_ref[...], both)
    res = res + jnp.concatenate([dot_nt(low_ref[...], q_high), jnp.zeros((POINTS, RHS), F32)], axis=1)
    flipped = res.T
    out_ref[...] = flipped[:RHS] + flipped[RHS:]


def field_kernel(
    far_ref, near_ref, own_ref, swap_ref, cross_ref, up_ref, col_ref, row_ref, w_hbm, m_hbm, e_hbm, out_ref, m_ref,
    pad_ref, e_ref, dl_ref, xtab_ref, tab_ref, w_ref, left_ref, right_ref, mask_ref, high_ref, low_ref, sems,
):
    middle = LEAVES * 2 * RHS
    moves = [
        pltpu.make_async_copy(e_hbm, e_ref.at[middle : 2 * middle], sems.at[0]),
        pltpu.make_async_copy(w_hbm, w_ref, sems.at[1]),
        pltpu.make_async_copy(m_hbm, m_ref, sems.at[2]),
    ]
    for move in moves:
        move.start()
    odd = lax.rem(lax.axis_index("inner"), 2) == 1
    left_ref[...] = jnp.where(odd, swap_ref[...], cross_ref[...])
    right_ref[...] = jnp.where(odd, cross_ref[...], swap_ref[...])
    near_field(near_ref, left_ref, own_ref, right_ref, out_ref, mask_ref, high_ref, low_ref)
    inner = lax.axis_index("inner")
    device = lax.axis_index("outer") * INNER + inner
    up = padded(up_ref, pad_ref, 18.0 / TERMS)
    for side, ref in ((0, left_ref), (2, right_ref)):
        kern = split(leaf_kernel(ref[RHS : RHS + 3, :], col_ref))
        store_equivalents(leaf_equivalents(ref[0:RHS, :], kern, up), e_ref, side * middle)
    for move in moves:
        move.wait()
    first = (device - 1) * LEAVES
    boxes = [corner((device + side) * LEAVES, 4) for side in (-1, 0, 1)]
    boxes = [[(boxes[1][c] - box[c]).astype(F32) for c in range(3)] for box in boxes]
    cols = columns(col_ref)
    for side in range(3):
        for n in range(7):
            xtab_ref[side * 7 + n] = square_of(0, boxes[side][0] + (n - 3.0), 0.9, 1.8, cols, row_ref)
        for c in range(3):
            tab_ref[27 + c] = square_of(2, boxes[side][2] + (c - 1.0), 0.9, 1.8, cols, row_ref) + SOFTEN
        for b in range(3):
            ysq = square_of(1, boxes[side][1] + (b - 1.0), 0.9, 1.8, cols, row_ref)
            for c in range(3):
                tab_ref[side * 9 + b * 3 + c] = ysq + tab_ref[27 + c]

    def one_leaf(g, carry):
        own = local_leaf(g)
        wide = jnp.zeros((2 * RHS, LANE), F32)
        narrow = jnp.zeros((RHS, LANE), F32)
        rest = jnp.zeros((LANE - SUB, LANE), BF)
        for k in range(0, 12, 4):
            tops, lows, equivs = [], [], []
            for n in range(k, k + 4):
                window = far_ref[g, n] - first
                side = window >> 4
                place = local_leaf(window & 15)
                x = side * 7 + 3 + own[0] - place[0]
                yz = side * 9 + 4 + (own[1] - place[1]) * 3 + own[2] - place[2]
                k_high, k_low = split(lax.rsqrt(xtab_ref[x] + tab_ref[yz]))
                tops += [k_high, rest]
                lows += [k_low, rest]
                equivs.append(e_ref[pl.ds(pl.multiple_of(window * (2 * RHS), 2 * RHS), 2 * RHS), :])
            equiv = jnp.concatenate(equivs, axis=1)
            wide = wide + dot(equiv, jnp.concatenate(tops, axis=0))
            narrow = narrow + dot(equiv[:RHS], jnp.concatenate(lows, axis=0))
        acc = wide[:RHS] + wide[RHS:] + narrow
        high, low = split(acc)
        start = pl.multiple_of(g * RHS, RHS)
        dl_ref[0, pl.ds(start, RHS), :] = high
        dl_ref[1, pl.ds(start, RHS), :] = low
        return carry

    lax.fori_loop(0, LEAVES, one_leaf, 0)
    block = lax.broadcasted_iota(jnp.int32, (RHS, 256), 1) // SLOTS
    for half in range(2):
        lanes = slice(half * 256, half * 256 + 256)
        rows = slice(half * 8 * RHS, (half + 1) * 8 * RHS)
        local = (dl_ref[0, rows, :][:, :SUB], dl_ref[1, rows, :][:, :SUB])
        res = mm3(local, (w_ref[0, :, lanes], w_ref[1, :, lanes]))
        acc = out_ref[:, lanes]
        for g in range(8):
            acc = acc + jnp.where(block == g, res[g * RHS : (g + 1) * RHS], 0.0)
        out_ref[:, lanes] = acc


def tail_kernel(x_ref, base_ref, m_ref, out_ref):
    local = split(unpack(x_ref[...])[:, :SUB])
    out_ref[...] = base_ref[...] + mm3(local, (m_ref[0], m_ref[1]))


VM = pl.BlockSpec(memory_space=pltpu.VMEM)
SM = pl.BlockSpec(memory_space=pltpu.SMEM)
HB = pl.BlockSpec(memory_space=pltpu.HBM)


def call(kernel, name, outs, specs, scratch, vmem, *args, out_specs=None):
    return pl.pallas_call(
        kernel,
        name=name,
        out_shape=outs,
        in_specs=specs,
        out_specs=out_specs or jax.tree.map(lambda _: VM, outs),
        scratch_shapes=scratch,
        compiler_params=pltpu.CompilerParams(vmem_limit_bytes=vmem * 1024 * 1024),
        cost_estimate=pl.CostEstimate(flops=1000, bytes_accessed=1000, transcendentals=0),
    )(*args)


def in_hbm(x):
    return pltpu.with_memory_space_constraint(x, pltpu.HBM)


def tie(value, *others):
    return lax.optimization_barrier((value,) + others)[0]


def shards(offsets, charges, counts, near, far, upward, downward):
    col_np, row_np = sphere_tables()
    sds = jax.ShapeDtypeStruct
    pad = pltpu.VMEM((SUB, LANE), F32)
    flow = sds((2 * RHS, 128), F32)
    square = sds((TERMS, TERMS), F32)

    def tables(n):
        return pltpu.VMEM((n, SUB, LANE), F32)

    inputs = (offsets, charges, counts, upward, downward, jnp.asarray(col_np), jnp.asarray(row_np))
    equiv_rows = LEAVES * 2 * RHS
    dev_equiv, own, upward, downward, col, row, equiv = call(
        head_kernel, "leaf_and_device_equiv",
        (flow, sds((ROWS, POINTS), F32), square, square, sds((SUB, 128), F32), sds((8, LANE), F32), pltpu.HBM((equiv_rows, LANE), BF)),
        [HB] * 7,
        [
            pltpu.VMEM((3, POINTS), F32),
            pltpu.VMEM((RHS, POINTS), F32),
            pltpu.SMEM((LEAVES,), jnp.int32),
            pad,
            tables(10),
            pltpu.VMEM((equiv_rows, LANE), BF),
            pltpu.SemaphoreType.DMA((8,)),
        ],
        16, *map(in_hbm, inputs), out_specs=(VM, VM, VM, VM, VM, VM, HB),
    )
    peers_equiv = lax.all_to_all(dev_equiv, "inner", 0, 0, tiled=True)
    leaf_maps = pltpu.HBM((2, SUB, POINTS), BF)
    up_maps, weights, evaluate = call(
        operator_kernel, "evaluation_and_group_maps", (sds((INNER, 2, SUB, LANE), BF), leaf_maps, leaf_maps),
        [VM, VM, VM, VM, VM],
        [pltpu.VMEM((2, SUB, POINTS), BF), pltpu.VMEM((2, SUB, POINTS), BF), pad, tables(14), pltpu.SemaphoreType.DMA((2,))],
        14, dev_equiv, own, downward, col, row, out_specs=(VM, HB, HB),
    )
    swap = lax.ppermute(own, "inner", [(i, i ^ 1) for i in range(INNER)])
    cross = lax.ppermute(own, "inner", [(i, ((i + 1) ^ 1) - 1) for i in range(1, INNER - 1)])
    group_equiv = call(
        group_up_kernel, "group_equiv", pltpu.HBM((8 * OUTER, 128), F32), [VM, VM, VM],
        [pad, pltpu.VMEM((8 * OUTER, 128), F32), pltpu.SemaphoreType.DMA], 6,
        peers_equiv, up_maps, upward, out_specs=HB,
    )
    groups = lax.all_to_all(group_equiv, "outer", 0, 0, tiled=True)
    peers_part = call(
        peers_kernel, "device_to_device", sds((RHS, LANE), F32), [VM, VM, VM],
        [tables(12), pltpu.VMEM((4, 2, 3 * RHS, LANE), BF)], 10, peers_equiv, col, row,
    )
    groups = tie(groups, peers_part)
    local = call(
        local_kernel, "group_and_device_local", flow, [VM, VM, VM, VM, VM], [pad, tables(14)], 8,
        groups, peers_part, downward, col, row,
    )
    dev_local = lax.all_to_all(local, "inner", 0, 0, tiled=True)
    base, evaluate = call(
        field_kernel, "near_and_far_field", (sds((RHS, POINTS), F32), sds((2, SUB, POINTS), BF)),
        [SM, VM, VM, VM, VM, VM, VM, VM, HB, HB, HB],
        [
            pad,
            pltpu.VMEM((3 * LEAVES * 2 * RHS, LANE), BF),
            pltpu.VMEM((2, LEAVES * RHS, LANE), BF),
            tables(21),
            tables(30),
            pltpu.VMEM((2, SUB, POINTS), BF),
            pltpu.VMEM((ROWS, POINTS), F32),
            pltpu.VMEM((ROWS, POINTS), F32),
            pltpu.VMEM((LEAVES, 3 * POINTS), F32),
            pltpu.VMEM((POINTS, 3 * POINTS), BF),
            pltpu.VMEM((POINTS, 3 * POINTS), BF),
            pltpu.SemaphoreType.DMA((3,)),
        ],
        32, far, near, own, swap, cross, upward, col, row, in_hbm(weights), in_hbm(evaluate), in_hbm(equiv),
    )
    return call(tail_kernel, "potential", sds((RHS, POINTS), F32), [VM, VM, VM], [], 4, dev_local, base, evaluate)


def solution(mesh):
    both = ("outer", "inner")
    in_specs = (P(None, both), P(None, both), P(both), P(both, None), P(both, None), P(), P())
    return jax.shard_map(shards, mesh=mesh, in_specs=in_specs, out_specs=P(None, both), check_vma=False)
```

```python
import functools

import jax
import jax.numpy as jnp
import numpy as np
from jax import lax
from jax.experimental import pallas as pl
from jax.experimental.pallas import tpu as pltpu
from jax.sharding import PartitionSpec as P

SOFTEN = 0.25
GOLDEN = 2.399963229728653
RHS = 64
TERMS = 165
SUB = 176
LANE = 256
LEAVES = 16
SLOTS = 32
POINTS = LEAVES * SLOTS
ROWS = 72
INNER = 16
OUTER = 32
PART = RHS // INNER
EARLY = 6
HALF_E = LEAVES * 2 * RHS
BF = jnp.bfloat16
F32 = jnp.float32


def sphere_tables():
    steps = np.arange(TERMS, dtype=np.float32)
    height = (np.float32(1.0) - (np.float32(2.0) * steps + np.float32(1.0)) / np.float32(TERMS)).astype(np.float32)
    radial = np.sqrt(np.maximum(np.float32(1.0) - height * height, np.float32(0.0))).astype(np.float32)
    angle = (steps * np.float32(GOLDEN)).astype(np.float32)
    dirs = np.stack([radial * np.cos(angle), radial * np.sin(angle), height]).astype(np.float32)
    col = np.zeros((SUB, 128), np.float32)
    col[:TERMS, :3] = dirs.T
    row = np.zeros((8, LANE), np.float32)
    row[:3, :TERMS] = dirs
    return col, row


def split(x):
    high = x.astype(BF)
    return high, (x - high.astype(F32)).astype(BF)


def dot(a, b):
    return jnp.dot(a, b, preferred_element_type=F32)


def dot_nt(a, b):
    return lax.dot_general(a, b, (((1,), (1,)), ((), ())), preferred_element_type=F32)


def mm3(a, b, f=dot):
    return f(a[0], b[0]) + f(a[1], b[0]) + f(a[0], b[1])


def columns(col_ref):
    return [jnp.broadcast_to(col_ref[:, c : c + 1], (SUB, 128)) for c in range(3)]


def two(x):
    return jnp.concatenate([x, x], axis=1)


def square_of(axis, shift, radius_t, radius_i, cols, row_ref):
    diff = (radius_t * row_ref[axis : axis + 1, :] + shift) - two(radius_i * cols[axis])
    return diff * diff


def box_kernels(xs, ys, zs, radius_t, radius_i, col_ref, row_ref, tab_ref):
    cols = columns(col_ref)
    for n, shift in enumerate(xs):
        tab_ref[n] = square_of(0, shift, radius_t, radius_i, cols, row_ref)
    zsq = len(xs)
    for n, shift in enumerate(zs):
        tab_ref[zsq + n] = square_of(2, shift, radius_t, radius_i, cols, row_ref) + SOFTEN
    start = zsq + len(zs)
    for b, shift in enumerate(ys):
        ysq = square_of(1, shift, radius_t, radius_i, cols, row_ref)
        for c in range(len(zs)):
            tab_ref[start + b * len(zs) + c] = ysq + tab_ref[zsq + c]
    for b in range(len(ys)):
        for c in range(len(zs)):
            for a in range(len(xs)):
                yield (a, b, c), lax.rsqrt(tab_ref[a] + tab_ref[start + b * len(zs) + c])


def bits(ids, low, axis, top=14):
    total = 0
    for level in range(5):
        place = 3 * level + axis
        if low <= place < top:
            total = total + (((ids >> place) & 1) << level)
    return total


def corner(leaf_id, low):
    return [bits(leaf_id, low, axis) for axis in range(3)]


def local_leaf(index):
    return ((index & 1) + ((index >> 3) & 1) * 2, (index >> 1) & 1, (index >> 2) & 1)


def peer_box(inner):
    return (((inner >> 2) & 1) * 4, (inner & 1) * 2 + ((inner >> 3) & 1) * 4, ((inner >> 1) & 1) * 2)


def leaf_kernel(offs, col_ref):
    total = SOFTEN
    for c in range(3):
        col = jnp.broadcast_to(col_ref[:, c : c + 1], (SUB, 128)) * 1.8
        diff = jnp.concatenate([col] * (POINTS // 128), axis=1) - offs[c : c + 1, :]
        total = total + diff * diff
    return lax.rsqrt(total)


def padded(map_ref, pad_ref, scale):
    pad_ref[...] = jnp.zeros_like(pad_ref)
    pad_ref[0:TERMS, 0:TERMS] = map_ref[...] * scale
    return split(pad_ref[...])


def leaf_equivalents(charges, kern, up):
    block = lax.broadcasted_iota(jnp.int32, (RHS, 256), 1) // SLOTS
    keep = [(block == g).astype(F32).astype(BF) for g in range(8)]
    pieces = split(charges)
    out = []
    for half in range(2):
        lanes = slice(half * 256, half * 256 + 256)
        spread = [jnp.concatenate([piece[:, lanes] * keep[g] for g in range(8)], axis=0) for piece in pieces]
        high, low = kern[0][:, lanes], kern[1][:, lanes]
        spread = jnp.concatenate([spread[0], spread[1], spread[0]], axis=1)
        check = dot_nt(spread, jnp.concatenate([high, high, low], axis=1))
        out.append(mm3(split(check), up))
    return out


def store_equivalents(halves, e_ref, first):
    for half in range(2):
        e_high, e_low = split(halves[half])
        for g in range(8):
            start = first + (half * 8 + g) * 2 * RHS
            e_ref[start : start + RHS, :] = e_high[g * RHS : g * RHS + RHS]
            e_ref[start + RHS : start + 2 * RHS, :] = e_low[g * RHS : g * RHS + RHS]


def pack(rows):
    low, high = rows[:, :128], rows[:, 128:]
    n = rows.shape[0]
    top = lax.broadcasted_iota(jnp.int32, (n, 128), 0) % 8 < 4
    first = jnp.where(top, low, pltpu.roll(high, 4, 0))
    second = jnp.where(top, pltpu.roll(low, n - 4, 0), high)
    tiles = []
    for m in range(n // 8):
        tiles += [first[8 * m : 8 * m + 8], second[8 * m : 8 * m + 8]]
    return jnp.concatenate(tiles, axis=0)


def unpack(tiles):
    n = tiles.shape[0] // 2
    first = jnp.concatenate([tiles[16 * m : 16 * m + 8] for m in range(n // 8)], axis=0)
    second = jnp.concatenate([tiles[16 * m + 8 : 16 * m + 16] for m in range(n // 8)], axis=0)
    top = lax.broadcasted_iota(jnp.int32, (n, 128), 0) % 8 < 4
    low = jnp.where(top, first, pltpu.roll(second, 4, 0))
    high = jnp.where(top, pltpu.roll(first, n - 4, 0), second)
    return jnp.concatenate([low, high], axis=1)


def tile_dot(tile, high, low, acc):
    a_high, a_low = split(tile)
    both = jnp.concatenate([a_high, a_low], axis=0)
    rest = SUB - 128
    front = dot(both, high[:128]) + dot(both, low[:128])
    back = dot(both[:, :rest], high[128:]) + dot(both[:, :rest], low[128:])
    return acc[0] + front, acc[1] + back


def tile_sum(acc):
    front = acc[0][:8] + acc[0][8:]
    back = acc[1][:8] + acc[1][8:]
    return front + pltpu.roll(back, 4, 0)


def head_kernel(
    off_hbm, q_hbm, counts_hbm, up_hbm, down_hbm, col_hbm, row_hbm,
    out_ref, halo_ref, up_ref, down_ref, col_ref, row_ref, e_hbm,
    off_ref, q_ref, counts_ref, pad_ref, tab_ref, e_ref, sems,
):
    moves = [
        pltpu.make_async_copy(src, dst, sems.at[n])
        for n, (src, dst) in enumerate(
            (
                (q_hbm, q_ref),
                (off_hbm, off_ref),
                (counts_hbm, counts_ref),
                (up_hbm, up_ref),
                (col_hbm, col_ref),
                (row_hbm, row_ref),
                (down_hbm, down_ref),
            )
        )
    ]
    for move in moves:
        move.start()
    for move in moves[:-1]:
        move.wait()
    lane = lax.broadcasted_iota(jnp.int32, (8, POINTS), 1)
    limit = jnp.zeros((8, POINTS), jnp.int32)
    for g in range(LEAVES):
        limit = jnp.where(lane // SLOTS == g, counts_ref[g], limit)
    filled = (lane % SLOTS < limit)[0:1]
    charges = jnp.where(filled, q_ref[...], 0.0)
    halo_ref[0:RHS, :] = charges
    halo_ref[RHS:ROWS, :] = jnp.zeros((ROWS - RHS, POINTS), F32)
    halo_ref[RHS : RHS + 3, :] = off_ref[...]
    kern = split(leaf_kernel(off_ref[...], col_ref))
    up = padded(up_ref, pad_ref, 18.0 / TERMS)
    up = (up[0][:, :], up[1][:, :])
    halves = leaf_equivalents(charges, kern, up)
    store_equivalents(halves, e_ref, 0)
    e_move = pltpu.make_async_copy(e_ref, e_hbm, sems.at[7])
    e_move.start()
    acc = jnp.zeros((RHS, LANE), F32)
    for (x, y, z), kern in box_kernels(
        (1.5, 0.5, -0.5, -1.5), (0.5, -0.5), (0.5, -0.5), 6.0, 0.9, col_ref, row_ref, tab_ref
    ):
        start = ((x >> 1) * 8 + (x & 1) + 2 * y + 4 * z) * 2 * RHS
        high, low = split(kern)
        wide = dot(e_ref[start : start + 2 * RHS, :][:, :SUB], high)
        acc = acc + wide[:RHS] + wide[RHS:] + dot(e_ref[start : start + RHS, :][:, :SUB], low)
    up60 = padded(up_ref, pad_ref, 60.0 / TERMS)
    out_ref[...] = pack(mm3(split(acc[:, :SUB]), up60))
    moves[-1].wait()
    e_move.wait()


def group_up_kernel(x_ref, maps_ref, up_ref, out_hbm, pad_ref, out_ref, sem):
    acc = (jnp.zeros((16, LANE), F32), jnp.zeros((16, LANE), F32))
    for e in range(INNER):
        acc = tile_dot(x_ref[8 * e : 8 * e + 8, :], maps_ref[e, 0], maps_ref[e, 1], acc)
    check = tile_sum(acc)
    both = jnp.concatenate([check, check], axis=0)
    equiv = mm3(split(both[:, :SUB]), padded(up_ref, pad_ref, 200.0 / TERMS))[:8]
    top = lax.broadcasted_iota(jnp.int32, (8, 128), 0) < 4
    tile = jnp.where(top, equiv[:, :128], pltpu.roll(equiv[:, 128:], 4, 0))
    for p in range(OUTER):
        out_ref[8 * p : 8 * p + 8, :] = tile
    move = pltpu.make_async_copy(out_ref, out_hbm, sem)
    move.start()
    move.wait()


def box_order(rows):
    return jnp.concatenate(
        [rows[8 * k : 8 * k + 8] for k in (y * 4 + x * 2 + z for x in (0, 1) for z in (0, 1) for y in (0, 1))], axis=0
    )


def index_order(rows):
    return jnp.concatenate(
        [rows[8 * k : 8 * k + 8] for k in (x * 4 + z * 2 + y for y in (0, 1) for x in (0, 1) for z in (0, 1))], axis=0
    )


def peers_kernel(x_ref, col_ref, row_ref, out_ref, tab_ref, shifted_ref):
    equiv = jnp.concatenate([box_order(unpack(x_ref[...])), jnp.zeros((16, LANE), F32)], axis=0)
    shifted_ref[...] = jnp.zeros_like(shifted_ref)
    for q in range(4):
        high, low = split(pltpu.roll(equiv, 4 * q, 0) if q else equiv)
        shifted_ref[q, 0, RHS : RHS + 80, :] = high
        shifted_ref[q, 1, RHS : RHS + 80, :] = low
    cols = columns(col_ref)
    for dy in range(-3, 4):
        tab_ref[dy + 3] = square_of(1, 2.0 * dy, 3.0, 3.0, cols, row_ref) + SOFTEN
    row = lax.broadcasted_iota(jnp.int32, (RHS, 128), 0)
    lane = lax.broadcasted_iota(jnp.int32, (RHS, 128), 1)
    px, pz, py = row >> 5, (row >> 4) & 1, (row >> 2) & 3
    dest = (py & 1) + pz * 2 + px * 4 + (py >> 1) * 8

    def valid(dx, dz):
        sx, sy, sz = px - dx, py - (lane - 3), pz - dz
        inside = (sx >= 0) & (sx < 2) & (sy >= 0) & (sy < 4) & (sz >= 0) & (sz < 2)
        source = (sy & 1) + sz * 2 + sx * 4 + (sy >> 1) * 8
        return (inside & (jnp.abs(source - dest) >= 2)).astype(F32)

    def moved(dx, dy, dz, mask):
        q = dy % 4
        start = RHS - (dx * 2 + dz) * 16 - 4 * (dy - q)
        keep = two(jnp.broadcast_to(mask[:, dy + 3 : dy + 4], (RHS, 128))).astype(BF)
        rows = [(shifted_ref[q, n, start : start + RHS, :] * keep)[:, :SUB] for n in range(2)]
        return rows

    acc = (jnp.zeros((RHS, LANE), F32), jnp.zeros((RHS, SUB), F32))
    planes = [(0, 0, (1, 2, 3))] + [(dx, dz, range(-3, 4)) for dx, dz in ((0, 1), (1, -1), (1, 0), (1, 1))]
    for n, (dx, dz, steps) in enumerate(planes):
        plane = square_of(0, dx * 4.0, 3.0, 3.0, cols, row_ref)
        tab_ref[7 + n] = plane + square_of(2, dz * 2.0, 3.0, 3.0, cols, row_ref)
        ahead, behind = valid(dx, dz), valid(-dx, -dz)
        for dy in steps:
            kern = split(lax.rsqrt(tab_ref[7 + n] + tab_ref[dy + 3]))
            forward = acc[0] + mm3(moved(dx, dy, dz, ahead), kern)
            kern = (kern[0][:, :SUB], kern[1][:, :SUB])
            acc = (forward, acc[1] + mm3(moved(-dx, -dy, -dz, behind), kern, dot_nt))
    back = jnp.concatenate([acc[1], jnp.zeros((RHS, LANE - SUB), F32)], axis=1)
    out_ref[...] = index_order(acc[0] + back)


def local_kernel(x_ref, peers_ref, down_ref, col_ref, row_ref, out_ref, pad_ref, tab_ref):
    outer = lax.axis_index("outer")
    own = [p.astype(F32) for p in corner(outer * 256, 8)]
    cols = columns(col_ref)
    for n in range(4):
        tab_ref[n] = square_of(2, own[2] - 4.0 * n, 10.0, 20.0, cols, row_ref) + SOFTEN
    for x in range(4):
        xsq = square_of(0, own[0] - 8.0 * x, 10.0, 20.0, cols, row_ref)
        for y in range(2):
            tab_ref[4 + x * 2 + y] = xsq + square_of(1, own[1] - 8.0 * y, 10.0, 20.0, cols, row_ref)
    acc = (jnp.zeros((16, LANE), F32), jnp.zeros((16, LANE), F32))
    for p in range(OUTER):
        z, x, y = (p & 1) + ((p >> 3) & 1) * 2, ((p >> 1) & 1) + ((p >> 4) & 1) * 2, (p >> 2) & 1
        weight = (jnp.abs(p - outer) >= 2).astype(F32)
        kern = split(lax.rsqrt(tab_ref[4 + x * 2 + y] + tab_ref[z]))
        acc = tile_dot(x_ref[8 * p : 8 * p + 8, :] * weight, kern[0], kern[1], acc)
    check = tile_sum(acc)
    both = jnp.concatenate([check, check], axis=0)
    group = mm3(split(both[:, :SUB]), padded(down_ref, pad_ref, 200.0 / TERMS))[:8]
    pieces = jnp.concatenate(split(group[:, :SUB]), axis=0)
    top = lax.broadcasted_iota(jnp.int32, (8, LANE), 0) < 4
    found = [None] * INNER
    for (x, y, z), kern in box_kernels(
        (-2.0, 2.0), (-3.0, -1.0, 1.0, 3.0), (-1.0, 1.0), 3.0, 20.0, col_ref, row_ref, tab_ref
    ):
        high, low = split(kern)
        part = dot(pieces, high) + dot(pieces, low)
        found[(y & 1) + z * 2 + x * 4 + (y >> 1) * 8] = part[:8] + part[8:]
    merged = [jnp.where(top, found[2 * m], pltpu.roll(found[2 * m + 1], 4, 0)) for m in range(INNER // 2)]
    total = jnp.concatenate(merged, axis=0) + peers_ref[...]
    out_ref[...] = pack(mm3(split(total[:, :SUB]), padded(down_ref, pad_ref, 60.0 / TERMS)))


def operator_kernel(
    flow_ref, off_ref, down_ref, col_ref, row_ref, up_ref, w_hbm, m_hbm, w_ref, m_ref, pad_ref, tab_ref, sems
):
    for (x, y, z), kern in box_kernels(
        (2.0, -2.0), (3.0, 1.0, -1.0, -3.0), (1.0, -1.0), 20.0, 3.0, col_ref, row_ref, tab_ref
    ):
        e = (y & 1) + z * 2 + x * 4 + (y >> 1) * 8
        high, low = split(kern)
        up_ref[e, 0, :, :] = high
        up_ref[e, 1, :, :] = low
    kern = split(leaf_kernel(off_ref[RHS : RHS + 3, :], col_ref))
    down = padded(down_ref, pad_ref, 18.0 / TERMS)
    down = (down[0][:, :SUB], down[1][:, :SUB])
    weights = split(mm3(down, kern))
    w_ref[0, :, :] = weights[0]
    w_ref[1, :, :] = weights[1]
    w_move = pltpu.make_async_copy(w_ref, w_hbm, sems.at[0])
    w_move.start()
    block = lax.broadcasted_iota(jnp.int32, (SUB, 256), 1) // SLOTS
    found = [jnp.zeros((SUB, 256), F32)] * 2
    for (x, y, z), kern in box_kernels(
        (-1.5, -0.5, 0.5, 1.5), (-0.5, 0.5), (-0.5, 0.5), 0.9, 6.0, col_ref, row_ref, tab_ref
    ):
        half, g = (x >> 1), (x & 1) + 2 * y + 4 * z
        lanes = slice(half * 256, half * 256 + 256)
        own = (weights[0][:, lanes], weights[1][:, lanes])
        found[half] = jnp.where(block == g, mm3(split(kern[:, :SUB]), own), found[half])
    for half in range(2):
        lanes = slice(half * 256, half * 256 + 256)
        m_high, m_low = split(found[half])
        m_ref[0, :, lanes] = m_high
        m_ref[1, :, lanes] = m_low
    m_move = pltpu.make_async_copy(m_ref, m_hbm, sems.at[1])
    m_move.start()
    w_move.wait()
    m_move.wait()


def near_field(near_ref, left_ref, own_ref, right_ref, out_ref, mask_ref, high_ref, low_ref):
    offs = jnp.concatenate([own_ref[RHS:ROWS, :], jnp.zeros((120, POINTS), F32)], axis=0).T
    inner = lax.axis_index("inner")
    device = lax.axis_index("outer") * INNER + inner
    base = (device - 1) * LEAVES
    total = 3 * POINTS
    lane = lax.broadcasted_iota(jnp.int32, (LEAVES, total), 1) // SLOTS
    found = jnp.zeros((LEAVES, total), F32)
    near = near_ref[...] - base
    for k in range(12):
        found = jnp.where(lane == near[:, k : k + 1], 1.0, found)
    mask_ref[...] = found
    leaf = lax.broadcasted_iota(jnp.int32, (1, POINTS), 1) // SLOTS
    within = local_leaf(leaf)
    own_box = corner(device * LEAVES, 4)
    sources = []
    for c in range(3):
        lanes = []
        for side, ref in ((-1, left_ref), (0, own_ref), (1, right_ref)):
            box = corner((device + side) * LEAVES, 4)[c] - own_box[c]
            lanes.append(ref[RHS + c : RHS + c + 1, :] + (box + within[c]).astype(F32))
        sources.append(jnp.concatenate(lanes, axis=1))
    for g in range(LEAVES):
        rows = slice(g * SLOTS, g * SLOTS + SLOTS)
        place = local_leaf(g)
        dist = SOFTEN
        for c in range(3):
            diff = (offs[rows, c : c + 1] + float(place[c])) - sources[c]
            dist = dist + diff * diff
        k_high, k_low = split(lax.rsqrt(dist) * mask_ref[g : g + 1, :])
        high_ref[rows, :] = k_high
        low_ref[rows, :] = k_low
    charges = jnp.concatenate([r[0:RHS, :] for r in (left_ref, own_ref, right_ref)], axis=1)
    q_high, q_low = split(charges)
    both = jnp.concatenate([q_high, q_low], axis=0)
    res = dot_nt(high_ref[...], both)
    res = res + jnp.concatenate([dot_nt(low_ref[...], q_high), jnp.zeros((POINTS, RHS), F32)], axis=1)
    flipped = res.T
    out_ref[...] = flipped[:RHS] + flipped[RHS:]


def side_moves(sources, places, sems):
    return [pltpu.make_async_copy(src, dst, sems.at[n]) for n, (src, dst) in enumerate(zip(sources, places))]


def from_sides(own_ref, up_ref, col_ref, out_ref, e_ref, starts, work):
    near_ref, swap_ref, cross_ref, pad_ref, left_ref, right_ref, mask_ref, high_ref, low_ref = work
    odd = lax.rem(lax.axis_index("inner"), 2) == 1
    left_ref[...] = jnp.where(odd, swap_ref[...], cross_ref[...])
    right_ref[...] = jnp.where(odd, cross_ref[...], swap_ref[...])
    near_field(near_ref, left_ref, own_ref, right_ref, out_ref, mask_ref, high_ref, low_ref)
    up = padded(up_ref, pad_ref, 18.0 / TERMS)
    for start, ref in zip(starts, (left_ref, right_ref)):
        kern = split(leaf_kernel(ref[RHS : RHS + 3, :], col_ref))
        store_equivalents(leaf_equivalents(ref[0:RHS, :], kern, up), e_ref, start)


def early_kernel(
    own_ref, up_ref, col_ref, near_hbm, swap_ref, cross_ref, base_hbm, e_hbm, swap_hbm, cross_hbm,
    base_ref, e_ref, near_ref, *work
):
    *work, sems, keep_sems = work
    keeps = side_moves((swap_ref, cross_ref), (swap_hbm, cross_hbm), keep_sems)
    for move in keeps:
        move.start()
    work = (near_ref, swap_ref, cross_ref, *work)

    @pl.when(lax.axis_index("inner") < EARLY)
    def _():
        for step in ("start", "wait"):
            for move in side_moves((near_hbm,), (near_ref,), sems):
                getattr(move, step)()
        from_sides(own_ref, up_ref, col_ref, base_ref, e_ref, (0, HALF_E), work)
        for step in ("start", "wait"):
            for move in side_moves((base_ref, e_ref), (base_hbm, e_hbm), sems):
                getattr(move, step)()

    for move in keeps:
        move.wait()


def field_kernel(
    far_ref, own_ref, up_ref, col_ref, row_ref, near_hbm, swap_hbm, cross_hbm, w_hbm, m_hbm, e_hbm, base_hbm, sides_hbm,
    out_ref, m_ref, e_ref, dl_ref, xtab_ref, tab_ref, w_ref, *work,
):
    *work, sems, early_sems, late_sems = work
    inner = lax.axis_index("inner")
    device = lax.axis_index("outer") * INNER + inner
    moves = side_moves((e_hbm, w_hbm, m_hbm), (e_ref.at[HALF_E : 2 * HALF_E], w_ref, m_ref), sems)
    early = side_moves(
        (base_hbm, sides_hbm.at[0:HALF_E], sides_hbm.at[HALF_E : 2 * HALF_E]),
        (out_ref, e_ref.at[0:HALF_E], e_ref.at[2 * HALF_E : 3 * HALF_E]),
        early_sems,
    )
    late = side_moves((near_hbm, swap_hbm, cross_hbm), work, late_sems)
    for move in moves:
        move.start()

    @pl.when(inner < EARLY)
    def _():
        for move in early:
            move.start()

    @pl.when(inner >= EARLY)
    def _():
        for move in late:
            move.start()

    first = (device - 1) * LEAVES
    boxes = [corner((device + side) * LEAVES, 4) for side in (-1, 0, 1)]
    boxes = [[(boxes[1][c] - box[c]).astype(F32) for c in range(3)] for box in boxes]
    cols = columns(col_ref)
    for side in range(3):
        for n in range(7):
            xtab_ref[side * 7 + n] = square_of(0, boxes[side][0] + (n - 3.0), 0.9, 1.8, cols, row_ref)
        for c in range(3):
            tab_ref[27 + c] = square_of(2, boxes[side][2] + (c - 1.0), 0.9, 1.8, cols, row_ref) + SOFTEN
        for b in range(3):
            ysq = square_of(1, boxes[side][1] + (b - 1.0), 0.9, 1.8, cols, row_ref)
            for c in range(3):
                tab_ref[side * 9 + b * 3 + c] = ysq + tab_ref[27 + c]

    @pl.when(inner < EARLY)
    def _():
        for move in early:
            move.wait()

    @pl.when(inner >= EARLY)
    def _():
        for move in late:
            move.wait()
        from_sides(own_ref, up_ref, col_ref, out_ref, e_ref, (0, 2 * HALF_E), work)

    for move in moves:
        move.wait()

    def one_leaf(g, carry):
        own = local_leaf(g)
        wide = jnp.zeros((2 * RHS, LANE), F32)
        narrow = jnp.zeros((RHS, LANE), F32)
        rest = jnp.zeros((LANE - SUB, LANE), BF)
        for k in range(0, 12, 4):
            tops, lows, equivs = [], [], []
            for n in range(k, k + 4):
                window = far_ref[g, n] - first
                side = window >> 4
                place = local_leaf(window & 15)
                x = side * 7 + 3 + own[0] - place[0]
                yz = side * 9 + 4 + (own[1] - place[1]) * 3 + own[2] - place[2]
                k_high, k_low = split(lax.rsqrt(xtab_ref[x] + tab_ref[yz]))
                tops += [k_high, rest]
                lows += [k_low, rest]
                equivs.append(e_ref[pl.ds(pl.multiple_of(window * (2 * RHS), 2 * RHS), 2 * RHS), :])
            equiv = jnp.concatenate(equivs, axis=1)
            wide = wide + dot(equiv, jnp.concatenate(tops, axis=0))
            narrow = narrow + dot(equiv[:RHS], jnp.concatenate(lows, axis=0))
        acc = wide[:RHS] + wide[RHS:] + narrow
        high, low = split(acc)
        start = pl.multiple_of(g * RHS, RHS)
        dl_ref[0, pl.ds(start, RHS), :] = high
        dl_ref[1, pl.ds(start, RHS), :] = low
        return carry

    lax.fori_loop(0, LEAVES, one_leaf, 0)
    block = lax.broadcasted_iota(jnp.int32, (RHS, 256), 1) // SLOTS
    for half in range(2):
        lanes = slice(half * 256, half * 256 + 256)
        rows = slice(half * 8 * RHS, (half + 1) * 8 * RHS)
        local = (dl_ref[0, rows, :][:, :SUB], dl_ref[1, rows, :][:, :SUB])
        res = mm3(local, (w_ref[0, :, lanes], w_ref[1, :, lanes]))
        acc = out_ref[:, lanes]
        for g in range(8):
            acc = acc + jnp.where(block == g, res[g * RHS : (g + 1) * RHS], 0.0)
        out_ref[:, lanes] = acc


def tail_kernel(x_ref, base_ref, m_ref, out_ref):
    local = split(unpack(x_ref[...])[:, :SUB])
    out_ref[...] = base_ref[...] + mm3(local, (m_ref[0], m_ref[1]))


VM = pl.BlockSpec(memory_space=pltpu.VMEM)
SM = pl.BlockSpec(memory_space=pltpu.SMEM)
HB = pl.BlockSpec(memory_space=pltpu.HBM)


def call(kernel, name, outs, specs, scratch, vmem, *args, out_specs=None):
    return pl.pallas_call(
        kernel,
        name=name,
        out_shape=outs,
        in_specs=specs,
        out_specs=out_specs or jax.tree.map(lambda _: VM, outs),
        scratch_shapes=scratch,
        compiler_params=pltpu.CompilerParams(vmem_limit_bytes=vmem * 1024 * 1024),
        cost_estimate=pl.CostEstimate(flops=1000, bytes_accessed=1000, transcendentals=0),
    )(*args)


def in_hbm(x):
    return pltpu.with_memory_space_constraint(x, pltpu.HBM)


def tie(value, *others):
    return lax.optimization_barrier((value,) + others)[0]


def shards(offsets, charges, counts, near, far, upward, downward):
    col_np, row_np = sphere_tables()
    sds = jax.ShapeDtypeStruct
    pad = pltpu.VMEM((SUB, LANE), F32)
    flow = sds((2 * RHS, 128), F32)
    square = sds((TERMS, TERMS), F32)

    def tables(n):
        return pltpu.VMEM((n, SUB, LANE), F32)

    inputs = (offsets, charges, counts, upward, downward, jnp.asarray(col_np), jnp.asarray(row_np))
    equiv_rows = LEAVES * 2 * RHS
    dev_equiv, own, upward, downward, col, row, equiv = call(
        head_kernel, "leaf_and_device_equiv",
        (flow, sds((ROWS, POINTS), F32), square, square, sds((SUB, 128), F32), sds((8, LANE), F32), pltpu.HBM((equiv_rows, LANE), BF)),
        [HB] * 7,
        [
            pltpu.VMEM((3, POINTS), F32),
            pltpu.VMEM((RHS, POINTS), F32),
            pltpu.SMEM((LEAVES,), jnp.int32),
            pad,
            tables(10),
            pltpu.VMEM((equiv_rows, LANE), BF),
            pltpu.SemaphoreType.DMA((8,)),
        ],
        16, *map(in_hbm, inputs), out_specs=(VM, VM, VM, VM, VM, VM, HB),
    )
    swap = lax.ppermute(own, "inner", [(i, i ^ 1) for i in range(INNER)])
    cross = lax.ppermute(own, "inner", [(i, ((i + 1) ^ 1) - 1) for i in range(1, INNER - 1)])
    points = pltpu.VMEM((ROWS, POINTS), F32)
    spread = pltpu.VMEM((POINTS, 3 * POINTS), BF)
    side = [
        pltpu.VMEM((LEAVES, 12), jnp.int32),
        points,
        points,
        pad,
        points,
        points,
        pltpu.VMEM((LEAVES, 3 * POINTS), F32),
        spread,
        spread,
    ]
    dma = pltpu.SemaphoreType.DMA((3,))
    near = in_hbm(near)
    halo = pltpu.HBM((ROWS, POINTS), F32)
    early_base, early_sides, swap, cross = call(
        early_kernel, "early_near_field", (pltpu.HBM((RHS, POINTS), F32), pltpu.HBM((2 * HALF_E, LANE), BF), halo, halo),
        [VM, VM, VM, HB, VM, VM],
        [pltpu.VMEM((RHS, POINTS), F32), pltpu.VMEM((2 * HALF_E, LANE), BF), side[0], *side[3:], dma, dma],
        20, own, upward, col, near, swap, cross, out_specs=(HB, HB, HB, HB),
    )
    peers_equiv = lax.all_to_all(tie(dev_equiv, early_base, early_sides), "inner", 0, 0, tiled=True)
    leaf_maps = pltpu.HBM((2, SUB, POINTS), BF)
    up_maps, weights, evaluate = call(
        operator_kernel, "evaluation_and_group_maps", (sds((INNER, 2, SUB, LANE), BF), leaf_maps, leaf_maps),
        [VM, VM, VM, VM, VM],
        [pltpu.VMEM((2, SUB, POINTS), BF), pltpu.VMEM((2, SUB, POINTS), BF), pad, tables(14), pltpu.SemaphoreType.DMA((2,))],
        14, dev_equiv, own, downward, col, row, out_specs=(VM, HB, HB),
    )
    group_equiv = call(
        group_up_kernel, "group_equiv", pltpu.HBM((8 * OUTER, 128), F32), [VM, VM, VM],
        [pad, pltpu.VMEM((8 * OUTER, 128), F32), pltpu.SemaphoreType.DMA], 6,
        peers_equiv, up_maps, upward, out_specs=HB,
    )
    groups = lax.all_to_all(group_equiv, "outer", 0, 0, tiled=True)
    peers_part = call(
        peers_kernel, "device_to_device", sds((RHS, LANE), F32), [VM, VM, VM],
        [tables(12), pltpu.VMEM((4, 2, 3 * RHS, LANE), BF)], 10, peers_equiv, col, row,
    )
    groups = tie(groups, peers_part)
    local = call(
        local_kernel, "group_and_device_local", flow, [VM, VM, VM, VM, VM], [pad, tables(14)], 8,
        groups, peers_part, downward, col, row,
    )
    dev_local = lax.all_to_all(local, "inner", 0, 0, tiled=True)
    base, evaluate = call(
        field_kernel, "near_and_far_field", (sds((RHS, POINTS), F32), sds((2, SUB, POINTS), BF)),
        [SM, VM, VM, VM, VM, HB, HB, HB, HB, HB, HB, HB, HB],
        [
            pltpu.VMEM((3 * HALF_E, LANE), BF),
            pltpu.VMEM((2, LEAVES * RHS, LANE), BF),
            tables(21),
            tables(30),
            pltpu.VMEM((2, SUB, POINTS), BF),
            *side,
            dma,
            dma,
            dma,
        ],
        32, far, own, upward, col, row, near, *map(in_hbm, (swap, cross)),
        *map(in_hbm, (weights, evaluate, equiv, early_base, early_sides)),
    )
    return call(tail_kernel, "potential", sds((RHS, POINTS), F32), [VM, VM, VM], [], 4, dev_local, base, evaluate)


def solution(mesh):
    both = ("outer", "inner")
    in_specs = (P(None, both), P(None, both), P(both), P(both, None), P(both, None), P(), P())
    return jax.shard_map(shards, mesh=mesh, in_specs=in_specs, out_specs=P(None, both), check_vma=False)
```

```python
import functools

import jax
import jax.numpy as jnp
import numpy as np
from jax import lax
from jax.experimental import pallas as pl
from jax.experimental.pallas import tpu as pltpu
from jax.sharding import PartitionSpec as P

SOFTEN = 0.25
GOLDEN = 2.399963229728653
RHS = 64
TERMS = 165
SUB = 176
LANE = 256
LEAVES = 16
SLOTS = 32
POINTS = LEAVES * SLOTS
ROWS = 72
INNER = 16
OUTER = 32
PART = RHS // INNER
BF = jnp.bfloat16
F32 = jnp.float32


def sphere_tables():
    steps = np.arange(TERMS, dtype=np.float32)
    height = (np.float32(1.0) - (np.float32(2.0) * steps + np.float32(1.0)) / np.float32(TERMS)).astype(np.float32)
    radial = np.sqrt(np.maximum(np.float32(1.0) - height * height, np.float32(0.0))).astype(np.float32)
    angle = (steps * np.float32(GOLDEN)).astype(np.float32)
    dirs = np.stack([radial * np.cos(angle), radial * np.sin(angle), height]).astype(np.float32)
    col = np.zeros((SUB, 128), np.float32)
    col[:TERMS, :3] = dirs.T
    row = np.zeros((8, LANE), np.float32)
    row[:3, :TERMS] = dirs
    return col, row


def split(x):
    high = x.astype(BF)
    return high, (x - high.astype(F32)).astype(BF)


def dot(a, b):
    return jnp.dot(a, b, preferred_element_type=F32)


def dot_nt(a, b):
    return lax.dot_general(a, b, (((1,), (1,)), ((), ())), preferred_element_type=F32)


def mm3(a, b, f=dot):
    return f(a[0], b[0]) + f(a[1], b[0]) + f(a[0], b[1])


def columns(col_ref):
    return [jnp.broadcast_to(col_ref[:, c : c + 1], (SUB, 128)) for c in range(3)]


def two(x):
    return jnp.concatenate([x, x], axis=1)


def square_of(axis, shift, radius_t, radius_i, cols, row_ref):
    diff = (radius_t * row_ref[axis : axis + 1, :] + shift) - two(radius_i * cols[axis])
    return diff * diff


def box_kernels(xs, ys, zs, radius_t, radius_i, col_ref, row_ref, tab_ref):
    cols = columns(col_ref)
    for n, shift in enumerate(xs):
        tab_ref[n] = square_of(0, shift, radius_t, radius_i, cols, row_ref)
    zsq = len(xs)
    for n, shift in enumerate(zs):
        tab_ref[zsq + n] = square_of(2, shift, radius_t, radius_i, cols, row_ref) + SOFTEN
    start = zsq + len(zs)
    for b, shift in enumerate(ys):
        ysq = square_of(1, shift, radius_t, radius_i, cols, row_ref)
        for c in range(len(zs)):
            tab_ref[start + b * len(zs) + c] = ysq + tab_ref[zsq + c]
    for b in range(len(ys)):
        for c in range(len(zs)):
            for a in range(len(xs)):
                yield (a, b, c), lax.rsqrt(tab_ref[a] + tab_ref[start + b * len(zs) + c])


def bits(ids, low, axis, top=14):
    total = 0
    for level in range(5):
        place = 3 * level + axis
        if low <= place < top:
            total = total + (((ids >> place) & 1) << level)
    return total


def corner(leaf_id, low):
    return [bits(leaf_id, low, axis) for axis in range(3)]


def local_leaf(index):
    return ((index & 1) + ((index >> 3) & 1) * 2, (index >> 1) & 1, (index >> 2) & 1)


def peer_box(inner):
    return (((inner >> 2) & 1) * 4, (inner & 1) * 2 + ((inner >> 3) & 1) * 4, ((inner >> 1) & 1) * 2)


def leaf_kernel(offs, col_ref):
    total = SOFTEN
    for c in range(3):
        col = jnp.broadcast_to(col_ref[:, c : c + 1], (SUB, 128)) * 1.8
        diff = jnp.concatenate([col] * (POINTS // 128), axis=1) - offs[c : c + 1, :]
        total = total + diff * diff
    return lax.rsqrt(total)


def padded(map_ref, pad_ref, scale):
    pad_ref[...] = jnp.zeros_like(pad_ref)
    pad_ref[0:TERMS, 0:TERMS] = map_ref[...] * scale
    return split(pad_ref[...])


def leaf_equivalents(charges, kern, up):
    block = lax.broadcasted_iota(jnp.int32, (RHS, 256), 1) // SLOTS
    keep = [(block == g).astype(F32).astype(BF) for g in range(8)]
    pieces = split(charges)
    out = []
    for half in range(2):
        lanes = slice(half * 256, half * 256 + 256)
        spread = [jnp.concatenate([piece[:, lanes] * keep[g] for g in range(8)], axis=0) for piece in pieces]
        high, low = kern[0][:, lanes], kern[1][:, lanes]
        spread = jnp.concatenate([spread[0], spread[1], spread[0]], axis=1)
        check = dot_nt(spread, jnp.concatenate([high, high, low], axis=1))
        out.append(mm3(split(check), up))
    return out


def store_equivalents(halves, e_ref, first):
    for half in range(2):
        e_high, e_low = split(halves[half])
        for g in range(8):
            start = first + (half * 8 + g) * 2 * RHS
            e_ref[start : start + RHS, :] = e_high[g * RHS : g * RHS + RHS]
            e_ref[start + RHS : start + 2 * RHS, :] = e_low[g * RHS : g * RHS + RHS]


def pack(rows):
    low, high = rows[:, :128], rows[:, 128:]
    n = rows.shape[0]
    top = lax.broadcasted_iota(jnp.int32, (n, 128), 0) % 8 < 4
    first = jnp.where(top, low, pltpu.roll(high, 4, 0))
    second = jnp.where(top, pltpu.roll(low, n - 4, 0), high)
    tiles = []
    for m in range(n // 8):
        tiles += [first[8 * m : 8 * m + 8], second[8 * m : 8 * m + 8]]
    return jnp.concatenate(tiles, axis=0)


def unpack(tiles):
    n = tiles.shape[0] // 2
    first = jnp.concatenate([tiles[16 * m : 16 * m + 8] for m in range(n // 8)], axis=0)
    second = jnp.concatenate([tiles[16 * m + 8 : 16 * m + 16] for m in range(n // 8)], axis=0)
    top = lax.broadcasted_iota(jnp.int32, (n, 128), 0) % 8 < 4
    low = jnp.where(top, first, pltpu.roll(second, 4, 0))
    high = jnp.where(top, pltpu.roll(first, n - 4, 0), second)
    return jnp.concatenate([low, high], axis=1)


def tile_dot(tile, high, low, acc):
    a_high, a_low = split(tile)
    both = jnp.concatenate([a_high, a_low], axis=0)
    rest = SUB - 128
    front = dot(both, high[:128]) + dot(both, low[:128])
    back = dot(both[:, :rest], high[128:]) + dot(both[:, :rest], low[128:])
    return acc[0] + front, acc[1] + back


def tile_sum(acc):
    front = acc[0][:8] + acc[0][8:]
    back = acc[1][:8] + acc[1][8:]
    return front + pltpu.roll(back, 4, 0)


def head_kernel(
    off_hbm, q_hbm, counts_hbm, up_hbm, down_hbm, col_hbm, row_hbm,
    out_ref, halo_ref, up_ref, down_ref, col_ref, row_ref, e_hbm,
    off_ref, q_ref, counts_ref, pad_ref, tab_ref, e_ref, sems,
):
    moves = [
        pltpu.make_async_copy(src, dst, sems.at[n])
        for n, (src, dst) in enumerate(
            (
                (q_hbm, q_ref),
                (off_hbm, off_ref),
                (counts_hbm, counts_ref),
                (up_hbm, up_ref),
                (col_hbm, col_ref),
                (row_hbm, row_ref),
                (down_hbm, down_ref),
            )
        )
    ]
    for move in moves:
        move.start()
    for move in moves[:-1]:
        move.wait()
    lane = lax.broadcasted_iota(jnp.int32, (8, POINTS), 1)
    limit = jnp.zeros((8, POINTS), jnp.int32)
    for g in range(LEAVES):
        limit = jnp.where(lane // SLOTS == g, counts_ref[g], limit)
    filled = (lane % SLOTS < limit)[0:1]
    charges = jnp.where(filled, q_ref[...], 0.0)
    halo_ref[0:RHS, :] = charges
    halo_ref[RHS:ROWS, :] = jnp.zeros((ROWS - RHS, POINTS), F32)
    halo_ref[RHS : RHS + 3, :] = off_ref[...]
    kern = split(leaf_kernel(off_ref[...], col_ref))
    up = padded(up_ref, pad_ref, 18.0 / TERMS)
    up = (up[0][:, :], up[1][:, :])
    halves = leaf_equivalents(charges, kern, up)
    store_equivalents(halves, e_ref, 0)
    e_move = pltpu.make_async_copy(e_ref, e_hbm, sems.at[7])
    e_move.start()
    acc = jnp.zeros((RHS, LANE), F32)
    for (x, y, z), kern in box_kernels(
        (1.5, 0.5, -0.5, -1.5), (0.5, -0.5), (0.5, -0.5), 6.0, 0.9, col_ref, row_ref, tab_ref
    ):
        start = ((x >> 1) * 8 + (x & 1) + 2 * y + 4 * z) * 2 * RHS
        high, low = split(kern)
        wide = dot(e_ref[start : start + 2 * RHS, :][:, :SUB], high)
        acc = acc + wide[:RHS] + wide[RHS:] + dot(e_ref[start : start + RHS, :][:, :SUB], low)
    up60 = padded(up_ref, pad_ref, 60.0 / TERMS)
    out_ref[...] = pack(mm3(split(acc[:, :SUB]), up60))
    moves[-1].wait()
    e_move.wait()


def group_up_kernel(x_ref, maps_ref, up_ref, out_hbm, pad_ref, out_ref, sem):
    acc = (jnp.zeros((16, LANE), F32), jnp.zeros((16, LANE), F32))
    for e in range(INNER):
        acc = tile_dot(x_ref[8 * e : 8 * e + 8, :], maps_ref[e, 0], maps_ref[e, 1], acc)
    check = tile_sum(acc)
    both = jnp.concatenate([check, check], axis=0)
    equiv = mm3(split(both[:, :SUB]), padded(up_ref, pad_ref, 200.0 / TERMS))[:8]
    top = lax.broadcasted_iota(jnp.int32, (8, 128), 0) < 4
    tile = jnp.where(top, equiv[:, :128], pltpu.roll(equiv[:, 128:], 4, 0))
    for p in range(OUTER):
        out_ref[8 * p : 8 * p + 8, :] = tile
    move = pltpu.make_async_copy(out_ref, out_hbm, sem)
    move.start()
    move.wait()


def box_order(rows):
    return jnp.concatenate(
        [rows[8 * k : 8 * k + 8] for k in (y * 4 + x * 2 + z for x in (0, 1) for z in (0, 1) for y in (0, 1))], axis=0
    )


def index_order(rows):
    return jnp.concatenate(
        [rows[8 * k : 8 * k + 8] for k in (x * 4 + z * 2 + y for y in (0, 1) for x in (0, 1) for z in (0, 1))], axis=0
    )


def peers_kernel(x_ref, col_ref, row_ref, out_ref, tab_ref, shifted_ref):
    equiv = jnp.concatenate([box_order(unpack(x_ref[...])), jnp.zeros((16, LANE), F32)], axis=0)
    shifted_ref[...] = jnp.zeros_like(shifted_ref)
    for q in range(4):
        high, low = split(pltpu.roll(equiv, 4 * q, 0) if q else equiv)
        shifted_ref[q, 0, RHS : RHS + 80, :] = high
        shifted_ref[q, 1, RHS : RHS + 80, :] = low
    cols = columns(col_ref)
    for dy in range(-3, 4):
        tab_ref[dy + 3] = square_of(1, 2.0 * dy, 3.0, 3.0, cols, row_ref) + SOFTEN
    row = lax.broadcasted_iota(jnp.int32, (RHS, 128), 0)
    lane = lax.broadcasted_iota(jnp.int32, (RHS, 128), 1)
    px, pz, py = row >> 5, (row >> 4) & 1, (row >> 2) & 3
    dest = (py & 1) + pz * 2 + px * 4 + (py >> 1) * 8

    def valid(dx, dz):
        sx, sy, sz = px - dx, py - (lane - 3), pz - dz
        inside = (sx >= 0) & (sx < 2) & (sy >= 0) & (sy < 4) & (sz >= 0) & (sz < 2)
        source = (sy & 1) + sz * 2 + sx * 4 + (sy >> 1) * 8
        return (inside & (jnp.abs(source - dest) >= 2)).astype(F32)

    def moved(dx, dy, dz, mask):
        q = dy % 4
        start = RHS - (dx * 2 + dz) * 16 - 4 * (dy - q)
        keep = two(jnp.broadcast_to(mask[:, dy + 3 : dy + 4], (RHS, 128))).astype(BF)
        rows = [(shifted_ref[q, n, start : start + RHS, :] * keep)[:, :SUB] for n in range(2)]
        return jnp.concatenate(rows, axis=0)

    def add(acc, rows, kern, f):
        return acc[0] + f(rows, kern[0]), acc[1] + f(rows[:RHS], kern[1])

    def fold(acc):
        return acc[0][:RHS] + acc[0][RHS:] + acc[1]

    ahead_sum = (jnp.zeros((2 * RHS, LANE), F32), jnp.zeros((RHS, LANE), F32))
    behind_sum = (jnp.zeros((2 * RHS, SUB), F32), jnp.zeros((RHS, SUB), F32))
    planes = [(0, 0, (1, 2, 3))] + [(dx, dz, range(-3, 4)) for dx, dz in ((0, 1), (1, -1), (1, 0), (1, 1))]
    for n, (dx, dz, steps) in enumerate(planes):
        plane = square_of(0, dx * 4.0, 3.0, 3.0, cols, row_ref)
        tab_ref[7 + n] = plane + square_of(2, dz * 2.0, 3.0, 3.0, cols, row_ref)
        ahead, behind = valid(dx, dz), valid(-dx, -dz)
        for dy in steps:
            kern = split(lax.rsqrt(tab_ref[7 + n] + tab_ref[dy + 3]))
            ahead_sum = add(ahead_sum, moved(dx, dy, dz, ahead), kern, dot)
            kern = (kern[0][:, :SUB], kern[1][:, :SUB])
            behind_sum = add(behind_sum, moved(-dx, -dy, -dz, behind), kern, dot_nt)
    back = jnp.concatenate([fold(behind_sum), jnp.zeros((RHS, LANE - SUB), F32)], axis=1)
    out_ref[...] = index_order(fold(ahead_sum) + back)


def local_kernel(x_ref, peers_ref, down_ref, col_ref, row_ref, out_ref, pad_ref, tab_ref):
    outer = lax.axis_index("outer")
    own = [p.astype(F32) for p in corner(outer * 256, 8)]
    cols = columns(col_ref)
    for n in range(4):
        tab_ref[n] = square_of(2, own[2] - 4.0 * n, 10.0, 20.0, cols, row_ref) + SOFTEN
    for x in range(4):
        xsq = square_of(0, own[0] - 8.0 * x, 10.0, 20.0, cols, row_ref)
        for y in range(2):
            tab_ref[4 + x * 2 + y] = xsq + square_of(1, own[1] - 8.0 * y, 10.0, 20.0, cols, row_ref)
    acc = (jnp.zeros((16, LANE), F32), jnp.zeros((16, LANE), F32))
    for p in range(OUTER):
        z, x, y = (p & 1) + ((p >> 3) & 1) * 2, ((p >> 1) & 1) + ((p >> 4) & 1) * 2, (p >> 2) & 1
        weight = (jnp.abs(p - outer) >= 2).astype(F32)
        kern = split(lax.rsqrt(tab_ref[4 + x * 2 + y] + tab_ref[z]))
        acc = tile_dot(x_ref[8 * p : 8 * p + 8, :] * weight, kern[0], kern[1], acc)
    check = tile_sum(acc)
    both = jnp.concatenate([check, check], axis=0)
    group = mm3(split(both[:, :SUB]), padded(down_ref, pad_ref, 200.0 / TERMS))[:8]
    pieces = jnp.concatenate(split(group[:, :SUB]), axis=0)
    top = lax.broadcasted_iota(jnp.int32, (8, LANE), 0) < 4
    found = [None] * INNER
    for (x, y, z), kern in box_kernels(
        (-2.0, 2.0), (-3.0, -1.0, 1.0, 3.0), (-1.0, 1.0), 3.0, 20.0, col_ref, row_ref, tab_ref
    ):
        high, low = split(kern)
        part = dot(pieces, high) + dot(pieces, low)
        found[(y & 1) + z * 2 + x * 4 + (y >> 1) * 8] = part[:8] + part[8:]
    merged = [jnp.where(top, found[2 * m], pltpu.roll(found[2 * m + 1], 4, 0)) for m in range(INNER // 2)]
    total = jnp.concatenate(merged, axis=0) + peers_ref[...]
    out_ref[...] = pack(mm3(split(total[:, :SUB]), padded(down_ref, pad_ref, 60.0 / TERMS)))


def operator_kernel(
    flow_ref, off_ref, down_ref, col_ref, row_ref, up_ref, w_hbm, m_hbm, w_ref, m_ref, pad_ref, tab_ref, sems
):
    for (x, y, z), kern in box_kernels(
        (2.0, -2.0), (3.0, 1.0, -1.0, -3.0), (1.0, -1.0), 20.0, 3.0, col_ref, row_ref, tab_ref
    ):
        e = (y & 1) + z * 2 + x * 4 + (y >> 1) * 8
        high, low = split(kern)
        up_ref[e, 0, :, :] = high
        up_ref[e, 1, :, :] = low
    kern = split(leaf_kernel(off_ref[RHS : RHS + 3, :], col_ref))
    down = padded(down_ref, pad_ref, 18.0 / TERMS)
    down = (down[0][:, :SUB], down[1][:, :SUB])
    weights = split(mm3(down, kern))
    w_ref[0, :, :] = weights[0]
    w_ref[1, :, :] = weights[1]
    w_move = pltpu.make_async_copy(w_ref, w_hbm, sems.at[0])
    w_move.start()
    block = lax.broadcasted_iota(jnp.int32, (SUB, 256), 1) // SLOTS
    found = [jnp.zeros((SUB, 256), F32)] * 2
    for (x, y, z), kern in box_kernels(
        (-1.5, -0.5, 0.5, 1.5), (-0.5, 0.5), (-0.5, 0.5), 0.9, 6.0, col_ref, row_ref, tab_ref
    ):
        half, g = (x >> 1), (x & 1) + 2 * y + 4 * z
        lanes = slice(half * 256, half * 256 + 256)
        own = (weights[0][:, lanes], weights[1][:, lanes])
        found[half] = jnp.where(block == g, mm3(split(kern[:, :SUB]), own), found[half])
    for half in range(2):
        lanes = slice(half * 256, half * 256 + 256)
        m_high, m_low = split(found[half])
        m_ref[0, :, lanes] = m_high
        m_ref[1, :, lanes] = m_low
    m_move = pltpu.make_async_copy(m_ref, m_hbm, sems.at[1])
    m_move.start()
    w_move.wait()
    m_move.wait()


def near_field(near_ref, left_ref, own_ref, right_ref, out_ref, mask_ref, high_ref, low_ref):
    offs = jnp.concatenate([own_ref[RHS:ROWS, :], jnp.zeros((120, POINTS), F32)], axis=0).T
    inner = lax.axis_index("inner")
    device = lax.axis_index("outer") * INNER + inner
    base = (device - 1) * LEAVES
    total = 3 * POINTS
    lane = lax.broadcasted_iota(jnp.int32, (LEAVES, total), 1) // SLOTS
    found = jnp.full((LEAVES, total), jnp.inf, F32)
    near = near_ref[...] - base
    for k in range(12):
        found = jnp.where(lane == near[:, k : k + 1], SOFTEN, found)
    leaf = lax.broadcasted_iota(jnp.int32, (1, POINTS), 1) // SLOTS
    within = local_leaf(leaf)
    own_box = corner(device * LEAVES, 4)
    sources = []
    for c in range(3):
        lanes = []
        for side, ref in ((-1, left_ref), (0, own_ref), (1, right_ref)):
            box = corner((device + side) * LEAVES, 4)[c] - own_box[c]
            lanes.append(ref[RHS + c : RHS + c + 1, :] + (box + within[c]).astype(F32))
        sources.append(jnp.concatenate(lanes, axis=1))
    norms = sources[0] * sources[0] + sources[1] * sources[1] + sources[2] * sources[2]
    mask_ref[...] = found + norms
    for g in range(LEAVES):
        rows = slice(g * SLOTS, g * SLOTS + SLOTS)
        place = local_leaf(g)
        target = [offs[rows, c : c + 1] + float(place[c]) for c in range(3)]
        dist = mask_ref[g : g + 1, :] + (target[0] * target[0] + target[1] * target[1] + target[2] * target[2])
        for c in range(3):
            dist = dist + (-2.0 * target[c]) * sources[c]
        k_high, k_low = split(lax.rsqrt(dist))
        high_ref[rows, :] = k_high
        low_ref[rows, :] = k_low
    charges = jnp.concatenate([r[0:RHS, :] for r in (left_ref, own_ref, right_ref)], axis=1)
    q_high, q_low = split(charges)
    both = jnp.concatenate([q_high, q_low], axis=0)
    res = dot_nt(high_ref[...], both)
    res = res + jnp.concatenate([dot_nt(low_ref[...], q_high), jnp.zeros((POINTS, RHS), F32)], axis=1)
    flipped = res.T
    out_ref[...] = flipped[:RHS] + flipped[RHS:]


def field_kernel(
    far_ref, near_ref, own_ref, swap_ref, cross_ref, up_ref, col_ref, row_ref, w_hbm, m_hbm, e_hbm, out_ref, m_ref,
    pad_ref, e_ref, dl_ref, xtab_ref, tab_ref, w_ref, left_ref, right_ref, mask_ref, high_ref, low_ref, sems,
):
    middle = LEAVES * 2 * RHS
    moves = [
        pltpu.make_async_copy(e_hbm, e_ref.at[middle : 2 * middle], sems.at[0]),
        pltpu.make_async_copy(w_hbm, w_ref, sems.at[1]),
        pltpu.make_async_copy(m_hbm, m_ref, sems.at[2]),
    ]
    for move in moves:
        move.start()
    odd = lax.rem(lax.axis_index("inner"), 2) == 1
    left_ref[...] = jnp.where(odd, swap_ref[...], cross_ref[...])
    right_ref[...] = jnp.where(odd, cross_ref[...], swap_ref[...])
    near_field(near_ref, left_ref, own_ref, right_ref, out_ref, mask_ref, high_ref, low_ref)
    inner = lax.axis_index("inner")
    device = lax.axis_index("outer") * INNER + inner
    up = padded(up_ref, pad_ref, 18.0 / TERMS)
    for side, ref in ((0, left_ref), (2, right_ref)):
        kern = split(leaf_kernel(ref[RHS : RHS + 3, :], col_ref))
        store_equivalents(leaf_equivalents(ref[0:RHS, :], kern, up), e_ref, side * middle)
    for move in moves:
        move.wait()
    first = (device - 1) * LEAVES
    boxes = [corner((device + side) * LEAVES, 4) for side in (-1, 0, 1)]
    boxes = [[(boxes[1][c] - box[c]).astype(F32) for c in range(3)] for box in boxes]
    cols = columns(col_ref)
    for side in range(3):
        for n in range(7):
            xtab_ref[side * 7 + n] = square_of(0, boxes[side][0] + (n - 3.0), 0.9, 1.8, cols, row_ref)
        for c in range(3):
            tab_ref[27 + c] = square_of(2, boxes[side][2] + (c - 1.0), 0.9, 1.8, cols, row_ref) + SOFTEN
        for b in range(3):
            ysq = square_of(1, boxes[side][1] + (b - 1.0), 0.9, 1.8, cols, row_ref)
            for c in range(3):
                tab_ref[side * 9 + b * 3 + c] = ysq + tab_ref[27 + c]

    def one_leaf(g, carry):
        own = local_leaf(g)
        wide = jnp.zeros((2 * RHS, LANE), F32)
        narrow = jnp.zeros((RHS, LANE), F32)
        rest = jnp.zeros((LANE - SUB, LANE), BF)
        for k in range(0, 12, 4):
            tops, lows, equivs = [], [], []
            for n in range(k, k + 4):
                window = far_ref[g, n] - first
                side = window >> 4
                place = local_leaf(window & 15)
                x = side * 7 + 3 + own[0] - place[0]
                yz = side * 9 + 4 + (own[1] - place[1]) * 3 + own[2] - place[2]
                k_high, k_low = split(lax.rsqrt(xtab_ref[x] + tab_ref[yz]))
                tops += [k_high, rest]
                lows += [k_low, rest]
                equivs.append(e_ref[pl.ds(pl.multiple_of(window * (2 * RHS), 2 * RHS), 2 * RHS), :])
            equiv = jnp.concatenate(equivs, axis=1)
            wide = wide + dot(equiv, jnp.concatenate(tops, axis=0))
            narrow = narrow + dot(equiv[:RHS], jnp.concatenate(lows, axis=0))
        acc = wide[:RHS] + wide[RHS:] + narrow
        high, low = split(acc)
        start = pl.multiple_of(g * RHS, RHS)
        dl_ref[0, pl.ds(start, RHS), :] = high
        dl_ref[1, pl.ds(start, RHS), :] = low
        return carry

    lax.fori_loop(0, LEAVES, one_leaf, 0)
    block = lax.broadcasted_iota(jnp.int32, (RHS, 256), 1) // SLOTS
    for half in range(2):
        lanes = slice(half * 256, half * 256 + 256)
        rows = slice(half * 8 * RHS, (half + 1) * 8 * RHS)
        local = (dl_ref[0, rows, :][:, :SUB], dl_ref[1, rows, :][:, :SUB])
        res = mm3(local, (w_ref[0, :, lanes], w_ref[1, :, lanes]))
        acc = out_ref[:, lanes]
        for g in range(8):
            acc = acc + jnp.where(block == g, res[g * RHS : (g + 1) * RHS], 0.0)
        out_ref[:, lanes] = acc


def tail_kernel(x_ref, base_ref, m_ref, out_ref):
    high, low = split(unpack(x_ref[...])[:, :SUB])
    wide = dot(jnp.concatenate([high, low], axis=0), m_ref[0])
    out_ref[...] = base_ref[...] + wide[:RHS] + wide[RHS:] + dot(high, m_ref[1])


VM = pl.BlockSpec(memory_space=pltpu.VMEM)
SM = pl.BlockSpec(memory_space=pltpu.SMEM)
HB = pl.BlockSpec(memory_space=pltpu.HBM)


def call(kernel, name, outs, specs, scratch, vmem, *args, out_specs=None):
    return pl.pallas_call(
        kernel,
        name=name,
        out_shape=outs,
        in_specs=specs,
        out_specs=out_specs or jax.tree.map(lambda _: VM, outs),
        scratch_shapes=scratch,
        compiler_params=pltpu.CompilerParams(vmem_limit_bytes=vmem * 1024 * 1024),
        cost_estimate=pl.CostEstimate(flops=1000, bytes_accessed=1000, transcendentals=0),
    )(*args)


def in_hbm(x):
    return pltpu.with_memory_space_constraint(x, pltpu.HBM)


def tie(value, *others):
    return lax.optimization_barrier((value,) + others)[0]


def shards(offsets, charges, counts, near, far, upward, downward):
    col_np, row_np = sphere_tables()
    sds = jax.ShapeDtypeStruct
    pad = pltpu.VMEM((SUB, LANE), F32)
    flow = sds((2 * RHS, 128), F32)
    square = sds((TERMS, TERMS), F32)

    def tables(n):
        return pltpu.VMEM((n, SUB, LANE), F32)

    inputs = (offsets, charges, counts, upward, downward, jnp.asarray(col_np), jnp.asarray(row_np))
    equiv_rows = LEAVES * 2 * RHS
    dev_equiv, own, upward, downward, col, row, equiv = call(
        head_kernel, "leaf_and_device_equiv",
        (flow, sds((ROWS, POINTS), F32), square, square, sds((SUB, 128), F32), sds((8, LANE), F32), pltpu.HBM((equiv_rows, LANE), BF)),
        [HB] * 7,
        [
            pltpu.VMEM((3, POINTS), F32),
            pltpu.VMEM((RHS, POINTS), F32),
            pltpu.SMEM((LEAVES,), jnp.int32),
            pad,
            tables(10),
            pltpu.VMEM((equiv_rows, LANE), BF),
            pltpu.SemaphoreType.DMA((8,)),
        ],
        16, *map(in_hbm, inputs), out_specs=(VM, VM, VM, VM, VM, VM, HB),
    )
    peers_equiv = lax.all_to_all(dev_equiv, "inner", 0, 0, tiled=True)
    leaf_maps = pltpu.HBM((2, SUB, POINTS), BF)
    up_maps, weights, evaluate = call(
        operator_kernel, "evaluation_and_group_maps", (sds((INNER, 2, SUB, LANE), BF), leaf_maps, leaf_maps),
        [VM, VM, VM, VM, VM],
        [pltpu.VMEM((2, SUB, POINTS), BF), pltpu.VMEM((2, SUB, POINTS), BF), pad, tables(14), pltpu.SemaphoreType.DMA((2,))],
        14, dev_equiv, own, downward, col, row, out_specs=(VM, HB, HB),
    )
    swap = lax.ppermute(own, "inner", [(i, i ^ 1) for i in range(INNER)])
    cross = lax.ppermute(own, "inner", [(i, ((i + 1) ^ 1) - 1) for i in range(1, INNER - 1)])
    group_equiv = call(
        group_up_kernel, "group_equiv", pltpu.HBM((8 * OUTER, 128), F32), [VM, VM, VM],
        [pad, pltpu.VMEM((8 * OUTER, 128), F32), pltpu.SemaphoreType.DMA], 6,
        peers_equiv, up_maps, upward, out_specs=HB,
    )
    groups = lax.all_to_all(group_equiv, "outer", 0, 0, tiled=True)
    peers_part = call(
        peers_kernel, "device_to_device", sds((RHS, LANE), F32), [VM, VM, VM],
        [tables(12), pltpu.VMEM((4, 2, 3 * RHS, LANE), BF)], 10, peers_equiv, col, row,
    )
    groups = tie(groups, peers_part)
    local = call(
        local_kernel, "group_and_device_local", flow, [VM, VM, VM, VM, VM], [pad, tables(14)], 8,
        groups, peers_part, downward, col, row,
    )
    dev_local = lax.all_to_all(local, "inner", 0, 0, tiled=True)
    base, evaluate = call(
        field_kernel, "near_and_far_field", (sds((RHS, POINTS), F32), sds((2, SUB, POINTS), BF)),
        [SM, VM, VM, VM, VM, VM, VM, VM, HB, HB, HB],
        [
            pad,
            pltpu.VMEM((3 * LEAVES * 2 * RHS, LANE), BF),
            pltpu.VMEM((2, LEAVES * RHS, LANE), BF),
            tables(21),
            tables(30),
            pltpu.VMEM((2, SUB, POINTS), BF),
            pltpu.VMEM((ROWS, POINTS), F32),
            pltpu.VMEM((ROWS, POINTS), F32),
            pltpu.VMEM((LEAVES, 3 * POINTS), F32),
            pltpu.VMEM((POINTS, 3 * POINTS), BF),
            pltpu.VMEM((POINTS, 3 * POINTS), BF),
            pltpu.SemaphoreType.DMA((3,)),
        ],
        32, far, near, own, swap, cross, upward, col, row, in_hbm(weights), in_hbm(evaluate), in_hbm(equiv),
    )
    return call(tail_kernel, "potential", sds((RHS, POINTS), F32), [VM, VM, VM], [], 4, dev_local, base, evaluate)


def solution(mesh):
    both = ("outer", "inner")
    in_specs = (P(None, both), P(None, both), P(both), P(both, None), P(both, None), P(), P())
    return jax.shard_map(shards, mesh=mesh, in_specs=in_specs, out_specs=P(None, both), check_vma=False)
```

```python
import functools

import jax
import jax.numpy as jnp
import numpy as np
from jax import lax
from jax.experimental import pallas as pl
from jax.experimental.pallas import tpu as pltpu
from jax.sharding import PartitionSpec as P

SOFTEN = 0.25
GOLDEN = 2.399963229728653
RHS = 64
TERMS = 165
SUB = 176
LANE = 256
LEAVES = 16
SLOTS = 32
POINTS = LEAVES * SLOTS
ROWS = 72
INNER = 16
OUTER = 32
PART = RHS // INNER
BF = jnp.bfloat16
F32 = jnp.float32


def sphere_tables():
    steps = np.arange(TERMS, dtype=np.float32)
    height = (np.float32(1.0) - (np.float32(2.0) * steps + np.float32(1.0)) / np.float32(TERMS)).astype(np.float32)
    radial = np.sqrt(np.maximum(np.float32(1.0) - height * height, np.float32(0.0))).astype(np.float32)
    angle = (steps * np.float32(GOLDEN)).astype(np.float32)
    dirs = np.stack([radial * np.cos(angle), radial * np.sin(angle), height]).astype(np.float32)
    col = np.zeros((SUB, 128), np.float32)
    col[:TERMS, :3] = dirs.T
    row = np.zeros((8, LANE), np.float32)
    row[:3, :TERMS] = dirs
    return col, row


def split(x):
    high = x.astype(BF)
    return high, (x - high.astype(F32)).astype(BF)


def dot(a, b):
    return jnp.dot(a, b, preferred_element_type=F32)


def dot_nt(a, b):
    return lax.dot_general(a, b, (((1,), (1,)), ((), ())), preferred_element_type=F32)


def mm3(a, b, f=dot):
    return f(a[0], b[0]) + f(a[1], b[0]) + f(a[0], b[1])


def columns(col_ref):
    return [jnp.broadcast_to(col_ref[:, c : c + 1], (SUB, 128)) for c in range(3)]


def two(x):
    return jnp.concatenate([x, x], axis=1)


def square_of(axis, shift, radius_t, radius_i, cols, row_ref):
    diff = (radius_t * row_ref[axis : axis + 1, :] + shift) - two(radius_i * cols[axis])
    return diff * diff


def box_tables(xs, ys, zs, radius_t, radius_i, col_ref, row_ref, tab_ref):
    cols = columns(col_ref)
    for n, shift in enumerate(xs):
        tab_ref[n] = square_of(0, shift, radius_t, radius_i, cols, row_ref)
    zsq = len(xs)
    for n, shift in enumerate(zs):
        tab_ref[zsq + n] = square_of(2, shift, radius_t, radius_i, cols, row_ref) + SOFTEN
    start = zsq + len(zs)
    for b, shift in enumerate(ys):
        ysq = square_of(1, shift, radius_t, radius_i, cols, row_ref)
        for c in range(len(zs)):
            tab_ref[start + b * len(zs) + c] = ysq + tab_ref[zsq + c]


def box_pairs(nx, ny, nz, tab_ref):
    for b in range(ny):
        for c in range(nz):
            for a in range(nx):
                yield (a, b, c), lax.rsqrt(tab_ref[a] + tab_ref[nx + nz + b * nz + c])


def box_kernels(xs, ys, zs, radius_t, radius_i, col_ref, row_ref, tab_ref):
    box_tables(xs, ys, zs, radius_t, radius_i, col_ref, row_ref, tab_ref)
    yield from box_pairs(len(xs), len(ys), len(zs), tab_ref)


def bits(ids, low, axis, top=14):
    total = 0
    for level in range(5):
        place = 3 * level + axis
        if low <= place < top:
            total = total + (((ids >> place) & 1) << level)
    return total


def corner(leaf_id, low):
    return [bits(leaf_id, low, axis) for axis in range(3)]


def local_leaf(index):
    return ((index & 1) + ((index >> 3) & 1) * 2, (index >> 1) & 1, (index >> 2) & 1)


def peer_box(inner):
    return (((inner >> 2) & 1) * 4, (inner & 1) * 2 + ((inner >> 3) & 1) * 4, ((inner >> 1) & 1) * 2)


def leaf_kernel(offs, col_ref):
    total = SOFTEN
    for c in range(3):
        col = jnp.broadcast_to(col_ref[:, c : c + 1], (SUB, 128)) * 1.8
        diff = jnp.concatenate([col] * (POINTS // 128), axis=1) - offs[c : c + 1, :]
        total = total + diff * diff
    return lax.rsqrt(total)


def padded(map_ref, pad_ref, scale):
    pad_ref[...] = jnp.zeros_like(pad_ref)
    pad_ref[0:TERMS, 0:TERMS] = map_ref[...] * scale
    return split(pad_ref[...])


def leaf_equivalents(charges, kern, up):
    block = lax.broadcasted_iota(jnp.int32, (RHS, 256), 1) // SLOTS
    keep = [(block == g).astype(F32).astype(BF) for g in range(8)]
    pieces = split(charges)
    out = []
    for half in range(2):
        lanes = slice(half * 256, half * 256 + 256)
        spread = [jnp.concatenate([piece[:, lanes] * keep[g] for g in range(8)], axis=0) for piece in pieces]
        high, low = kern[0][:, lanes], kern[1][:, lanes]
        spread = jnp.concatenate([spread[0], spread[1], spread[0]], axis=1)
        check = dot_nt(spread, jnp.concatenate([high, high, low], axis=1))
        out.append(mm3(split(check), up))
    return out


def store_equivalents(halves, e_ref, first):
    for half in range(2):
        e_high, e_low = split(halves[half])
        for g in range(8):
            start = first + (half * 8 + g) * 2 * RHS
            e_ref[start : start + RHS, :] = e_high[g * RHS : g * RHS + RHS]
            e_ref[start + RHS : start + 2 * RHS, :] = e_low[g * RHS : g * RHS + RHS]


def pack(rows):
    low, high = rows[:, :128], rows[:, 128:]
    n = rows.shape[0]
    top = lax.broadcasted_iota(jnp.int32, (n, 128), 0) % 8 < 4
    first = jnp.where(top, low, pltpu.roll(high, 4, 0))
    second = jnp.where(top, pltpu.roll(low, n - 4, 0), high)
    tiles = []
    for m in range(n // 8):
        tiles += [first[8 * m : 8 * m + 8], second[8 * m : 8 * m + 8]]
    return jnp.concatenate(tiles, axis=0)


def unpack(tiles):
    n = tiles.shape[0] // 2
    first = jnp.concatenate([tiles[16 * m : 16 * m + 8] for m in range(n // 8)], axis=0)
    second = jnp.concatenate([tiles[16 * m + 8 : 16 * m + 16] for m in range(n // 8)], axis=0)
    top = lax.broadcasted_iota(jnp.int32, (n, 128), 0) % 8 < 4
    low = jnp.where(top, first, pltpu.roll(second, 4, 0))
    high = jnp.where(top, pltpu.roll(first, n - 4, 0), second)
    return jnp.concatenate([low, high], axis=1)


def tile_dot(tile, high, low, acc):
    a_high, a_low = split(tile)
    both = jnp.concatenate([a_high, a_low], axis=0)
    rest = SUB - 128
    front = dot(both, high[:128]) + dot(both, low[:128])
    back = dot(both[:, :rest], high[128:]) + dot(both[:, :rest], low[128:])
    return acc[0] + front, acc[1] + back


def tile_sum(acc):
    front = acc[0][:8] + acc[0][8:]
    back = acc[1][:8] + acc[1][8:]
    return front + pltpu.roll(back, 4, 0)


def head_kernel(
    off_hbm, q_hbm, counts_hbm, up_hbm, down_hbm, col_hbm, row_hbm,
    out_ref, halo_ref, up_ref, down_ref, col_ref, row_ref, e_hbm,
    off_ref, q_ref, counts_ref, pad_ref, tab_ref, e_ref, sems,
):
    moves = [
        pltpu.make_async_copy(src, dst, sems.at[n])
        for n, (src, dst) in enumerate(
            (
                (q_hbm, q_ref),
                (off_hbm, off_ref),
                (counts_hbm, counts_ref),
                (up_hbm, up_ref),
                (col_hbm, col_ref),
                (row_hbm, row_ref),
                (down_hbm, down_ref),
            )
        )
    ]
    for move in moves:
        move.start()
    moves[4].wait()
    moves[5].wait()
    box_tables((1.5, 0.5, -0.5, -1.5), (0.5, -0.5), (0.5, -0.5), 6.0, 0.9, col_ref, row_ref, tab_ref)
    for move in moves[:4]:
        move.wait()
    lane = lax.broadcasted_iota(jnp.int32, (8, POINTS), 1)
    limit = jnp.zeros((8, POINTS), jnp.int32)
    for g in range(LEAVES):
        limit = jnp.where(lane // SLOTS == g, counts_ref[g], limit)
    filled = (lane % SLOTS < limit)[0:1]
    charges = jnp.where(filled, q_ref[...], 0.0)
    halo_ref[0:RHS, :] = charges
    halo_ref[RHS:ROWS, :] = jnp.zeros((ROWS - RHS, POINTS), F32)
    halo_ref[RHS : RHS + 3, :] = off_ref[...]
    kern = split(leaf_kernel(off_ref[...], col_ref))
    up = padded(up_ref, pad_ref, 18.0 / TERMS)
    up = (up[0][:, :], up[1][:, :])
    halves = leaf_equivalents(charges, kern, up)
    store_equivalents(halves, e_ref, 0)
    e_move = pltpu.make_async_copy(e_ref, e_hbm, sems.at[7])
    e_move.start()
    acc = jnp.zeros((RHS, LANE), F32)
    for (x, y, z), kern in box_pairs(4, 2, 2, tab_ref):
        start = ((x >> 1) * 8 + (x & 1) + 2 * y + 4 * z) * 2 * RHS
        high, low = split(kern)
        wide = dot(e_ref[start : start + 2 * RHS, :][:, :SUB], high)
        acc = acc + wide[:RHS] + wide[RHS:] + dot(e_ref[start : start + RHS, :][:, :SUB], low)
    out_ref[...] = pack(mm3(split(acc[:, :SUB] * (60.0 / 18.0)), up))
    moves[-1].wait()
    e_move.wait()


def group_up_kernel(x_ref, maps_ref, up_ref, out_hbm, pad_ref, out_ref, sem):
    acc = (jnp.zeros((16, LANE), F32), jnp.zeros((16, LANE), F32))
    for e in range(INNER):
        acc = tile_dot(x_ref[8 * e : 8 * e + 8, :], maps_ref[e, 0], maps_ref[e, 1], acc)
    check = tile_sum(acc)
    both = jnp.concatenate([check, check], axis=0)
    equiv = mm3(split(both[:, :SUB]), padded(up_ref, pad_ref, 200.0 / TERMS))[:8]
    top = lax.broadcasted_iota(jnp.int32, (8, 128), 0) < 4
    tile = jnp.where(top, equiv[:, :128], pltpu.roll(equiv[:, 128:], 4, 0))
    for p in range(OUTER):
        out_ref[8 * p : 8 * p + 8, :] = tile
    move = pltpu.make_async_copy(out_ref, out_hbm, sem)
    move.start()
    move.wait()


def box_order(rows):
    return jnp.concatenate(
        [rows[8 * k : 8 * k + 8] for k in (y * 4 + x * 2 + z for x in (0, 1) for z in (0, 1) for y in (0, 1))], axis=0
    )


def index_order(rows):
    return jnp.concatenate(
        [rows[8 * k : 8 * k + 8] for k in (x * 4 + z * 2 + y for y in (0, 1) for x in (0, 1) for z in (0, 1))], axis=0
    )


def peers_kernel(x_ref, col_ref, row_ref, out_ref, tab_ref, shifted_ref):
    equiv = jnp.concatenate([box_order(unpack(x_ref[...])), jnp.zeros((16, LANE), F32)], axis=0)
    shifted_ref[...] = jnp.zeros_like(shifted_ref)
    for q in range(4):
        high, low = split(pltpu.roll(equiv, 4 * q, 0) if q else equiv)
        shifted_ref[q, 0, RHS : RHS + 80, :] = high
        shifted_ref[q, 1, RHS : RHS + 80, :] = low
    cols = columns(col_ref)
    for dy in range(-3, 4):
        tab_ref[dy + 3] = square_of(1, 2.0 * dy, 3.0, 3.0, cols, row_ref) + SOFTEN
    row = lax.broadcasted_iota(jnp.int32, (RHS, 128), 0)
    lane = lax.broadcasted_iota(jnp.int32, (RHS, 128), 1)
    px, pz, py = row >> 5, (row >> 4) & 1, (row >> 2) & 3
    dest = (py & 1) + pz * 2 + px * 4 + (py >> 1) * 8

    def valid(dx, dz):
        sx, sy, sz = px - dx, py - (lane - 3), pz - dz
        inside = (sx >= 0) & (sx < 2) & (sy >= 0) & (sy < 4) & (sz >= 0) & (sz < 2)
        source = (sy & 1) + sz * 2 + sx * 4 + (sy >> 1) * 8
        return (inside & (jnp.abs(source - dest) >= 2)).astype(F32)

    def moved(dx, dy, dz, mask):
        q = dy % 4
        start = RHS - (dx * 2 + dz) * 16 - 4 * (dy - q)
        keep = two(jnp.broadcast_to(mask[:, dy + 3 : dy + 4], (RHS, 128))).astype(BF)
        rows = [(shifted_ref[q, n, start : start + RHS, :] * keep)[:, :SUB] for n in range(2)]
        return jnp.concatenate(rows, axis=0)

    def add(acc, rows, kern, f):
        return acc[0] + f(rows, kern[0]), acc[1] + f(rows[:RHS], kern[1])

    def fold(acc):
        return acc[0][:RHS] + acc[0][RHS:] + acc[1]

    ahead_sum = (jnp.zeros((2 * RHS, LANE), F32), jnp.zeros((RHS, LANE), F32))
    behind_sum = (jnp.zeros((2 * RHS, SUB), F32), jnp.zeros((RHS, SUB), F32))
    planes = [(0, 0, (1, 2, 3))] + [(dx, dz, range(-3, 4)) for dx, dz in ((0, 1), (1, -1), (1, 0), (1, 1))]
    for n, (dx, dz, steps) in enumerate(planes):
        plane = square_of(0, dx * 4.0, 3.0, 3.0, cols, row_ref)
        tab_ref[7 + n] = plane + square_of(2, dz * 2.0, 3.0, 3.0, cols, row_ref)
        ahead, behind = valid(dx, dz), valid(-dx, -dz)
        for dy in steps:
            kern = split(lax.rsqrt(tab_ref[7 + n] + tab_ref[dy + 3]))
            ahead_sum = add(ahead_sum, moved(dx, dy, dz, ahead), kern, dot)
            kern = (kern[0][:, :SUB], kern[1][:, :SUB])
            behind_sum = add(behind_sum, moved(-dx, -dy, -dz, behind), kern, dot_nt)
    back = jnp.concatenate([fold(behind_sum), jnp.zeros((RHS, LANE - SUB), F32)], axis=1)
    out_ref[...] = index_order(fold(ahead_sum) + back)


def local_kernel(x_ref, peers_ref, down_ref, col_ref, row_ref, out_ref, pad_ref, tab_ref):
    outer = lax.axis_index("outer")
    own = [p.astype(F32) for p in corner(outer * 256, 8)]
    cols = columns(col_ref)
    for n in range(4):
        tab_ref[n] = square_of(2, own[2] - 4.0 * n, 10.0, 20.0, cols, row_ref) + SOFTEN
    for x in range(4):
        xsq = square_of(0, own[0] - 8.0 * x, 10.0, 20.0, cols, row_ref)
        for y in range(2):
            tab_ref[4 + x * 2 + y] = xsq + square_of(1, own[1] - 8.0 * y, 10.0, 20.0, cols, row_ref)
    acc = (jnp.zeros((16, LANE), F32), jnp.zeros((16, LANE), F32))
    for p in range(OUTER):
        z, x, y = (p & 1) + ((p >> 3) & 1) * 2, ((p >> 1) & 1) + ((p >> 4) & 1) * 2, (p >> 2) & 1
        weight = (jnp.abs(p - outer) >= 2).astype(F32)
        kern = split(lax.rsqrt(tab_ref[4 + x * 2 + y] + tab_ref[z]))
        acc = tile_dot(x_ref[8 * p : 8 * p + 8, :] * weight, kern[0], kern[1], acc)
    check = tile_sum(acc)
    both = jnp.concatenate([check, check], axis=0)
    down = padded(down_ref, pad_ref, 60.0 / TERMS)
    group = mm3(split(both[:, :SUB] * (200.0 / 60.0)), down)[:8]
    pieces = jnp.concatenate(split(group[:, :SUB]), axis=0)
    top = lax.broadcasted_iota(jnp.int32, (8, LANE), 0) < 4
    found = [None] * INNER
    for (x, y, z), kern in box_kernels(
        (-2.0, 2.0), (-3.0, -1.0, 1.0, 3.0), (-1.0, 1.0), 3.0, 20.0, col_ref, row_ref, tab_ref
    ):
        high, low = split(kern)
        part = dot(pieces, high) + dot(pieces, low)
        found[(y & 1) + z * 2 + x * 4 + (y >> 1) * 8] = part[:8] + part[8:]
    merged = [jnp.where(top, found[2 * m], pltpu.roll(found[2 * m + 1], 4, 0)) for m in range(INNER // 2)]
    total = jnp.concatenate(merged, axis=0) + peers_ref[...]
    out_ref[...] = pack(mm3(split(total[:, :SUB]), down))


def operator_kernel(
    flow_ref, off_ref, down_ref, col_ref, row_ref, up_ref, w_hbm, m_hbm, w_ref, m_ref, pad_ref, tab_ref, sems
):
    for (x, y, z), kern in box_kernels(
        (2.0, -2.0), (3.0, 1.0, -1.0, -3.0), (1.0, -1.0), 20.0, 3.0, col_ref, row_ref, tab_ref
    ):
        e = (y & 1) + z * 2 + x * 4 + (y >> 1) * 8
        high, low = split(kern)
        up_ref[e, 0, :, :] = high
        up_ref[e, 1, :, :] = low
    kern = split(leaf_kernel(off_ref[RHS : RHS + 3, :], col_ref))
    down = padded(down_ref, pad_ref, 18.0 / TERMS)
    down = (down[0][:, :SUB], down[1][:, :SUB])
    weights = split(mm3(down, kern))
    w_ref[0, :, :] = weights[0]
    w_ref[1, :, :] = weights[1]
    w_move = pltpu.make_async_copy(w_ref, w_hbm, sems.at[0])
    w_move.start()
    block = lax.broadcasted_iota(jnp.int32, (SUB, 256), 1) // SLOTS
    found = [jnp.zeros((SUB, 256), F32)] * 2
    for (x, y, z), kern in box_kernels(
        (-1.5, -0.5, 0.5, 1.5), (-0.5, 0.5), (-0.5, 0.5), 0.9, 6.0, col_ref, row_ref, tab_ref
    ):
        half, g = (x >> 1), (x & 1) + 2 * y + 4 * z
        lanes = slice(half * 256, half * 256 + 256)
        own = (weights[0][:, lanes], weights[1][:, lanes])
        found[half] = jnp.where(block == g, mm3(split(kern[:, :SUB]), own), found[half])
    for half in range(2):
        lanes = slice(half * 256, half * 256 + 256)
        m_high, m_low = split(found[half])
        m_ref[0, :, lanes] = m_high
        m_ref[1, :, lanes] = m_low
    m_move = pltpu.make_async_copy(m_ref, m_hbm, sems.at[1])
    m_move.start()
    w_move.wait()
    m_move.wait()


def near_field(near_ref, left_ref, own_ref, right_ref, out_ref, mask_ref, high_ref, low_ref):
    offs = jnp.concatenate([own_ref[RHS:ROWS, :], jnp.zeros((120, POINTS), F32)], axis=0).T
    inner = lax.axis_index("inner")
    device = lax.axis_index("outer") * INNER + inner
    base = (device - 1) * LEAVES
    total = 3 * POINTS
    lane = lax.broadcasted_iota(jnp.int32, (LEAVES, total), 1) // SLOTS
    found = jnp.zeros((LEAVES, total), F32)
    near = near_ref[...] - base
    for k in range(12):
        found = jnp.where(lane == near[:, k : k + 1], 1.0, found)
    mask_ref[...] = found
    leaf = lax.broadcasted_iota(jnp.int32, (1, POINTS), 1) // SLOTS
    within = local_leaf(leaf)
    own_box = corner(device * LEAVES, 4)
    sources = []
    for c in range(3):
        lanes = []
        for side, ref in ((-1, left_ref), (0, own_ref), (1, right_ref)):
            box = corner((device + side) * LEAVES, 4)[c] - own_box[c]
            lanes.append(ref[RHS + c : RHS + c + 1, :] + (box + within[c]).astype(F32))
        sources.append(jnp.concatenate(lanes, axis=1))
    for g in range(LEAVES):
        rows = slice(g * SLOTS, g * SLOTS + SLOTS)
        place = local_leaf(g)
        dist = SOFTEN
        for c in range(3):
            diff = (offs[rows, c : c + 1] + float(place[c])) - sources[c]
            dist = dist + diff * diff
        k_high, k_low = split(lax.rsqrt(dist) * mask_ref[g : g + 1, :])
        high_ref[rows, :] = k_high
        low_ref[rows, :] = k_low
    charges = jnp.concatenate([r[0:RHS, :] for r in (left_ref, own_ref, right_ref)], axis=1)
    q_high, q_low = split(charges)
    both = jnp.concatenate([q_high, q_low], axis=0)
    res = dot_nt(high_ref[...], both)
    res = res + jnp.concatenate([dot_nt(low_ref[...], q_high), jnp.zeros((POINTS, RHS), F32)], axis=1)
    flipped = res.T
    out_ref[...] = flipped[:RHS] + flipped[RHS:]


def field_kernel(
    far_ref, near_ref, own_ref, swap_ref, cross_ref, up_ref, col_ref, row_ref, w_hbm, m_hbm, e_hbm, out_ref, m_ref,
    pad_ref, e_ref, dl_ref, xtab_ref, tab_ref, w_ref, left_ref, right_ref, mask_ref, high_ref, low_ref, sems,
):
    middle = LEAVES * 2 * RHS
    moves = [
        pltpu.make_async_copy(e_hbm, e_ref.at[middle : 2 * middle], sems.at[0]),
        pltpu.make_async_copy(w_hbm, w_ref, sems.at[1]),
        pltpu.make_async_copy(m_hbm, m_ref, sems.at[2]),
    ]
    for move in moves:
        move.start()
    odd = lax.rem(lax.axis_index("inner"), 2) == 1
    left_ref[...] = jnp.where(odd, swap_ref[...], cross_ref[...])
    right_ref[...] = jnp.where(odd, cross_ref[...], swap_ref[...])
    near_field(near_ref, left_ref, own_ref, right_ref, out_ref, mask_ref, high_ref, low_ref)
    inner = lax.axis_index("inner")
    device = lax.axis_index("outer") * INNER + inner
    up = padded(up_ref, pad_ref, 18.0 / TERMS)
    for side, ref in ((0, left_ref), (2, right_ref)):
        kern = split(leaf_kernel(ref[RHS : RHS + 3, :], col_ref))
        store_equivalents(leaf_equivalents(ref[0:RHS, :], kern, up), e_ref, side * middle)
    for move in moves:
        move.wait()
    first = (device - 1) * LEAVES
    boxes = [corner((device + side) * LEAVES, 4) for side in (-1, 0, 1)]
    boxes = [[(boxes[1][c] - box[c]).astype(F32) for c in range(3)] for box in boxes]
    cols = columns(col_ref)
    for side in range(3):
        for n in range(7):
            xtab_ref[side * 7 + n] = square_of(0, boxes[side][0] + (n - 3.0), 0.9, 1.8, cols, row_ref)
        for c in range(3):
            tab_ref[27 + c] = square_of(2, boxes[side][2] + (c - 1.0), 0.9, 1.8, cols, row_ref) + SOFTEN
        for b in range(3):
            ysq = square_of(1, boxes[side][1] + (b - 1.0), 0.9, 1.8, cols, row_ref)
            for c in range(3):
                tab_ref[side * 9 + b * 3 + c] = ysq + tab_ref[27 + c]

    def one_leaf(g, carry):
        own = local_leaf(g)
        wide = jnp.zeros((2 * RHS, LANE), F32)
        narrow = jnp.zeros((RHS, LANE), F32)
        rest = jnp.zeros((LANE - SUB, LANE), BF)
        for k in range(0, 12, 4):
            tops, lows, equivs = [], [], []
            for n in range(k, k + 4):
                window = far_ref[g, n] - first
                side = window >> 4
                place = local_leaf(window & 15)
                x = side * 7 + 3 + own[0] - place[0]
                yz = side * 9 + 4 + (own[1] - place[1]) * 3 + own[2] - place[2]
                k_high, k_low = split(lax.rsqrt(xtab_ref[x] + tab_ref[yz]))
                tops += [k_high, rest]
                lows += [k_low, rest]
                equivs.append(e_ref[pl.ds(pl.multiple_of(window * (2 * RHS), 2 * RHS), 2 * RHS), :])
            equiv = jnp.concatenate(equivs, axis=1)
            wide = wide + dot(equiv, jnp.concatenate(tops, axis=0))
            narrow = narrow + dot(equiv[:RHS], jnp.concatenate(lows, axis=0))
        acc = wide[:RHS] + wide[RHS:] + narrow
        high, low = split(acc)
        start = pl.multiple_of(g * RHS, RHS)
        dl_ref[0, pl.ds(start, RHS), :] = high
        dl_ref[1, pl.ds(start, RHS), :] = low
        return carry

    lax.fori_loop(0, LEAVES, one_leaf, 0)
    block = lax.broadcasted_iota(jnp.int32, (RHS, 256), 1) // SLOTS
    for half in range(2):
        lanes = slice(half * 256, half * 256 + 256)
        rows = slice(half * 8 * RHS, (half + 1) * 8 * RHS)
        local = (dl_ref[0, rows, :][:, :SUB], dl_ref[1, rows, :][:, :SUB])
        res = mm3(local, (w_ref[0, :, lanes], w_ref[1, :, lanes]))
        acc = out_ref[:, lanes]
        for g in range(8):
            acc = acc + jnp.where(block == g, res[g * RHS : (g + 1) * RHS], 0.0)
        out_ref[:, lanes] = acc


def tail_kernel(x_ref, base_ref, m_ref, out_ref):
    high, low = split(unpack(x_ref[...])[:, :SUB])
    wide = dot(jnp.concatenate([high, low], axis=0), m_ref[0])
    out_ref[...] = base_ref[...] + wide[:RHS] + wide[RHS:] + dot(high, m_ref[1])


VM = pl.BlockSpec(memory_space=pltpu.VMEM)
SM = pl.BlockSpec(memory_space=pltpu.SMEM)
HB = pl.BlockSpec(memory_space=pltpu.HBM)


def call(kernel, name, outs, specs, scratch, vmem, *args, out_specs=None):
    return pl.pallas_call(
        kernel,
        name=name,
        out_shape=outs,
        in_specs=specs,
        out_specs=out_specs or jax.tree.map(lambda _: VM, outs),
        scratch_shapes=scratch,
        compiler_params=pltpu.CompilerParams(vmem_limit_bytes=vmem * 1024 * 1024),
        cost_estimate=pl.CostEstimate(flops=1000, bytes_accessed=1000, transcendentals=0),
    )(*args)


def in_hbm(x):
    return pltpu.with_memory_space_constraint(x, pltpu.HBM)


def tie(value, *others):
    return lax.optimization_barrier((value,) + others)[0]


def shards(offsets, charges, counts, near, far, upward, downward):
    col_np, row_np = sphere_tables()
    sds = jax.ShapeDtypeStruct
    pad = pltpu.VMEM((SUB, LANE), F32)
    flow = sds((2 * RHS, 128), F32)
    square = sds((TERMS, TERMS), F32)

    def tables(n):
        return pltpu.VMEM((n, SUB, LANE), F32)

    inputs = (offsets, charges, counts, upward, downward, jnp.asarray(col_np), jnp.asarray(row_np))
    equiv_rows = LEAVES * 2 * RHS
    dev_equiv, own, upward, downward, col, row, equiv = call(
        head_kernel, "leaf_and_device_equiv",
        (flow, sds((ROWS, POINTS), F32), square, square, sds((SUB, 128), F32), sds((8, LANE), F32), pltpu.HBM((equiv_rows, LANE), BF)),
        [HB] * 7,
        [
            pltpu.VMEM((3, POINTS), F32),
            pltpu.VMEM((RHS, POINTS), F32),
            pltpu.SMEM((LEAVES,), jnp.int32),
            pad,
            tables(10),
            pltpu.VMEM((equiv_rows, LANE), BF),
            pltpu.SemaphoreType.DMA((8,)),
        ],
        16, *map(in_hbm, inputs), out_specs=(VM, VM, VM, VM, VM, VM, HB),
    )
    peers_equiv = lax.all_to_all(dev_equiv, "inner", 0, 0, tiled=True)
    leaf_maps = pltpu.HBM((2, SUB, POINTS), BF)
    up_maps, weights, evaluate = call(
        operator_kernel, "evaluation_and_group_maps", (sds((INNER, 2, SUB, LANE), BF), leaf_maps, leaf_maps),
        [VM, VM, VM, VM, VM],
        [pltpu.VMEM((2, SUB, POINTS), BF), pltpu.VMEM((2, SUB, POINTS), BF), pad, tables(14), pltpu.SemaphoreType.DMA((2,))],
        14, dev_equiv, own, downward, col, row, out_specs=(VM, HB, HB),
    )
    swap = lax.ppermute(own, "inner", [(i, i ^ 1) for i in range(INNER)])
    cross = lax.ppermute(own, "inner", [(i, ((i + 1) ^ 1) - 1) for i in range(1, INNER - 1)])
    group_equiv = call(
        group_up_kernel, "group_equiv", pltpu.HBM((8 * OUTER, 128), F32), [VM, VM, VM],
        [pad, pltpu.VMEM((8 * OUTER, 128), F32), pltpu.SemaphoreType.DMA], 6,
        peers_equiv, up_maps, upward, out_specs=HB,
    )
    groups = lax.all_to_all(group_equiv, "outer", 0, 0, tiled=True)
    peers_part = call(
        peers_kernel, "device_to_device", sds((RHS, LANE), F32), [VM, VM, VM],
        [tables(12), pltpu.VMEM((4, 2, 3 * RHS, LANE), BF)], 10, peers_equiv, col, row,
    )
    groups = tie(groups, peers_part)
    local = call(
        local_kernel, "group_and_device_local", flow, [VM, VM, VM, VM, VM], [pad, tables(14)], 8,
        groups, peers_part, downward, col, row,
    )
    dev_local = lax.all_to_all(local, "inner", 0, 0, tiled=True)
    base, evaluate = call(
        field_kernel, "near_and_far_field", (sds((RHS, POINTS), F32), sds((2, SUB, POINTS), BF)),
        [SM, VM, VM, VM, VM, VM, VM, VM, HB, HB, HB],
        [
            pad,
            pltpu.VMEM((3 * LEAVES * 2 * RHS, LANE), BF),
            pltpu.VMEM((2, LEAVES * RHS, LANE), BF),
            tables(21),
            tables(30),
            pltpu.VMEM((2, SUB, POINTS), BF),
            pltpu.VMEM((ROWS, POINTS), F32),
            pltpu.VMEM((ROWS, POINTS), F32),
            pltpu.VMEM((LEAVES, 3 * POINTS), F32),
            pltpu.VMEM((POINTS, 3 * POINTS), BF),
            pltpu.VMEM((POINTS, 3 * POINTS), BF),
            pltpu.SemaphoreType.DMA((3,)),
        ],
        32, far, near, own, swap, cross, upward, col, row, in_hbm(weights), in_hbm(evaluate), in_hbm(equiv),
    )
    return call(tail_kernel, "potential", sds((RHS, POINTS), F32), [VM, VM, VM], [], 4, dev_local, base, evaluate)


def solution(mesh):
    both = ("outer", "inner")
    in_specs = (P(None, both), P(None, both), P(both), P(both, None), P(both, None), P(), P())
    return jax.shard_map(shards, mesh=mesh, in_specs=in_specs, out_specs=P(None, both), check_vma=False)
```

```python
import functools

import jax
import jax.numpy as jnp
import numpy as np
from jax import lax
from jax.experimental import pallas as pl
from jax.experimental.pallas import tpu as pltpu
from jax.sharding import PartitionSpec as P

SOFTEN = 0.25
GOLDEN = 2.399963229728653
RHS = 64
TERMS = 165
SUB = 176
LANE = 256
LEAVES = 16
SLOTS = 32
POINTS = LEAVES * SLOTS
ROWS = 72
INNER = 16
OUTER = 32
PART = RHS // INNER
BF = jnp.bfloat16
F32 = jnp.float32


def sphere_tables():
    steps = np.arange(TERMS, dtype=np.float32)
    height = (np.float32(1.0) - (np.float32(2.0) * steps + np.float32(1.0)) / np.float32(TERMS)).astype(np.float32)
    radial = np.sqrt(np.maximum(np.float32(1.0) - height * height, np.float32(0.0))).astype(np.float32)
    angle = (steps * np.float32(GOLDEN)).astype(np.float32)
    dirs = np.stack([radial * np.cos(angle), radial * np.sin(angle), height]).astype(np.float32)
    col = np.zeros((SUB, 128), np.float32)
    col[:TERMS, :3] = dirs.T
    row = np.zeros((8, LANE), np.float32)
    row[:3, :TERMS] = dirs
    return col, row


def split(x):
    high = x.astype(BF)
    return high, (x - high.astype(F32)).astype(BF)


def dot(a, b):
    return jnp.dot(a, b, preferred_element_type=F32)


def dot_nt(a, b):
    return lax.dot_general(a, b, (((1,), (1,)), ((), ())), preferred_element_type=F32)


def mm3(a, b, f=dot):
    return f(a[0], b[0]) + f(a[1], b[0]) + f(a[0], b[1])


def columns(col_ref):
    return [jnp.broadcast_to(col_ref[:, c : c + 1], (SUB, 128)) for c in range(3)]


def two(x):
    return jnp.concatenate([x, x], axis=1)


def square_of(axis, shift, radius_t, radius_i, cols, row_ref):
    diff = (radius_t * row_ref[axis : axis + 1, :] + shift) - two(radius_i * cols[axis])
    return diff * diff


def box_tables(xs, ys, zs, radius_t, radius_i, col_ref, row_ref, tab_ref):
    cols = columns(col_ref)
    for n, shift in enumerate(xs):
        tab_ref[n] = square_of(0, shift, radius_t, radius_i, cols, row_ref)
    zsq = len(xs)
    for n, shift in enumerate(zs):
        tab_ref[zsq + n] = square_of(2, shift, radius_t, radius_i, cols, row_ref) + SOFTEN
    start = zsq + len(zs)
    for b, shift in enumerate(ys):
        ysq = square_of(1, shift, radius_t, radius_i, cols, row_ref)
        for c in range(len(zs)):
            tab_ref[start + b * len(zs) + c] = ysq + tab_ref[zsq + c]


def box_pairs(nx, ny, nz, tab_ref):
    for b in range(ny):
        for c in range(nz):
            for a in range(nx):
                yield (a, b, c), lax.rsqrt(tab_ref[a] + tab_ref[nx + nz + b * nz + c])


def box_kernels(xs, ys, zs, radius_t, radius_i, col_ref, row_ref, tab_ref):
    box_tables(xs, ys, zs, radius_t, radius_i, col_ref, row_ref, tab_ref)
    yield from box_pairs(len(xs), len(ys), len(zs), tab_ref)


def bits(ids, low, axis, top=14):
    total = 0
    for level in range(5):
        place = 3 * level + axis
        if low <= place < top:
            total = total + (((ids >> place) & 1) << level)
    return total


def corner(leaf_id, low):
    return [bits(leaf_id, low, axis) for axis in range(3)]


def local_leaf(index):
    return ((index & 1) + ((index >> 3) & 1) * 2, (index >> 1) & 1, (index >> 2) & 1)


def peer_box(inner):
    return (((inner >> 2) & 1) * 4, (inner & 1) * 2 + ((inner >> 3) & 1) * 4, ((inner >> 1) & 1) * 2)


def leaf_kernel(offs, col_ref):
    total = SOFTEN
    for c in range(3):
        col = jnp.broadcast_to(col_ref[:, c : c + 1], (SUB, 128)) * 1.8
        diff = jnp.concatenate([col] * (POINTS // 128), axis=1) - offs[c : c + 1, :]
        total = total + diff * diff
    return lax.rsqrt(total)


def padded(map_ref, pad_ref, scale):
    pad_ref[...] = jnp.zeros_like(pad_ref)
    pad_ref[0:TERMS, 0:TERMS] = map_ref[...] * scale
    return split(pad_ref[...])


def leaf_equivalents(charges, kern, up):
    block = lax.broadcasted_iota(jnp.int32, (RHS, 256), 1) // SLOTS
    keep = [(block == g).astype(F32).astype(BF) for g in range(8)]
    pieces = split(charges)
    out = []
    for half in range(2):
        lanes = slice(half * 256, half * 256 + 256)
        spread = [jnp.concatenate([piece[:, lanes] * keep[g] for g in range(8)], axis=0) for piece in pieces]
        high, low = kern[0][:, lanes], kern[1][:, lanes]
        spread = jnp.concatenate([spread[0], spread[1], spread[0]], axis=1)
        check = dot_nt(spread, jnp.concatenate([high, high, low], axis=1))
        out.append(mm3(split(check), up))
    return out


def store_equivalents(halves, e_ref, first):
    for half in range(2):
        e_high, e_low = split(halves[half])
        for g in range(8):
            start = first + (half * 8 + g) * 2 * RHS
            e_ref[start : start + RHS, :] = e_high[g * RHS : g * RHS + RHS]
            e_ref[start + RHS : start + 2 * RHS, :] = e_low[g * RHS : g * RHS + RHS]


def pack(rows):
    low, high = rows[:, :128], rows[:, 128:]
    n = rows.shape[0]
    top = lax.broadcasted_iota(jnp.int32, (n, 128), 0) % 8 < 4
    first = jnp.where(top, low, pltpu.roll(high, 4, 0))
    second = jnp.where(top, pltpu.roll(low, n - 4, 0), high)
    tiles = []
    for m in range(n // 8):
        tiles += [first[8 * m : 8 * m + 8], second[8 * m : 8 * m + 8]]
    return jnp.concatenate(tiles, axis=0)


def unpack(tiles):
    n = tiles.shape[0] // 2
    first = jnp.concatenate([tiles[16 * m : 16 * m + 8] for m in range(n // 8)], axis=0)
    second = jnp.concatenate([tiles[16 * m + 8 : 16 * m + 16] for m in range(n // 8)], axis=0)
    top = lax.broadcasted_iota(jnp.int32, (n, 128), 0) % 8 < 4
    low = jnp.where(top, first, pltpu.roll(second, 4, 0))
    high = jnp.where(top, pltpu.roll(first, n - 4, 0), second)
    return jnp.concatenate([low, high], axis=1)


def tile_dot(tile, high, low, acc):
    a_high, a_low = split(tile)
    both = jnp.concatenate([a_high, a_low], axis=0)
    rest = SUB - 128
    front = dot(both, high[:128]) + dot(both, low[:128])
    back = dot(both[:, :rest], high[128:]) + dot(both[:, :rest], low[128:])
    return acc[0] + front, acc[1] + back


def tile_sum(acc):
    front = acc[0][:8] + acc[0][8:]
    back = acc[1][:8] + acc[1][8:]
    return front + pltpu.roll(back, 4, 0)


def head_kernel(
    off_hbm, q_hbm, counts_hbm, up_hbm, down_hbm, col_hbm, row_hbm,
    out_ref, halo_ref, up_ref, down_ref, col_ref, row_ref, e_hbm,
    off_ref, q_ref, counts_ref, pad_ref, tab_ref, e_ref, sems,
):
    moves = [
        pltpu.make_async_copy(src, dst, sems.at[n])
        for n, (src, dst) in enumerate(
            (
                (q_hbm, q_ref),
                (off_hbm, off_ref),
                (counts_hbm, counts_ref),
                (up_hbm, up_ref),
                (col_hbm, col_ref),
                (row_hbm, row_ref),
                (down_hbm, down_ref),
            )
        )
    ]
    for move in moves:
        move.start()
    for move in moves[:-1]:
        move.wait()
    lane = lax.broadcasted_iota(jnp.int32, (8, POINTS), 1)
    limit = jnp.zeros((8, POINTS), jnp.int32)
    for g in range(LEAVES):
        limit = jnp.where(lane // SLOTS == g, counts_ref[g], limit)
    filled = (lane % SLOTS < limit)[0:1]
    charges = jnp.where(filled, q_ref[...], 0.0)
    halo_ref[0:RHS, :] = charges
    halo_ref[RHS:ROWS, :] = jnp.zeros((ROWS - RHS, POINTS), F32)
    halo_ref[RHS : RHS + 3, :] = off_ref[...]
    kern = split(leaf_kernel(off_ref[...], col_ref))
    up = padded(up_ref, pad_ref, 18.0 / TERMS)
    up = (up[0][:, :], up[1][:, :])
    halves = leaf_equivalents(charges, kern, up)
    store_equivalents(halves, e_ref, 0)
    e_move = pltpu.make_async_copy(e_ref, e_hbm, sems.at[7])
    e_move.start()
    acc = jnp.zeros((RHS, LANE), F32)
    box_tables((1.5, 0.5, -0.5, -1.5), (0.5, -0.5), (0.5, -0.5), 6.0, 0.9, col_ref, row_ref, tab_ref)
    for (x, y, z), kern in box_pairs(4, 2, 2, tab_ref):
        start = ((x >> 1) * 8 + (x & 1) + 2 * y + 4 * z) * 2 * RHS
        high, low = split(kern)
        wide = dot(e_ref[start : start + 2 * RHS, :][:, :SUB], high)
        acc = acc + wide[:RHS] + wide[RHS:] + dot(e_ref[start : start + RHS, :][:, :SUB], low)
    out_ref[...] = pack(mm3(split(acc[:, :SUB] * (60.0 / 18.0)), up))
    moves[-1].wait()
    e_move.wait()


def group_up_kernel(x_ref, maps_ref, up_ref, out_hbm, pad_ref, out_ref, sem):
    acc = (jnp.zeros((16, LANE), F32), jnp.zeros((16, LANE), F32))
    for e in range(INNER):
        acc = tile_dot(x_ref[8 * e : 8 * e + 8, :], maps_ref[e, 0], maps_ref[e, 1], acc)
    check = tile_sum(acc)
    both = jnp.concatenate([check, check], axis=0)
    equiv = mm3(split(both[:, :SUB]), padded(up_ref, pad_ref, 200.0 / TERMS))[:8]
    top = lax.broadcasted_iota(jnp.int32, (8, 128), 0) < 4
    tile = jnp.where(top, equiv[:, :128], pltpu.roll(equiv[:, 128:], 4, 0))
    for p in range(OUTER):
        out_ref[8 * p : 8 * p + 8, :] = tile
    move = pltpu.make_async_copy(out_ref, out_hbm, sem)
    move.start()
    move.wait()


def box_order(rows):
    return jnp.concatenate(
        [rows[8 * k : 8 * k + 8] for k in (y * 4 + x * 2 + z for x in (0, 1) for z in (0, 1) for y in (0, 1))], axis=0
    )


def index_order(rows):
    return jnp.concatenate(
        [rows[8 * k : 8 * k + 8] for k in (x * 4 + z * 2 + y for y in (0, 1) for x in (0, 1) for z in (0, 1))], axis=0
    )


def peers_kernel(x_ref, col_ref, row_ref, out_ref, tab_ref, shifted_ref):
    equiv = jnp.concatenate([box_order(unpack(x_ref[...])), jnp.zeros((16, LANE), F32)], axis=0)
    shifted_ref[...] = jnp.zeros_like(shifted_ref)
    for q in range(4):
        high, low = split(pltpu.roll(equiv, 4 * q, 0) if q else equiv)
        shifted_ref[q, 0, RHS : RHS + 80, :] = high
        shifted_ref[q, 1, RHS : RHS + 80, :] = low
    cols = columns(col_ref)
    for dy in range(-3, 4):
        tab_ref[dy + 3] = square_of(1, 2.0 * dy, 3.0, 3.0, cols, row_ref) + SOFTEN
    row = lax.broadcasted_iota(jnp.int32, (RHS, 128), 0)
    lane = lax.broadcasted_iota(jnp.int32, (RHS, 128), 1)
    px, pz, py = row >> 5, (row >> 4) & 1, (row >> 2) & 3
    dest = (py & 1) + pz * 2 + px * 4 + (py >> 1) * 8

    def valid(dx, dz):
        sx, sy, sz = px - dx, py - (lane - 3), pz - dz
        inside = (sx >= 0) & (sx < 2) & (sy >= 0) & (sy < 4) & (sz >= 0) & (sz < 2)
        source = (sy & 1) + sz * 2 + sx * 4 + (sy >> 1) * 8
        return (inside & (jnp.abs(source - dest) >= 2)).astype(F32)

    def moved(dx, dy, dz, mask):
        q = dy % 4
        start = RHS - (dx * 2 + dz) * 16 - 4 * (dy - q)
        keep = two(jnp.broadcast_to(mask[:, dy + 3 : dy + 4], (RHS, 128))).astype(BF)
        rows = [(shifted_ref[q, n, start : start + RHS, :] * keep)[:, :SUB] for n in range(2)]
        return jnp.concatenate(rows, axis=0)

    def add(acc, rows, kern, f):
        return acc[0] + f(rows, kern[0]), acc[1] + f(rows[:RHS], kern[1])

    def fold(acc):
        return acc[0][:RHS] + acc[0][RHS:] + acc[1]

    ahead_sum = (jnp.zeros((2 * RHS, LANE), F32), jnp.zeros((RHS, LANE), F32))
    behind_sum = (jnp.zeros((2 * RHS, SUB), F32), jnp.zeros((RHS, SUB), F32))
    planes = [(0, 0, (1, 2, 3))] + [(dx, dz, range(-3, 4)) for dx, dz in ((0, 1), (1, -1), (1, 0), (1, 1))]
    for n, (dx, dz, steps) in enumerate(planes):
        plane = square_of(0, dx * 4.0, 3.0, 3.0, cols, row_ref)
        tab_ref[7 + n] = plane + square_of(2, dz * 2.0, 3.0, 3.0, cols, row_ref)
        ahead, behind = valid(dx, dz), valid(-dx, -dz)
        for dy in steps:
            kern = split(lax.rsqrt(tab_ref[7 + n] + tab_ref[dy + 3]))
            ahead_sum = add(ahead_sum, moved(dx, dy, dz, ahead), kern, dot)
            kern = (kern[0][:, :SUB], kern[1][:, :SUB])
            behind_sum = add(behind_sum, moved(-dx, -dy, -dz, behind), kern, dot_nt)
    back = jnp.concatenate([fold(behind_sum), jnp.zeros((RHS, LANE - SUB), F32)], axis=1)
    out_ref[...] = index_order(fold(ahead_sum) + back)


def local_kernel(x_ref, peers_ref, down_ref, col_ref, row_ref, out_ref, pad_ref, tab_ref):
    outer = lax.axis_index("outer")
    own = [p.astype(F32) for p in corner(outer * 256, 8)]
    cols = columns(col_ref)
    for n in range(4):
        tab_ref[n] = square_of(2, own[2] - 4.0 * n, 10.0, 20.0, cols, row_ref) + SOFTEN
    for x in range(4):
        xsq = square_of(0, own[0] - 8.0 * x, 10.0, 20.0, cols, row_ref)
        for y in range(2):
            tab_ref[4 + x * 2 + y] = xsq + square_of(1, own[1] - 8.0 * y, 10.0, 20.0, cols, row_ref)
    acc = (jnp.zeros((16, LANE), F32), jnp.zeros((16, LANE), F32))
    for p in range(OUTER):
        z, x, y = (p & 1) + ((p >> 3) & 1) * 2, ((p >> 1) & 1) + ((p >> 4) & 1) * 2, (p >> 2) & 1
        weight = (jnp.abs(p - outer) >= 2).astype(F32)
        kern = split(lax.rsqrt(tab_ref[4 + x * 2 + y] + tab_ref[z]))
        acc = tile_dot(x_ref[8 * p : 8 * p + 8, :] * weight, kern[0], kern[1], acc)
    check = tile_sum(acc)
    both = jnp.concatenate([check, check], axis=0)
    down = padded(down_ref, pad_ref, 60.0 / TERMS)
    group = mm3(split(both[:, :SUB] * (200.0 / 60.0)), down)[:8]
    pieces = jnp.concatenate(split(group[:, :SUB]), axis=0)
    top = lax.broadcasted_iota(jnp.int32, (8, LANE), 0) < 4
    found = [None] * INNER
    for (x, y, z), kern in box_kernels(
        (-2.0, 2.0), (-3.0, -1.0, 1.0, 3.0), (-1.0, 1.0), 3.0, 20.0, col_ref, row_ref, tab_ref
    ):
        high, low = split(kern)
        part = dot(pieces, high) + dot(pieces, low)
        found[(y & 1) + z * 2 + x * 4 + (y >> 1) * 8] = part[:8] + part[8:]
    merged = [jnp.where(top, found[2 * m], pltpu.roll(found[2 * m + 1], 4, 0)) for m in range(INNER // 2)]
    total = jnp.concatenate(merged, axis=0) + peers_ref[...]
    out_ref[...] = pack(mm3(split(total[:, :SUB]), down))


def operator_kernel(
    flow_ref, off_ref, down_ref, col_ref, row_ref, up_ref, w_hbm, m_hbm, w_ref, m_ref, pad_ref, tab_ref, sems
):
    for (x, y, z), kern in box_kernels(
        (2.0, -2.0), (3.0, 1.0, -1.0, -3.0), (1.0, -1.0), 20.0, 3.0, col_ref, row_ref, tab_ref
    ):
        e = (y & 1) + z * 2 + x * 4 + (y >> 1) * 8
        high, low = split(kern)
        up_ref[e, 0, :, :] = high
        up_ref[e, 1, :, :] = low
    kern = split(leaf_kernel(off_ref[RHS : RHS + 3, :], col_ref))
    down = padded(down_ref, pad_ref, 18.0 / TERMS)
    down = (down[0][:, :SUB], down[1][:, :SUB])
    weights = split(mm3(down, kern))
    w_ref[0, :, :] = weights[0]
    w_ref[1, :, :] = weights[1]
    w_move = pltpu.make_async_copy(w_ref, w_hbm, sems.at[0])
    w_move.start()
    block = lax.broadcasted_iota(jnp.int32, (SUB, 256), 1) // SLOTS
    found = [jnp.zeros((SUB, 256), F32)] * 2
    for (x, y, z), kern in box_kernels(
        (-1.5, -0.5, 0.5, 1.5), (-0.5, 0.5), (-0.5, 0.5), 0.9, 6.0, col_ref, row_ref, tab_ref
    ):
        half, g = (x >> 1), (x & 1) + 2 * y + 4 * z
        lanes = slice(half * 256, half * 256 + 256)
        own = (weights[0][:, lanes], weights[1][:, lanes])
        found[half] = jnp.where(block == g, mm3(split(kern[:, :SUB]), own), found[half])
    for half in range(2):
        lanes = slice(half * 256, half * 256 + 256)
        m_high, m_low = split(found[half])
        m_ref[0, :, lanes] = m_high
        m_ref[1, :, lanes] = m_low
    m_move = pltpu.make_async_copy(m_ref, m_hbm, sems.at[1])
    m_move.start()
    w_move.wait()
    m_move.wait()


def near_field(near_ref, left_ref, own_ref, right_ref, out_ref, mask_ref, high_ref, low_ref):
    offs = jnp.concatenate([own_ref[RHS:ROWS, :], jnp.zeros((120, POINTS), F32)], axis=0).T
    inner = lax.axis_index("inner")
    device = lax.axis_index("outer") * INNER + inner
    base = (device - 1) * LEAVES
    total = 3 * POINTS
    lane = lax.broadcasted_iota(jnp.int32, (LEAVES, total), 1) // SLOTS
    found = jnp.zeros((LEAVES, total), F32)
    near = near_ref[...] - base
    for k in range(12):
        found = jnp.where(lane == near[:, k : k + 1], 1.0, found)
    mask_ref[...] = found
    leaf = lax.broadcasted_iota(jnp.int32, (1, POINTS), 1) // SLOTS
    within = local_leaf(leaf)
    own_box = corner(device * LEAVES, 4)
    sources = []
    for c in range(3):
        lanes = []
        for side, ref in ((-1, left_ref), (0, own_ref), (1, right_ref)):
            box = corner((device + side) * LEAVES, 4)[c] - own_box[c]
            lanes.append(ref[RHS + c : RHS + c + 1, :] + (box + within[c]).astype(F32))
        sources.append(jnp.concatenate(lanes, axis=1))
    for g in range(LEAVES):
        rows = slice(g * SLOTS, g * SLOTS + SLOTS)
        place = local_leaf(g)
        dist = SOFTEN
        for c in range(3):
            diff = (offs[rows, c : c + 1] + float(place[c])) - sources[c]
            dist = dist + diff * diff
        k_high, k_low = split(lax.rsqrt(dist) * mask_ref[g : g + 1, :])
        high_ref[rows, :] = k_high
        low_ref[rows, :] = k_low
    charges = jnp.concatenate([r[0:RHS, :] for r in (left_ref, own_ref, right_ref)], axis=1)
    q_high, q_low = split(charges)
    both = jnp.concatenate([q_high, q_low], axis=0)
    res = dot_nt(high_ref[...], both)
    res = res + jnp.concatenate([dot_nt(low_ref[...], q_high), jnp.zeros((POINTS, RHS), F32)], axis=1)
    flipped = res.T
    out_ref[...] = flipped[:RHS] + flipped[RHS:]


def sides(swap_ref, cross_ref, left_ref, right_ref):
    odd = lax.rem(lax.axis_index("inner"), 2) == 1
    left_ref[...] = jnp.where(odd, swap_ref[...], cross_ref[...])
    right_ref[...] = jnp.where(odd, cross_ref[...], swap_ref[...])


def near_kernel(
    near_ref, own_ref, swap_ref, cross_ref, out_hbm, out_ref, left_ref, right_ref, mask_ref, high_ref, low_ref, sem
):
    sides(swap_ref, cross_ref, left_ref, right_ref)
    near_field(near_ref, left_ref, own_ref, right_ref, out_ref, mask_ref, high_ref, low_ref)
    move = pltpu.make_async_copy(out_ref, out_hbm, sem)
    move.start()
    move.wait()


def field_kernel(
    far_ref, swap_ref, cross_ref, up_ref, col_ref, row_ref, w_hbm, m_hbm, e_hbm, near_hbm, out_ref, m_ref,
    pad_ref, e_ref, dl_ref, xtab_ref, tab_ref, w_ref, left_ref, right_ref, sems,
):
    middle = LEAVES * 2 * RHS
    moves = [
        pltpu.make_async_copy(e_hbm, e_ref.at[middle : 2 * middle], sems.at[0]),
        pltpu.make_async_copy(w_hbm, w_ref, sems.at[1]),
        pltpu.make_async_copy(m_hbm, m_ref, sems.at[2]),
        pltpu.make_async_copy(near_hbm, out_ref, sems.at[3]),
    ]
    for move in moves:
        move.start()
    sides(swap_ref, cross_ref, left_ref, right_ref)
    inner = lax.axis_index("inner")
    device = lax.axis_index("outer") * INNER + inner
    up = padded(up_ref, pad_ref, 18.0 / TERMS)
    for side, ref in ((0, left_ref), (2, right_ref)):
        kern = split(leaf_kernel(ref[RHS : RHS + 3, :], col_ref))
        store_equivalents(leaf_equivalents(ref[0:RHS, :], kern, up), e_ref, side * middle)
    for move in moves:
        move.wait()
    first = (device - 1) * LEAVES
    boxes = [corner((device + side) * LEAVES, 4) for side in (-1, 0, 1)]
    boxes = [[(boxes[1][c] - box[c]).astype(F32) for c in range(3)] for box in boxes]
    cols = columns(col_ref)
    for side in range(3):
        for n in range(7):
            xtab_ref[side * 7 + n] = square_of(0, boxes[side][0] + (n - 3.0), 0.9, 1.8, cols, row_ref)
        for c in range(3):
            tab_ref[27 + c] = square_of(2, boxes[side][2] + (c - 1.0), 0.9, 1.8, cols, row_ref) + SOFTEN
        for b in range(3):
            ysq = square_of(1, boxes[side][1] + (b - 1.0), 0.9, 1.8, cols, row_ref)
            for c in range(3):
                tab_ref[side * 9 + b * 3 + c] = ysq + tab_ref[27 + c]

    def one_leaf(g, carry):
        own = local_leaf(g)
        wide = jnp.zeros((2 * RHS, LANE), F32)
        narrow = jnp.zeros((RHS, LANE), F32)
        rest = jnp.zeros((LANE - SUB, LANE), BF)
        for k in range(0, 12, 4):
            tops, lows, equivs = [], [], []
            for n in range(k, k + 4):
                window = far_ref[g, n] - first
                side = window >> 4
                place = local_leaf(window & 15)
                x = side * 7 + 3 + own[0] - place[0]
                yz = side * 9 + 4 + (own[1] - place[1]) * 3 + own[2] - place[2]
                k_high, k_low = split(lax.rsqrt(xtab_ref[x] + tab_ref[yz]))
                tops += [k_high, rest]
                lows += [k_low, rest]
                equivs.append(e_ref[pl.ds(pl.multiple_of(window * (2 * RHS), 2 * RHS), 2 * RHS), :])
            equiv = jnp.concatenate(equivs, axis=1)
            wide = wide + dot(equiv, jnp.concatenate(tops, axis=0))
            narrow = narrow + dot(equiv[:RHS], jnp.concatenate(lows, axis=0))
        acc = wide[:RHS] + wide[RHS:] + narrow
        high, low = split(acc)
        start = pl.multiple_of(g * RHS, RHS)
        dl_ref[0, pl.ds(start, RHS), :] = high
        dl_ref[1, pl.ds(start, RHS), :] = low
        return carry

    lax.fori_loop(0, LEAVES, one_leaf, 0)
    block = lax.broadcasted_iota(jnp.int32, (RHS, 256), 1) // SLOTS
    for half in range(2):
        lanes = slice(half * 256, half * 256 + 256)
        rows = slice(half * 8 * RHS, (half + 1) * 8 * RHS)
        local = (dl_ref[0, rows, :][:, :SUB], dl_ref[1, rows, :][:, :SUB])
        res = mm3(local, (w_ref[0, :, lanes], w_ref[1, :, lanes]))
        acc = out_ref[:, lanes]
        for g in range(8):
            acc = acc + jnp.where(block == g, res[g * RHS : (g + 1) * RHS], 0.0)
        out_ref[:, lanes] = acc


def tail_kernel(x_ref, base_ref, m_ref, out_ref):
    high, low = split(unpack(x_ref[...])[:, :SUB])
    wide = dot(jnp.concatenate([high, low], axis=0), m_ref[0])
    out_ref[...] = base_ref[...] + wide[:RHS] + wide[RHS:] + dot(high, m_ref[1])


VM = pl.BlockSpec(memory_space=pltpu.VMEM)
SM = pl.BlockSpec(memory_space=pltpu.SMEM)
HB = pl.BlockSpec(memory_space=pltpu.HBM)


def call(kernel, name, outs, specs, scratch, vmem, *args, out_specs=None):
    return pl.pallas_call(
        kernel,
        name=name,
        out_shape=outs,
        in_specs=specs,
        out_specs=out_specs or jax.tree.map(lambda _: VM, outs),
        scratch_shapes=scratch,
        compiler_params=pltpu.CompilerParams(vmem_limit_bytes=vmem * 1024 * 1024),
        cost_estimate=pl.CostEstimate(flops=1000, bytes_accessed=1000, transcendentals=0),
    )(*args)


def in_hbm(x):
    return pltpu.with_memory_space_constraint(x, pltpu.HBM)


def tie(value, *others):
    return lax.optimization_barrier((value,) + others)[0]


def shards(offsets, charges, counts, near, far, upward, downward):
    col_np, row_np = sphere_tables()
    sds = jax.ShapeDtypeStruct
    pad = pltpu.VMEM((SUB, LANE), F32)
    flow = sds((2 * RHS, 128), F32)
    square = sds((TERMS, TERMS), F32)

    def tables(n):
        return pltpu.VMEM((n, SUB, LANE), F32)

    inputs = (offsets, charges, counts, upward, downward, jnp.asarray(col_np), jnp.asarray(row_np))
    equiv_rows = LEAVES * 2 * RHS
    dev_equiv, own, upward, downward, col, row, equiv = call(
        head_kernel, "leaf_and_device_equiv",
        (flow, sds((ROWS, POINTS), F32), square, square, sds((SUB, 128), F32), sds((8, LANE), F32), pltpu.HBM((equiv_rows, LANE), BF)),
        [HB] * 7,
        [
            pltpu.VMEM((3, POINTS), F32),
            pltpu.VMEM((RHS, POINTS), F32),
            pltpu.SMEM((LEAVES,), jnp.int32),
            pad,
            tables(10),
            pltpu.VMEM((equiv_rows, LANE), BF),
            pltpu.SemaphoreType.DMA((8,)),
        ],
        16, *map(in_hbm, inputs), out_specs=(VM, VM, VM, VM, VM, VM, HB),
    )
    peers_equiv = lax.all_to_all(dev_equiv, "inner", 0, 0, tiled=True)
    leaf_maps = pltpu.HBM((2, SUB, POINTS), BF)
    up_maps, weights, evaluate = call(
        operator_kernel, "evaluation_and_group_maps", (sds((INNER, 2, SUB, LANE), BF), leaf_maps, leaf_maps),
        [VM, VM, VM, VM, VM],
        [pltpu.VMEM((2, SUB, POINTS), BF), pltpu.VMEM((2, SUB, POINTS), BF), pad, tables(14), pltpu.SemaphoreType.DMA((2,))],
        14, dev_equiv, own, downward, col, row, out_specs=(VM, HB, HB),
    )
    swap = lax.ppermute(own, "inner", [(i, i ^ 1) for i in range(INNER)])
    cross = lax.ppermute(own, "inner", [(i, ((i + 1) ^ 1) - 1) for i in range(1, INNER - 1)])
    group_equiv = call(
        group_up_kernel, "group_equiv", pltpu.HBM((8 * OUTER, 128), F32), [VM, VM, VM],
        [pad, pltpu.VMEM((8 * OUTER, 128), F32), pltpu.SemaphoreType.DMA], 6,
        peers_equiv, up_maps, upward, out_specs=HB,
    )
    groups = lax.all_to_all(group_equiv, "outer", 0, 0, tiled=True)
    peers_part = call(
        peers_kernel, "device_to_device", sds((RHS, LANE), F32), [VM, VM, VM],
        [tables(12), pltpu.VMEM((4, 2, 3 * RHS, LANE), BF)], 10, peers_equiv, col, row,
    )
    points = pltpu.VMEM((ROWS, POINTS), F32)
    spread = pltpu.VMEM((POINTS, 3 * POINTS), BF)
    near_part = call(
        near_kernel, "near_field", pltpu.HBM((RHS, POINTS), F32), [VM, VM, VM, VM],
        [pltpu.VMEM((RHS, POINTS), F32), points, points, pltpu.VMEM((LEAVES, 3 * POINTS), F32), spread, spread, pltpu.SemaphoreType.DMA],
        14, near, own, swap, cross, out_specs=HB,
    )
    groups = tie(groups, peers_part, near_part)
    local = call(
        local_kernel, "group_and_device_local", flow, [VM, VM, VM, VM, VM], [pad, tables(14)], 8,
        groups, peers_part, downward, col, row,
    )
    dev_local = lax.all_to_all(local, "inner", 0, 0, tiled=True)
    base, evaluate = call(
        field_kernel, "near_and_far_field", (sds((RHS, POINTS), F32), sds((2, SUB, POINTS), BF)),
        [SM, VM, VM, VM, VM, VM, HB, HB, HB, HB],
        [
            pad,
            pltpu.VMEM((3 * LEAVES * 2 * RHS, LANE), BF),
            pltpu.VMEM((2, LEAVES * RHS, LANE), BF),
            tables(21),
            tables(30),
            pltpu.VMEM((2, SUB, POINTS), BF),
            points,
            points,
            pltpu.SemaphoreType.DMA((4,)),
        ],
        26, far, swap, cross, upward, col, row, *map(in_hbm, (weights, evaluate, equiv, near_part)),
    )
    return call(tail_kernel, "potential", sds((RHS, POINTS), F32), [VM, VM, VM], [], 4, dev_local, base, evaluate)


def solution(mesh):
    both = ("outer", "inner")
    in_specs = (P(None, both), P(None, both), P(both), P(both, None), P(both, None), P(), P())
    return jax.shard_map(shards, mesh=mesh, in_specs=in_specs, out_specs=P(None, both), check_vma=False)
```
